32 devices in a mesh: mp: 2 (over x), dp: 8 (over z, core), tensor: 2 (over y).
Axes of the slice: x: 2, y: 2, z: 4, core: 2. Of those that a mesh axis runs over, the one named last changes fastest.
Arguments:
- acts: bfloat16 [2, 256, 8192], P('mp', 'dp', 'tensor'), may hold values from -6 to 6
- gate_w: bfloat16 [2, 8192, 28672], P('mp', 'tensor', 'dp'), may hold values from -0.0625 to 0.0625
- up_w: bfloat16 [2, 8192, 28672], P('mp', 'tensor', 'dp'), may hold values from -0.0625 to 0.0625
- panel_units: int32 [8192], replicated, may hold values from 0 to 28671, as said below
Outputs:
- score: bfloat16 [8192, 28672], P(('mp', 'tensor'), 'dp')
The draws below stay inside these ranges and needn't reach their ends.
Inputs may be any that keep to these rules, and one draw needn't show every extreme that they name: `panel_units`: write an entry's position as ((r * 8) + b) * 256 + k with 0 <= k < 256; the entry lies in [b * 3584, (b + 1) * 3584), all entries are distinct, and the first and the last unit of every block are among them.
All inputs are finite; a program needn't handle non-finite values.
Results may differ from the reference program's by a relative error of at most 0.03.
Values may be sent and summed in bfloat16 or wider, within the bound.
No kernel may reach another device: no remote copies, remote signals or barrier semaphores. Data moves between devices by JAX's collectives and lax.ppermute only.
A program may use at most 128 MiB of HBM per device.

```python
import jax
import jax.numpy as jnp
from jax import lax

D = 8192
FF = 28672
PANEL = 8192
TOKENS = 256
UNITS_DEV = 3584
PER_BLOCK = 1024
SELK = 256
N_TENSOR = 2


def draw_panel_units(key, part):
    blocks = FF // UNITS_DEV

    def one_block(index):
        block_key = jax.random.fold_in(key, index)
        order_list = jax.random.permutation(jax.random.fold_in(block_key, 1), UNITS_DEV).astype(jnp.int32)
        local_units = jnp.arange(UNITS_DEV, dtype=jnp.int32)
        at_ends = (local_units == 0) | (local_units == UNITS_DEV - 1)
        ranking = jnp.where(at_ends, -1, order_list)
        chosen = jnp.argsort(ranking, stable=True)[:PER_BLOCK].astype(jnp.int32)
        chosen = jax.random.permutation(jax.random.fold_in(block_key, 2), chosen)
        return chosen + index * UNITS_DEV
    table = jax.vmap(one_block)(jnp.arange(blocks, dtype=jnp.int32))
    table = table.reshape(blocks, PER_BLOCK // SELK, SELK).transpose(1, 0, 2).reshape(-1)
    return table.astype(jnp.int32)


def steps_of(key, shape, pieces, least, top_value):
    def one(dim, blocks):
        heights = jax.random.uniform(jax.random.fold_in(jax.random.fold_in(key, 6), dim), (blocks,), jnp.float32, least / len(pieces), top_value / len(pieces))
        return jnp.repeat(jnp.exp(heights), shape[dim] // blocks).reshape((-1,) + (1,) * (len(shape) - dim - 1))

    loudness = one(*pieces[0])
    for cut in pieces[1:]:
        loudness = loudness * one(*cut)
    return loudness


def centred(key, shape, deviation, limit, split=(), kind=jnp.bfloat16):
    loudness = steps_of(key, shape, split, -0.22, 0.18) if split else 1.0
    entries = jax.random.normal(key, shape, jnp.float32) * deviation * loudness
    return jnp.minimum(jnp.maximum(entries, -limit), limit).astype(kind)


def setup_inputs(seed: int = 0) -> dict:
    seeds = jax.random.split(jax.random.key(seed), 5)
    acts = centred(seeds[0], (2, TOKENS, D), 1.0, 6.0, ((0, 2), (1, 8), (2, 2)))
    gate_w = centred(seeds[1], (2, D, FF), D ** -0.5, 0.0625, ((0, 2), (1, 2), (2, 8)))
    up_w = centred(seeds[2], (2, D, FF), D ** -0.5, 0.0625, ((0, 2), (1, 2), (2, 8)))
    panel_units = draw_panel_units(jax.random.fold_in(seeds[4], 71), 0)
    return dict(acts=acts, gate_w=gate_w, up_w=up_w, panel_units=panel_units)


epsilon = 1e-05

def width_sum(inputs, weight):
    width = D // N_TENSOR

    def add_slice(index, total):
        start = (index * width).astype(jnp.int32)
        rows_slice = lax.dynamic_slice_in_dim(inputs, start, width, 1)
        weight_slice = lax.dynamic_slice_in_dim(weight, start, width, 0)
        partial_sum = jnp.dot(rows_slice, weight_slice, preferred_element_type=jnp.float32)
        rounded = lax.optimization_barrier(partial_sum.astype(jnp.bfloat16))
        return total + rounded.astype(jnp.float32)
    start_total = jnp.zeros((inputs.shape[0], weight.shape[1]), jnp.float32)
    return lax.fori_loop(jnp.int32(0), jnp.int32(N_TENSOR), add_slice, start_total)

def zscores(inputs, weight_gate, weight_up):
    gate = width_sum(inputs, weight_gate)
    upward = width_sum(inputs, weight_up)
    hidden = (jax.nn.silu(gate) * upward).astype(jnp.bfloat16)
    wide_hidden = hidden.astype(jnp.float32)
    unit_mean = lax.optimization_barrier(jnp.mean(wide_hidden, axis=0))
    unit_var = lax.optimization_barrier(jnp.mean(wide_hidden * wide_hidden, axis=0)) - unit_mean * unit_mean
    return ((wide_hidden - unit_mean) * lax.rsqrt(unit_var + epsilon)).astype(jnp.bfloat16)

def reference(acts, gate_w, up_w, panel_units):
    first_z = zscores(acts[0], gate_w[0], up_w[0])
    second_z = zscores(acts[1], gate_w[1], up_w[1])
    panel = jnp.take(first_z, panel_units, axis=1)
    row_size = min(512, PANEL)
    panel_blocks = panel.T.reshape(PANEL // row_size, row_size, TOKENS)
    score_scale = 1.0 / jnp.sqrt(jnp.float32(TOKENS))

    def one_block(rows_block):
        product = jnp.dot(rows_block, second_z, preferred_element_type=jnp.float32)
        return (product * score_scale).astype(jnp.bfloat16)
    result = lax.map(one_block, panel_blocks)
    return result.reshape(PANEL, FF)
```

```python
import functools
import math

import jax
import jax.numpy as jnp
from jax import lax
from jax.experimental import pallas as pl
from jax.experimental.pallas import tpu as pltpu
from jax.sharding import PartitionSpec as P

epsilon = 1e-05
AXES = ("mp", "dp", "tensor")
MIB = 1 << 20


def from_partner(block, axis, distance):
    count = lax.axis_size(axis)
    route = []
    for low in range(count):
        high = low | 1 << distance
        if high != low and high < count:
            route += [(low, high), (high, low)]
    return lax.ppermute(block, axis, route)


def cross_models(full_units, panel_own, panel_next, model_index):
    other_units, other_panel = from_partner((full_units, panel_next), "mp", 0)
    is_first = model_index == 0
    return (
        jnp.where(is_first, panel_own, other_panel),
        jnp.where(is_first, other_units, full_units),
    )


def general_body(acts, gate_w, up_w, panel_units):
    model_index = lax.axis_index("mp")
    unit_block = lax.axis_index("dp")
    n_model = lax.axis_size("mp")
    n_data = lax.axis_size("dp")
    n_width = lax.axis_size("tensor")
    weight_gate = gate_w[0]
    weight_up = up_w[0]
    units = weight_gate.shape[1]
    gathered = lax.all_gather(acts[0], "dp", axis=0, tiled=True)
    tokens = gathered.shape[0]
    token_share = tokens // n_width
    score_scale = 1.0 / math.sqrt(tokens)
    panel_picks = panel_units.reshape(n_model, n_width, n_data, -1)
    panel_picks = (
        lax.dynamic_index_in_dim(panel_picks, unit_block, axis=2, keepdims=False)
        - unit_block * units
    )
    gate_part = jnp.dot(gathered, weight_gate, preferred_element_type=jnp.float32)
    up_part = jnp.dot(gathered, weight_up, preferred_element_type=jnp.float32)
    summed = lax.psum_scatter(
        jnp.concatenate([gate_part, up_part], axis=1).astype(jnp.bfloat16),
        "tensor",
        scatter_dimension=0,
        tiled=True,
    ).astype(jnp.float32)
    hidden = (jax.nn.silu(summed[:, :units]) * summed[:, units:]).astype(jnp.bfloat16)
    wide_hidden = hidden.astype(jnp.float32)
    totals = lax.psum(
        (jnp.sum(wide_hidden, axis=0), jnp.sum(wide_hidden * wide_hidden, axis=0)), "tensor"
    )
    unit_mean = totals[0] / tokens
    unit_var = totals[1] / tokens - unit_mean * unit_mean
    scored = ((wide_hidden - unit_mean) * lax.rsqrt(unit_var + epsilon)).astype(jnp.bfloat16)
    full_units = lax.all_gather(scored, "tensor", axis=0, tiled=True)
    order_list = panel_picks.transpose(1, 0, 2).reshape(-1)
    chosen = jnp.take(scored, order_list, axis=1).reshape(token_share, n_width, -1)
    moved_rows = lax.all_to_all(chosen, "tensor", split_axis=1, concat_axis=0, tiled=True)
    moved_rows = moved_rows.reshape(tokens, n_model, -1)
    panel_cols = lax.all_gather(moved_rows, "dp", axis=2, tiled=True)
    mine_a, mine_b = cross_models(full_units, panel_cols[:, 0], panel_cols[:, 1], model_index)
    result = lax.dot_general(
        mine_a, mine_b, (((0,), (0,)), ((), ())), preferred_element_type=jnp.float32
    )
    return (result * score_scale).astype(jnp.bfloat16)


def routes(sizes, move):
    n_model, n_data, n_width = sizes
    pairs = []
    for m in range(n_model):
        for d in range(n_data):
            for t in range(n_width):
                to = move(m, d, t)
                if to is not None:
                    source = (m * n_data + d) * n_width + t
                    pairs.append((source, (to[0] * n_data + to[1]) * n_width + to[2]))
    return pairs


def send(block, sizes, move):
    return lax.ppermute(block, AXES, routes(sizes, move))


def along_chips(step, sources):
    def move(m, d, t):
        return (m, d + 2 * step, t) if d // 2 in sources else None

    return move


def gather_chips(block, sizes, chip, core):
    up = send(block, sizes, along_chips(1, (0, 1, 2)))
    down = send(block, sizes, along_chips(-1, (1, 2, 3)))
    far = jnp.where(chip == 2, down, up)

    def across(m, d, t):
        return {2: (m, d - 4, t), 1: (m, d + 4, t)}.get(d // 2)

    further_down = send(down, sizes, along_chips(-1, (1, 2)))
    further_up = send(up, sizes, along_chips(1, (1, 2)))
    ends = send(far, sizes, across)
    line = jnp.stack([ends, further_up, up, block, down, further_down, ends])
    same = lax.dynamic_slice_in_dim(line, 3 - chip, 4, axis=0)
    other = send(same, sizes, lambda m, d, t: (m, d ^ 1, t))
    first = core == 0
    pairs = jnp.stack([jnp.where(first, same, other), jnp.where(first, other, same)], axis=1)
    return pairs.reshape((-1,) + block.shape[1:])


def partial_kernel(place_ref, x_ref, gate_ref, up_ref, out_ref):
    x = x_ref[...]
    out_ref[0] = jnp.dot(x, gate_ref[...], preferred_element_type=jnp.float32).astype(jnp.bfloat16)
    out_ref[1] = jnp.dot(x, up_ref[...], preferred_element_type=jnp.float32).astype(jnp.bfloat16)


def partials(place, x, gate, up, tile, first, count):
    tokens, width = x.shape
    weights = pl.BlockSpec((width, tile), lambda i, place_ref: (0, place_ref[0] + first + i))
    return pl.pallas_call(
        partial_kernel,
        out_shape=jax.ShapeDtypeStruct((2, tokens, tile * count), jnp.bfloat16),
        grid_spec=pltpu.PrefetchScalarGridSpec(
            num_scalar_prefetch=1,
            grid=(count,),
            in_specs=[
                pl.BlockSpec((tokens, width), lambda i, place_ref: (0, 0)),
                weights,
                weights,
            ],
            out_specs=pl.BlockSpec((2, tokens, tile), lambda i, place_ref: (0, 0, i)),
        ),
        compiler_params=pltpu.CompilerParams(vmem_limit_bytes=32 * MIB),
        cost_estimate=pl.CostEstimate(
            flops=4 * tokens * width * tile * count,
            bytes_accessed=4 * width * tile * count,
            transcendentals=0,
        ),
    )(place, x, gate, up)


def pick_kernel(counts, tile, bases_ref, picks_ref, *refs):
    out_ref = refs[-1]
    tokens, picked = out_ref.shape[1:]
    total = jnp.zeros((2 * tokens, picked), jnp.float32)
    for part, (ref, count) in enumerate(zip(refs[:-1], counts)):
        for i in range(count):
            base = bases_ref[part] + i * tile
            unit = lax.broadcasted_iota(jnp.int32, (tile, picked), 0) + base
            chosen = jnp.where(unit == picks_ref[...], 1.0, 0.0).astype(jnp.bfloat16)
            block = ref[:, :, i * tile : (i + 1) * tile].reshape(2 * tokens, tile)
            total += jnp.dot(block, chosen, preferred_element_type=jnp.float32)
    out_ref[...] = total.astype(jnp.bfloat16).reshape(2, tokens, picked)


def pick(bases, picks, parts, tile):
    tokens = parts[0].shape[1]
    picked = picks.shape[1]
    counts = [part.shape[2] // tile for part in parts]
    vmem = pl.BlockSpec(memory_space=pltpu.VMEM)
    return pl.pallas_call(
        functools.partial(pick_kernel, counts, tile),
        out_shape=jax.ShapeDtypeStruct((2, tokens, picked), jnp.bfloat16),
        in_specs=[pl.BlockSpec(memory_space=pltpu.SMEM), vmem] + [vmem] * len(parts),
        out_specs=vmem,
        compiler_params=pltpu.CompilerParams(vmem_limit_bytes=32 * MIB),
        cost_estimate=pl.CostEstimate(
            flops=4 * tokens * picked * tile * sum(counts),
            bytes_accessed=4 * tokens * tile * sum(counts),
            transcendentals=0,
        ),
    )(bases, picks, *parts)


def zscore(mine, theirs):
    tokens = mine.shape[1]
    gate = mine[0].astype(jnp.float32) + theirs[0].astype(jnp.float32)
    up = mine[1].astype(jnp.float32) + theirs[1].astype(jnp.float32)
    hidden = (gate / (1.0 + jnp.exp(-gate)) * up).astype(jnp.bfloat16).astype(jnp.float32)
    mean = jnp.sum(hidden, axis=0, keepdims=True) / tokens
    var = jnp.sum(hidden * hidden, axis=0, keepdims=True) / tokens - mean * mean
    return (hidden - mean) * lax.rsqrt(var + epsilon)


def unit_kernel(mine_ref, theirs_ref, out_ref):
    out_ref[...] = zscore(mine_ref[...], theirs_ref[...]).astype(jnp.bfloat16)


def unit_scores(mine, theirs, tile, first):
    _, tokens, count = theirs.shape
    return pl.pallas_call(
        unit_kernel,
        out_shape=jax.ShapeDtypeStruct((tokens, count), jnp.bfloat16),
        grid=(count // tile,),
        in_specs=[
            pl.BlockSpec((2, tokens, tile), lambda i: (0, 0, first + i)),
            pl.BlockSpec((2, tokens, tile), lambda i: (0, 0, i)),
        ],
        out_specs=pl.BlockSpec((tokens, tile), lambda i: (0, i)),
        compiler_params=pltpu.CompilerParams(vmem_limit_bytes=16 * MIB),
        cost_estimate=pl.CostEstimate(
            flops=20 * tokens * count, bytes_accessed=10 * tokens * count, transcendentals=tokens * count
        ),
    )(mine, theirs)


def panel_kernel(mine_ref, theirs_ref, out_ref):
    out_ref[...] = zscore(mine_ref[...], theirs_ref[...]).T.astype(jnp.bfloat16)


def panel_scores(mine, theirs, tile):
    _, tokens, count = theirs.shape
    block = pl.BlockSpec((2, tokens, tile), lambda i: (0, 0, i))
    return pl.pallas_call(
        panel_kernel,
        out_shape=jax.ShapeDtypeStruct((count, tokens), jnp.bfloat16),
        grid=(count // tile,),
        in_specs=[block, block],
        out_specs=pl.BlockSpec((tile, tokens), lambda i: (i, 0)),
        compiler_params=pltpu.CompilerParams(vmem_limit_bytes=16 * MIB),
        cost_estimate=pl.CostEstimate(
            flops=20 * tokens * count, bytes_accessed=10 * tokens * count, transcendentals=tokens * count
        ),
    )(mine, theirs)


def score_kernel(scale, count, where_ref, panel_ref, b_mine, a_mine, b_far, a_far, *refs):
    out_ref = refs[-1]
    is_b = where_ref[0] == 1
    step = pl.program_id(0)

    def write(units):
        total = jnp.dot(panel_ref[...], units, preferred_element_type=jnp.float32)
        out_ref[...] = (total * scale).astype(jnp.bfloat16)

    @pl.when(step < count)
    def _():
        write(jnp.where(is_b, b_mine[...], a_mine[...]))

    @pl.when(step >= count)
    def _():
        write(jnp.where(is_b, b_far[...], a_far[...]))


def scores(where, panel, pieces, tile, first, half, so_far):
    rows, tokens = panel.shape
    count = pieces[0].shape[1] // tile
    near = pl.BlockSpec((tokens, tile), lambda i, where_ref: (0, jnp.minimum(i, count - 1)))
    far = pl.BlockSpec((tokens, tile), lambda i, where_ref: (0, jnp.maximum(i - count, 0)))

    def place(i, where_ref):
        side = jnp.where(i < count, where_ref[1], 1 - where_ref[1])
        return 0, side * half + first + lax.rem(i, count)

    carried = [] if so_far is None else [so_far]
    return pl.pallas_call(
        functools.partial(score_kernel, 1.0 / math.sqrt(tokens), count),
        out_shape=jax.ShapeDtypeStruct((rows, 2 * half * tile), jnp.bfloat16),
        grid_spec=pltpu.PrefetchScalarGridSpec(
            num_scalar_prefetch=1,
            grid=(2 * count,),
            in_specs=[pl.BlockSpec((rows, tokens), lambda i, where_ref: (0, 0)), near, near, far, far]
            + [pl.BlockSpec(memory_space=pl.ANY)] * len(carried),
            out_specs=pl.BlockSpec((rows, tile), place),
        ),
        input_output_aliases={6: 0} if carried else {},
        compiler_params=pltpu.CompilerParams(vmem_limit_bytes=32 * MIB),
        cost_estimate=pl.CostEstimate(
            flops=4 * rows * tokens * tile * count,
            bytes_accessed=4 * rows * tile * count,
            transcendentals=0,
        ),
    )(where, panel, *pieces, *carried)


def split_tiles(count):
    sizes = []
    while count > 0:
        sizes.append(min(2, count))
        count -= sizes[-1]
    return sizes


def paired_body(acts, gate_w, up_w, panel_units):
    model = lax.axis_index("mp")
    block = lax.axis_index("dp")
    side = lax.axis_index("tensor")
    sizes = tuple(lax.axis_size(name) for name in AXES)
    gate, up = gate_w[0], up_w[0]
    units = gate.shape[1]
    tile = 256
    half = units // 2 // tile
    chunks = split_tiles(half)

    x = gather_chips(acts[0], sizes, block // 2, block % 2)

    to_side = jnp.reshape((1 - side) * half, (1,)).astype(jnp.int32)
    own_side = jnp.reshape(side * half, (1,)).astype(jnp.int32)

    def b_sides(m, d, t):
        return (m, d, 1 - t) if m == 1 else None

    def a_sides(m, d, t):
        return (m, d, 1 - t) if m == 0 else None

    def b_to_a(m, d, t):
        return (0, d, t) if m == 1 else None

    def a_to_b(m, d, t):
        return (1, d, t) if m == 0 else None

    sent, came, first = [], [], 0
    for count in chunks:
        sent.append(partials(to_side, x, gate, up, tile, first, count))
        came.append(send(sent[-1], sizes, b_sides))
        first += count
    kept = partials(own_side, x, gate, up, tile, 0, half)

    picks = panel_units.reshape(2, 2, sizes[1], -1)
    picks = lax.dynamic_index_in_dim(picks, block, axis=2, keepdims=False) - block * units
    picks_far = lax.dynamic_index_in_dim(picks, 1 - side, axis=1, keepdims=False).reshape(1, -1)
    picks_own = lax.dynamic_index_in_dim(picks, side, axis=1, keepdims=False).reshape(1, -1)
    bases, first = [], 0
    for count in chunks:
        bases.append((to_side[0] + first) * tile)
        first += count
    bases = jnp.stack(bases + [own_side[0] * tile]).astype(jnp.int32)
    parts = sent + [kept]
    panel_came = send(pick(bases, picks_far, parts, tile), sizes, a_sides)
    panel_kept = pick(bases, picks_own, parts, tile)
    rows = panel_scores(panel_kept, panel_came, tile)
    share = rows.shape[0] // 2
    rows_b = send(rows[share:], sizes, a_to_b)
    rows = jnp.where(model == 0, rows[:share], rows_b)
    panel = gather_chips(rows, sizes, block // 2, block % 2)

    pieces, first = [], 0
    for index, count in enumerate(chunks):
        z = unit_scores(kept, came[index], tile, first)
        first += count
        a_mine = send(z, sizes, b_to_a)
        a_far = send(a_mine, sizes, a_sides)
        if index == 0:
            b_far = send(a_far, sizes, a_to_b)
        else:
            b_far = send(z, sizes, b_sides)
        pieces.append((z, a_mine, b_far, a_far))

    where = jnp.stack([model, side]).astype(jnp.int32)
    result, first = None, 0
    for count, piece in zip(chunks, pieces):
        result = scores(where, panel, piece, tile, first, half, result)
        first += count
    return result


def solution(mesh):
    in_specs = (P("mp", "dp", "tensor"), P("mp", "tensor", "dp"), P("mp", "tensor", "dp"), P())
    out_specs = P(("mp", "tensor"), "dp")
    paired = mesh.shape["mp"] == 2 and mesh.shape["tensor"] == 2 and mesh.shape["dp"] == 8

    def body(acts, gate_w, up_w, panel_units):
        if paired and gate_w.shape[2] % 512 == 0:
            return paired_body(acts, gate_w, up_w, panel_units)
        return general_body(acts, gate_w, up_w, panel_units)

    return jax.shard_map(body, mesh=mesh, in_specs=in_specs, out_specs=out_specs, check_vma=False)
```

```python
import functools
import math

import jax
import jax.numpy as jnp
from jax import lax
from jax.experimental import pallas as pl
from jax.experimental.pallas import tpu as pltpu
from jax.sharding import PartitionSpec as P

epsilon = 1e-05
AXES = ("mp", "dp", "tensor")
MIB = 1 << 20


def from_partner(block, axis, distance):
    count = lax.axis_size(axis)
    route = []
    for low in range(count):
        high = low | 1 << distance
        if high != low and high < count:
            route += [(low, high), (high, low)]
    return lax.ppermute(block, axis, route)


def cross_models(full_units, panel_own, panel_next, model_index):
    other_units, other_panel = from_partner((full_units, panel_next), "mp", 0)
    is_first = model_index == 0
    return (
        jnp.where(is_first, panel_own, other_panel),
        jnp.where(is_first, other_units, full_units),
    )


def general_body(acts, gate_w, up_w, panel_units):
    model_index = lax.axis_index("mp")
    unit_block = lax.axis_index("dp")
    n_model = lax.axis_size("mp")
    n_data = lax.axis_size("dp")
    n_width = lax.axis_size("tensor")
    weight_gate = gate_w[0]
    weight_up = up_w[0]
    units = weight_gate.shape[1]
    gathered = lax.all_gather(acts[0], "dp", axis=0, tiled=True)
    tokens = gathered.shape[0]
    token_share = tokens // n_width
    score_scale = 1.0 / math.sqrt(tokens)
    panel_picks = panel_units.reshape(n_model, n_width, n_data, -1)
    panel_picks = (
        lax.dynamic_index_in_dim(panel_picks, unit_block, axis=2, keepdims=False)
        - unit_block * units
    )
    gate_part = jnp.dot(gathered, weight_gate, preferred_element_type=jnp.float32)
    up_part = jnp.dot(gathered, weight_up, preferred_element_type=jnp.float32)
    summed = lax.psum_scatter(
        jnp.concatenate([gate_part, up_part], axis=1).astype(jnp.bfloat16),
        "tensor",
        scatter_dimension=0,
        tiled=True,
    ).astype(jnp.float32)
    hidden = (jax.nn.silu(summed[:, :units]) * summed[:, units:]).astype(jnp.bfloat16)
    wide_hidden = hidden.astype(jnp.float32)
    totals = lax.psum(
        (jnp.sum(wide_hidden, axis=0), jnp.sum(wide_hidden * wide_hidden, axis=0)), "tensor"
    )
    unit_mean = totals[0] / tokens
    unit_var = totals[1] / tokens - unit_mean * unit_mean
    scored = ((wide_hidden - unit_mean) * lax.rsqrt(unit_var + epsilon)).astype(jnp.bfloat16)
    full_units = lax.all_gather(scored, "tensor", axis=0, tiled=True)
    order_list = panel_picks.transpose(1, 0, 2).reshape(-1)
    chosen = jnp.take(scored, order_list, axis=1).reshape(token_share, n_width, -1)
    moved_rows = lax.all_to_all(chosen, "tensor", split_axis=1, concat_axis=0, tiled=True)
    moved_rows = moved_rows.reshape(tokens, n_model, -1)
    panel_cols = lax.all_gather(moved_rows, "dp", axis=2, tiled=True)
    mine_a, mine_b = cross_models(full_units, panel_cols[:, 0], panel_cols[:, 1], model_index)
    result = lax.dot_general(
        mine_a, mine_b, (((0,), (0,)), ((), ())), preferred_element_type=jnp.float32
    )
    return (result * score_scale).astype(jnp.bfloat16)


CHIPS = 4


def routes(sizes, move):
    n_model, n_data, n_width = sizes
    pairs = []
    for m in range(n_model):
        for d in range(n_data):
            for t in range(n_width):
                to = move(m, d, t)
                if to is not None:
                    source = (m * n_data + d) * n_width + t
                    pairs.append((source, (to[0] * n_data + to[1]) * n_width + to[2]))
    return pairs


def send(block, sizes, move):
    return lax.ppermute(block, AXES, routes(sizes, move))


def other_core(m, d, t):
    return m, d ^ 1, t


def shifted(step):
    def move(m, d, t):
        return m, (d + 2 * step) % (2 * CHIPS), t

    return move


def shifts(block, sizes):
    came = [send(block, sizes, shifted(step)) for step in (1, CHIPS - 1, 2)]
    return [block, came[0], came[2], came[1]]


def gather_line(block, sizes):
    return jnp.concatenate(shifts(block, sizes), axis=0)


def join_kernel(*refs):
    rows = refs[0].shape[0]
    for i in range(CHIPS):
        refs[-1][i * rows : (i + 1) * rows, :] = refs[i][...]


def join(blocks, after):
    rows, width = blocks[0].shape
    vmem = pl.BlockSpec(memory_space=pltpu.VMEM)
    return call(
        join_kernel,
        out_shape=jax.ShapeDtypeStruct((CHIPS * rows, width), blocks[0].dtype),
        in_specs=[vmem] * CHIPS + [pl.BlockSpec(memory_space=pl.ANY)] * len(after),
        out_specs=vmem,
        flops=0,
        moved=4 * CHIPS * rows * width,
        vmem=16,
    )(*blocks, *after)


def canonical(index, chip, core):
    line = lax.rem(chip + CHIPS - index % CHIPS, CHIPS)
    return line * 2 + (core if index < CHIPS else 1 - core)


def call(kernel, *, flops, moved, vmem, **rest):
    return pl.pallas_call(
        kernel,
        compiler_params=pltpu.CompilerParams(vmem_limit_bytes=vmem * MIB),
        cost_estimate=pl.CostEstimate(flops=flops, bytes_accessed=moved, transcendentals=0),
        **rest,
    )


def early_kernel(place_ref, same_ref, other_ref, gate_ref, up_ref, out_ref):
    x = jnp.concatenate([same_ref[...], other_ref[...]], axis=0)
    out_ref[0] = jnp.dot(x, gate_ref[...], preferred_element_type=jnp.float32)
    out_ref[1] = jnp.dot(x, up_ref[...], preferred_element_type=jnp.float32)


def early_products(place, same, other, gate, up, tile, count):
    tokens, width = 2 * same.shape[0], same.shape[1]
    weights = pl.BlockSpec((width, tile), lambda i, place_ref: (0, place_ref[0] + i))
    whole = pl.BlockSpec(same.shape, lambda i, place_ref: (0, 0))
    return call(
        early_kernel,
        out_shape=jax.ShapeDtypeStruct((2, tokens, tile * count), jnp.float32),
        grid_spec=pltpu.PrefetchScalarGridSpec(
            num_scalar_prefetch=1,
            grid=(count,),
            in_specs=[whole, whole, weights, weights],
            out_specs=pl.BlockSpec((2, tokens, tile), lambda i, place_ref: (0, 0, i)),
        ),
        flops=4 * tokens * width * tile * count,
        moved=4 * width * tile * count,
        vmem=32,
    )(place, same, other, gate, up)


def store_sorted(place_ref, out_ref, which, total):
    rows = total.shape[0] // (2 * CHIPS)
    total = total.astype(jnp.bfloat16)
    for i in range(2 * CHIPS):
        start = pl.multiple_of(canonical(i, place_ref[1], place_ref[2]) * rows, rows)
        out_ref[which, pl.ds(start, rows), :] = total[i * rows : (i + 1) * rows]


def late_kernel(place_ref, early_ref, same_ref, other_ref, gate_ref, up_ref, *refs):
    x = jnp.concatenate([same_ref[...], other_ref[...]], axis=0)
    for which, weight_ref in enumerate((gate_ref, up_ref)):
        total = jnp.dot(x, weight_ref[...], preferred_element_type=jnp.float32)
        store_sorted(place_ref, refs[-1], which, early_ref[which] + total)


def late_products(place, early, same, other, gate, up, tile, first, count, after):
    tokens, width = 2 * same.shape[0], same.shape[1]
    weights = pl.BlockSpec((width, tile), lambda i, place_ref: (1, place_ref[0] + first + i))
    whole = pl.BlockSpec(same.shape, lambda i, place_ref: (0, 0))
    return call(
        late_kernel,
        out_shape=jax.ShapeDtypeStruct((2, tokens, tile * count), jnp.bfloat16),
        grid_spec=pltpu.PrefetchScalarGridSpec(
            num_scalar_prefetch=1,
            grid=(count,),
            in_specs=[
                pl.BlockSpec((2, tokens, tile), lambda i, place_ref: (0, 0, first + i)),
                whole,
                whole,
                weights,
                weights,
            ]
            + [pl.BlockSpec(memory_space=pl.ANY)] * len(after),
            out_specs=pl.BlockSpec((2, tokens, tile), lambda i, place_ref: (0, 0, i)),
        ),
        flops=4 * tokens * width * tile * count,
        moved=4 * width * tile * count,
        vmem=32,
    )(place, early, same, other, gate, up, *after)


KEPT_PARTS = 2
KEPT_STEPS = 2


def kept_kernel(place_ref, same_a, other_a, same_b, other_b, gate_ref, up_ref, *refs):
    out_ref, total_ref = refs[-2:]
    step = pl.program_id(1)
    depth = gate_ref.shape[0]
    for at in range(2 * KEPT_STEPS):
        same_ref, other_ref = ((same_a, other_a), (same_b, other_b))[at // KEPT_STEPS]
        start = at % KEPT_STEPS * depth

        @pl.when(step == at)
        def _():
            x = jnp.concatenate(
                [same_ref[:, start : start + depth], other_ref[:, start : start + depth]], axis=0
            )
            for which, weight_ref in enumerate((gate_ref, up_ref)):
                total = jnp.dot(x, weight_ref[...], preferred_element_type=jnp.float32)
                if at:
                    total += total_ref[which]
                if at < 2 * KEPT_STEPS - 1:
                    total_ref[which] = total
                else:
                    store_sorted(place_ref, out_ref, which, total)


def kept_products(place, same, other, gate, up, after):
    tokens, width = 2 * same[0].shape[0], same[0].shape[1]
    units = gate.shape[1] // 2
    part, depth = units // KEPT_PARTS, width // KEPT_STEPS
    weights = pl.BlockSpec((depth, part), lambda i, k, place_ref: (k, place_ref[3] * KEPT_PARTS + i))
    whole = pl.BlockSpec(same[0].shape, lambda i, k, place_ref: (0, 0))
    return call(
        kept_kernel,
        out_shape=jax.ShapeDtypeStruct((2, tokens, units), jnp.bfloat16),
        grid_spec=pltpu.PrefetchScalarGridSpec(
            num_scalar_prefetch=1,
            grid=(KEPT_PARTS, 2 * KEPT_STEPS),
            in_specs=[whole] * 4
            + [weights, weights]
            + [pl.BlockSpec(memory_space=pl.ANY)] * len(after),
            out_specs=pl.BlockSpec((2, tokens, part), lambda i, k, place_ref: (0, 0, i)),
            scratch_shapes=[pltpu.VMEM((2, tokens, part), jnp.float32)],
        ),
        flops=8 * tokens * width * units,
        moved=8 * width * units,
        vmem=40,
    )(place, same[0], other[0], same[1], other[1], gate, up, *after)


def pick_kernel(counts, tile, has_instead, bases_ref, picks_ref, *refs):
    out_ref = refs[-1]
    tokens, picked = out_ref.shape[1:]

    @pl.when(bases_ref[len(counts)] == 0)
    def _():
        total = jnp.zeros((2 * tokens, picked), jnp.float32)
        for part, (ref, count) in enumerate(zip(refs[: len(counts)], counts)):
            for i in range(count):
                base = bases_ref[part] + i * tile
                unit = lax.broadcasted_iota(jnp.int32, (tile, picked), 0) + base
                chosen = jnp.where(unit == picks_ref[...], 1.0, 0.0).astype(jnp.bfloat16)
                block = ref[:, :, i * tile : (i + 1) * tile].reshape(2 * tokens, tile)
                total += jnp.dot(block, chosen, preferred_element_type=jnp.float32)
        out_ref[...] = total.astype(jnp.bfloat16).reshape(2, tokens, picked)

    @pl.when(bases_ref[len(counts)] == 1)
    def _():
        out_ref[...] = refs[len(counts)][...] if has_instead else jnp.zeros_like(out_ref)


def pick(bases, picks, parts, instead, tile, after):
    tokens = parts[0].shape[1]
    picked = picks.shape[1]
    counts = [part.shape[2] // tile for part in parts]
    vmem = pl.BlockSpec(memory_space=pltpu.VMEM)
    return call(
        functools.partial(pick_kernel, counts, tile, len(instead)),
        out_shape=jax.ShapeDtypeStruct((2, tokens, picked), jnp.bfloat16),
        in_specs=[pl.BlockSpec(memory_space=pltpu.SMEM), vmem]
        + [vmem] * len(parts + instead)
        + [pl.BlockSpec(memory_space=pl.ANY)] * len(after),
        out_specs=vmem,
        flops=4 * tokens * picked * tile * sum(counts),
        moved=4 * tokens * tile * sum(counts),
        vmem=32,
    )(bases, picks, *parts, *instead, *after)


def zscore(mine, theirs):
    tokens = mine.shape[1]
    gate = mine[0].astype(jnp.float32) + theirs[0].astype(jnp.float32)
    up = mine[1].astype(jnp.float32) + theirs[1].astype(jnp.float32)
    hidden = (gate / (1.0 + jnp.exp(-gate)) * up).astype(jnp.bfloat16).astype(jnp.float32)
    mean = jnp.sum(hidden, axis=0, keepdims=True) / tokens
    var = jnp.sum(hidden * hidden, axis=0, keepdims=True) / tokens - mean * mean
    return (hidden - mean) * lax.rsqrt(var + epsilon)


def unit_kernel(bounds, mine_ref, *refs):
    out_ref = refs[-1]
    for (start, stop), theirs_ref in zip(bounds, refs):
        out_ref[:, start - bounds[0][0] : stop - bounds[0][0]] = zscore(
            mine_ref[:, :, start:stop], theirs_ref[...]
        ).astype(jnp.bfloat16)


def unit_scores(mine, theirs, start):
    tokens = mine.shape[1]
    bounds = []
    for part in theirs:
        bounds.append((start, start + part.shape[2]))
        start = bounds[-1][1]
    count = start - bounds[0][0]
    vmem = pl.BlockSpec(memory_space=pltpu.VMEM)
    return call(
        functools.partial(unit_kernel, bounds),
        out_shape=jax.ShapeDtypeStruct((tokens, count), jnp.bfloat16),
        in_specs=[vmem] * (1 + len(theirs)),
        out_specs=vmem,
        flops=20 * tokens * count,
        moved=10 * tokens * count,
        vmem=32,
    )(mine, *theirs)


def panel_kernel(mine_ref, theirs_ref, out_ref):
    out_ref[...] = zscore(mine_ref[...], theirs_ref[...]).T.astype(jnp.bfloat16)


def panel_scores(mine, theirs, first):
    _, tokens, count = theirs.shape
    return call(
        panel_kernel,
        out_shape=jax.ShapeDtypeStruct((count, tokens), jnp.bfloat16),
        grid=(1,),
        in_specs=[
            pl.BlockSpec((2, tokens, count), lambda i: (0, 0, first)),
            pl.BlockSpec((2, tokens, count), lambda i: (0, 0, 0)),
        ],
        out_specs=pl.BlockSpec((count, tokens), lambda i: (0, 0)),
        flops=20 * tokens * count,
        moved=10 * tokens * count,
        vmem=16,
    )(mine, theirs)


def score_kernel(scale, n_pieces, has_before, where_ref, same_ref, other_ref, *refs):
    pieces = refs[: 4 * n_pieces]
    out_ref, near_ref, far_ref, block_ref, sems = refs[4 * n_pieces + has_before :]
    model, chip, core, near_column, far_column = (where_ref[i] for i in range(5))
    rows = same_ref.shape[0] // CHIPS
    columns = near_ref.shape[1]

    def assemble(at, into):
        start = 0
        for piece in range(n_pieces):
            ref = pieces[4 * piece + at]
            into[:, start : start + ref.shape[1]] = ref[...]
            start += ref.shape[1]

    for holder in range(2):

        @pl.when(model == holder)
        def _():
            assemble(2 * holder, near_ref)
            assemble(2 * holder + 1, far_ref)

    def copy(slot, row, column):
        return pltpu.make_async_copy(
            block_ref.at[slot],
            out_ref.at[
                pl.ds(pl.multiple_of(row, rows), rows), pl.ds(pl.multiple_of(column, 128), columns)
            ],
            sems.at[slot],
        )

    def step(index, carry):
        line = lax.rem(chip + CHIPS - index, CHIPS)
        for which, panel_ref in enumerate((same_ref, other_ref)):
            panel = panel_ref[pl.ds(pl.multiple_of(index * rows, rows), rows), :]
            row = (line * 2 + (1 - core if which else core)) * rows
            for far, units_ref in enumerate((near_ref, far_ref)):
                slot = 2 * which + far
                column = far_column if far else near_column

                @pl.when(index > 0)
                def _():
                    copy(slot, row, column).wait()

                total = jnp.dot(panel, units_ref[...], preferred_element_type=jnp.float32)
                block_ref[slot] = (total * scale).astype(jnp.bfloat16)
                copy(slot, row, column).start()
        return carry

    lax.fori_loop(0, CHIPS, step, 0)
    for slot in range(4):
        copy(slot, 0, 0).wait()


def scores(where, same, other, pieces, tile, first, half, before):
    tokens = same.shape[1]
    rows = same.shape[0] // CHIPS
    columns = sum(piece[0].shape[1] for piece in pieces)
    model, chip, core, side = where
    near = (side * half + first) * tile
    far = ((1 - side) * half + first) * tile
    where = jnp.stack([model, chip, core, near, far]).astype(jnp.int32)
    vmem = pl.BlockSpec(memory_space=pltpu.VMEM)
    anywhere = pl.BlockSpec(memory_space=pl.ANY)
    flat = [array for piece in pieces for array in piece]
    return call(
        functools.partial(score_kernel, 1.0 / math.sqrt(tokens), len(pieces), len(before)),
        out_shape=jax.ShapeDtypeStruct((2 * CHIPS * rows, 2 * half * tile), jnp.bfloat16),
        in_specs=[pl.BlockSpec(memory_space=pltpu.SMEM), vmem, vmem]
        + [vmem] * len(flat)
        + [anywhere] * len(before),
        out_specs=anywhere,
        scratch_shapes=[
            pltpu.VMEM((tokens, columns), jnp.bfloat16),
            pltpu.VMEM((tokens, columns), jnp.bfloat16),
            pltpu.VMEM((4, rows, columns), jnp.bfloat16),
            pltpu.SemaphoreType.DMA((4,)),
        ],
        input_output_aliases={3 + len(flat): 0} if before else {},
        flops=8 * CHIPS * rows * tokens * columns,
        moved=8 * CHIPS * rows * columns,
        vmem=32,
    )(where, same, other, *flat, *before)


def paired_body(acts, gate_w, up_w, panel_units):
    model = lax.axis_index("mp")
    block = lax.axis_index("dp")
    side = lax.axis_index("tensor")
    sizes = tuple(lax.axis_size(name) for name in AXES)
    chip, core = block // 2, block % 2
    gate, up = gate_w[0], up_w[0]
    units = gate.shape[1]
    picks = panel_units.reshape(2, 2, sizes[1], -1)
    tile = picks.shape[3]
    half = units // 2 // tile
    large = (half - 1) // 2
    chunks = [large, half - 2 - large, 1, 1]
    starts = [0, large, half - 2, half - 1]

    def b_sides(m, d, t):
        return (m, d, 1 - t) if m == 1 else None

    def both_sides(m, d, t):
        return m, d, 1 - t

    def a_sides(m, d, t):
        return (m, d, 1 - t) if m == 0 else None

    def b_to_a(m, d, t):
        return (0, d, t) if m == 1 else None

    def b_to_far_a(m, d, t):
        return (0, d, 1 - t) if m == 1 else None

    def a_to_b(m, d, t):
        return (1, d, t) if m == 0 else None

    middle = acts.shape[2] // 2
    same = [gather_line(acts[0][:, :middle], sizes)]
    other = [send(same[0], sizes, other_core)]
    last = shifts(acts[0][:, middle:], sizes)

    to_side = jnp.stack([(1 - side) * half, chip, core]).astype(jnp.int32)
    own_side = jnp.stack([side * half, chip, core, side]).astype(jnp.int32)
    early = early_products(to_side, same[0], other[0], gate, up, tile, half)
    same.append(join(last, [early]))
    other.append(send(same[1], sizes, other_core))
    sent = []
    for first, count in zip(starts, chunks):
        sent.append(
            late_products(
                to_side, early, same[1], other[1], gate, up, tile, first, count, sent[-1:]
            )
        )
    kept = kept_products(own_side, same, other, gate, up, sent[-1:])

    picks = lax.dynamic_index_in_dim(picks, block, axis=2, keepdims=False) - block * units
    picks_far = lax.dynamic_index_in_dim(picks, 1 - side, axis=1, keepdims=False)
    picks_own = lax.dynamic_index_in_dim(picks, side, axis=1, keepdims=False).reshape(1, -1)
    bases = [(to_side[0] + first) * tile for first in starts] + [own_side[0] * tile, model]
    bases = jnp.stack(bases).astype(jnp.int32)
    parts = sent + [kept]
    shared_b = pick(bases, picks_far[1:], parts, sent[2:3], tile, [])
    shared_a = pick(bases, picks_far[:1], parts, sent[3:], tile, [shared_b])
    picked_own = pick(bases, picks_own, parts, [], tile, [shared_a])
    came = [send(part, sizes, b_sides) for part in sent[:2]]
    came += [send(part, sizes, both_sides) for part in (shared_b, shared_a)]

    rows_b = send(panel_scores(picked_own, came[2], 1), sizes, a_to_b)
    rows_a = panel_scores(picked_own, came[3], 0)
    panel = gather_line(jnp.where(model == 0, rows_a, rows_b), sizes)
    panel_other = send(panel, sizes, other_core)

    z = unit_scores(kept, came[:1], 0)
    a_mine = send(z, sizes, b_to_a)
    a_far = send(a_mine, sizes, a_sides)
    pieces = [(a_mine, a_far, z, send(a_far, sizes, a_to_b))]

    z = unit_scores(kept, came[1:3], starts[1] * tile)
    a_mine = send(z, sizes, b_to_a)
    far = send(jnp.where(model == 0, a_mine, z), sizes, both_sides)
    pieces.append((a_mine, far, z, far))

    z = unit_scores(kept, came[3:], starts[3] * tile)
    pieces.append(
        (send(z, sizes, b_to_a), send(z, sizes, b_to_far_a), z, send(z, sizes, b_sides))
    )

    where = (model, chip, core, side)
    result = scores(where, panel, panel_other, pieces[:1], tile, 0, half, [])
    return scores(where, panel, panel_other, pieces[1:], tile, starts[1], half, [result])


def solution(mesh):
    in_specs = (P("mp", "dp", "tensor"), P("mp", "tensor", "dp"), P("mp", "tensor", "dp"), P())
    out_specs = P(("mp", "tensor"), "dp")
    paired = mesh.shape["mp"] == 2 and mesh.shape["tensor"] == 2 and mesh.shape["dp"] == 2 * CHIPS

    def body(acts, gate_w, up_w, panel_units):
        picked = panel_units.shape[0] // (4 * 2 * CHIPS)
        units = gate_w.shape[2]
        fits = picked % 128 == 0 and units % (2 * picked) == 0 and units % 512 == 0
        fits = fits and units >= 8 * picked and acts.shape[2] % 512 == 0
        if paired and fits and acts.shape[1] % 16 == 0:
            return paired_body(acts, gate_w, up_w, panel_units)
        return general_body(acts, gate_w, up_w, panel_units)

    return jax.shard_map(body, mesh=mesh, in_specs=in_specs, out_specs=out_specs, check_vma=False)
```

```python
import functools
import math

import jax
import jax.numpy as jnp
from jax import lax
from jax.experimental import pallas as pl
from jax.experimental.pallas import tpu as pltpu
from jax.sharding import PartitionSpec as P

epsilon = 1e-05
AXES = ("mp", "dp", "tensor")
MIB = 1 << 20


def from_partner(block, axis, distance):
    count = lax.axis_size(axis)
    route = []
    for low in range(count):
        high = low | 1 << distance
        if high != low and high < count:
            route += [(low, high), (high, low)]
    return lax.ppermute(block, axis, route)


def cross_models(full_units, panel_own, panel_next, model_index):
    other_units, other_panel = from_partner((full_units, panel_next), "mp", 0)
    is_first = model_index == 0
    return (
        jnp.where(is_first, panel_own, other_panel),
        jnp.where(is_first, other_units, full_units),
    )


def general_body(acts, gate_w, up_w, panel_units):
    model_index = lax.axis_index("mp")
    unit_block = lax.axis_index("dp")
    n_model = lax.axis_size("mp")
    n_data = lax.axis_size("dp")
    n_width = lax.axis_size("tensor")
    weight_gate = gate_w[0]
    weight_up = up_w[0]
    units = weight_gate.shape[1]
    gathered = lax.all_gather(acts[0], "dp", axis=0, tiled=True)
    tokens = gathered.shape[0]
    token_share = tokens // n_width
    score_scale = 1.0 / math.sqrt(tokens)
    panel_picks = panel_units.reshape(n_model, n_width, n_data, -1)
    panel_picks = (
        lax.dynamic_index_in_dim(panel_picks, unit_block, axis=2, keepdims=False)
        - unit_block * units
    )
    gate_part = jnp.dot(gathered, weight_gate, preferred_element_type=jnp.float32)
    up_part = jnp.dot(gathered, weight_up, preferred_element_type=jnp.float32)
    summed = lax.psum_scatter(
        jnp.concatenate([gate_part, up_part], axis=1).astype(jnp.bfloat16),
        "tensor",
        scatter_dimension=0,
        tiled=True,
    ).astype(jnp.float32)
    hidden = (jax.nn.silu(summed[:, :units]) * summed[:, units:]).astype(jnp.bfloat16)
    wide_hidden = hidden.astype(jnp.float32)
    totals = lax.psum(
        (jnp.sum(wide_hidden, axis=0), jnp.sum(wide_hidden * wide_hidden, axis=0)), "tensor"
    )
    unit_mean = totals[0] / tokens
    unit_var = totals[1] / tokens - unit_mean * unit_mean
    scored = ((wide_hidden - unit_mean) * lax.rsqrt(unit_var + epsilon)).astype(jnp.bfloat16)
    full_units = lax.all_gather(scored, "tensor", axis=0, tiled=True)
    order_list = panel_picks.transpose(1, 0, 2).reshape(-1)
    chosen = jnp.take(scored, order_list, axis=1).reshape(token_share, n_width, -1)
    moved_rows = lax.all_to_all(chosen, "tensor", split_axis=1, concat_axis=0, tiled=True)
    moved_rows = moved_rows.reshape(tokens, n_model, -1)
    panel_cols = lax.all_gather(moved_rows, "dp", axis=2, tiled=True)
    mine_a, mine_b = cross_models(full_units, panel_cols[:, 0], panel_cols[:, 1], model_index)
    result = lax.dot_general(
        mine_a, mine_b, (((0,), (0,)), ((), ())), preferred_element_type=jnp.float32
    )
    return (result * score_scale).astype(jnp.bfloat16)


CHIPS = 4


def routes(sizes, move):
    n_model, n_data, n_width = sizes
    pairs = []
    for m in range(n_model):
        for d in range(n_data):
            for t in range(n_width):
                to = move(m, d, t)
                if to is not None:
                    source = (m * n_data + d) * n_width + t
                    pairs.append((source, (to[0] * n_data + to[1]) * n_width + to[2]))
    return pairs


def send(block, sizes, move):
    return lax.ppermute(block, AXES, routes(sizes, move))


def other_core(m, d, t):
    return m, d ^ 1, t


def shifted(step):
    def move(m, d, t):
        return m, (d + 2 * step) % (2 * CHIPS), t

    return move


def shifts(block, sizes):
    came = [send(block, sizes, shifted(step)) for step in (1, CHIPS - 1, 2)]
    return [block, came[0], came[2], came[1]]


def join_kernel(*refs):
    rows = refs[0].shape[0]
    for i in range(CHIPS):
        refs[-1][i * rows : (i + 1) * rows, :] = refs[i][...]


def join(blocks, after):
    rows, width = blocks[0].shape
    vmem = pl.BlockSpec(memory_space=pltpu.VMEM)
    return call(
        join_kernel,
        out_shape=jax.ShapeDtypeStruct((CHIPS * rows, width), blocks[0].dtype),
        in_specs=[vmem] * CHIPS + [pl.BlockSpec(memory_space=pl.ANY)] * len(after),
        out_specs=vmem,
        flops=0,
        moved=4 * CHIPS * rows * width,
        vmem=16,
    )(*blocks, *after)


def canonical(index, chip, core):
    line = lax.rem(chip + CHIPS - index % CHIPS, CHIPS)
    return line * 2 + (core if index < CHIPS else 1 - core)


def call(kernel, *, flops, moved, vmem, **rest):
    return pl.pallas_call(
        kernel,
        compiler_params=pltpu.CompilerParams(vmem_limit_bytes=vmem * MIB),
        cost_estimate=pl.CostEstimate(flops=flops, bytes_accessed=moved, transcendentals=0),
        **rest,
    )


def choose_kernel(model_ref, first_ref, second_ref, out_ref):
    for holder, ref in enumerate((first_ref, second_ref)):

        @pl.when(model_ref[0] == holder)
        def _():
            out_ref[...] = ref[...]


def choose(model_number, first, second):
    vmem = pl.BlockSpec(memory_space=pltpu.VMEM)
    return call(
        choose_kernel,
        out_shape=jax.ShapeDtypeStruct(first.shape, first.dtype),
        in_specs=[pl.BlockSpec(memory_space=pltpu.SMEM), vmem, vmem],
        out_specs=vmem,
        flops=0,
        moved=4 * first.size,
        vmem=16,
    )(model_number, first, second)


def early_kernel(place_ref, same_ref, other_ref, gate_ref, up_ref, *refs):
    out_ref = refs[-1]
    x = jnp.concatenate([same_ref[...], other_ref[...]], axis=0)
    out_ref[0] = jnp.dot(x, gate_ref[...], preferred_element_type=jnp.float32)
    out_ref[1] = jnp.dot(x, up_ref[...], preferred_element_type=jnp.float32)


def early_products(place, same, other, gate, up, tile, count, after):
    tokens, width = 2 * same.shape[0], same.shape[1]
    weights = pl.BlockSpec((width, tile), lambda i, place_ref: (0, place_ref[0] + i))
    whole = pl.BlockSpec(same.shape, lambda i, place_ref: (0, 0))
    return call(
        early_kernel,
        out_shape=jax.ShapeDtypeStruct((2, tokens, tile * count), jnp.float32),
        grid_spec=pltpu.PrefetchScalarGridSpec(
            num_scalar_prefetch=1,
            grid=(count,),
            in_specs=[whole, whole, weights, weights]
            + [pl.BlockSpec(memory_space=pl.ANY)] * len(after),
            out_specs=pl.BlockSpec((2, tokens, tile), lambda i, place_ref: (0, 0, i)),
        ),
        flops=4 * tokens * width * tile * count,
        moved=4 * width * tile * count,
        vmem=38,
    )(place, same, other, gate, up, *after)


def store_sorted(place_ref, out_ref, which, total):
    rows = total.shape[0] // (2 * CHIPS)
    total = total.astype(jnp.bfloat16)
    for i in range(2 * CHIPS):
        start = pl.multiple_of(canonical(i, place_ref[1], place_ref[2]) * rows, rows)
        out_ref[which, pl.ds(start, rows), :] = total[i * rows : (i + 1) * rows]


def late_kernel(place_ref, early_ref, same_ref, other_ref, gate_ref, up_ref, *refs):
    x = jnp.concatenate([same_ref[...], other_ref[...]], axis=0)
    for which, weight_ref in enumerate((gate_ref, up_ref)):
        total = jnp.dot(x, weight_ref[...], preferred_element_type=jnp.float32)
        store_sorted(place_ref, refs[-1], which, early_ref[which] + total)


def late_products(place, early, same, other, gate, up, tile, first, count, after):
    tokens, width = 2 * same.shape[0], same.shape[1]
    weights = pl.BlockSpec((width, tile), lambda i, place_ref: (1, place_ref[0] + first + i))
    whole = pl.BlockSpec(same.shape, lambda i, place_ref: (0, 0))
    return call(
        late_kernel,
        out_shape=jax.ShapeDtypeStruct((2, tokens, tile * count), jnp.bfloat16),
        grid_spec=pltpu.PrefetchScalarGridSpec(
            num_scalar_prefetch=1,
            grid=(count,),
            in_specs=[
                pl.BlockSpec((2, tokens, tile), lambda i, place_ref: (0, 0, first + i)),
                whole,
                whole,
                weights,
                weights,
            ]
            + [pl.BlockSpec(memory_space=pl.ANY)] * len(after),
            out_specs=pl.BlockSpec((2, tokens, tile), lambda i, place_ref: (0, 0, i)),
        ),
        flops=4 * tokens * width * tile * count,
        moved=4 * width * tile * count,
        vmem=38,
    )(place, early, same, other, gate, up, *after)


def kept_kernel(place_ref, same_a, other_a, same_b, other_b, gate_ref, up_ref, *refs):
    width = same_a.shape[1]
    xs = [
        jnp.concatenate([same_ref[...], other_ref[...]], axis=0)
        for same_ref, other_ref in ((same_a, other_a), (same_b, other_b))
    ]
    for which, weight_ref in enumerate((gate_ref, up_ref)):
        total = jnp.dot(xs[0], weight_ref[:width], preferred_element_type=jnp.float32)
        total += jnp.dot(xs[1], weight_ref[width:], preferred_element_type=jnp.float32)
        store_sorted(place_ref, refs[-1], which, total)


def kept_products(place, same, other, gate, up, tile, count, after):
    tokens, width = 2 * same[0].shape[0], same[0].shape[1]
    weights = pl.BlockSpec((2 * width, tile), lambda i, place_ref: (0, place_ref[0] + i))
    whole = pl.BlockSpec(same[0].shape, lambda i, place_ref: (0, 0))
    return call(
        kept_kernel,
        out_shape=jax.ShapeDtypeStruct((2, tokens, tile * count), jnp.bfloat16),
        grid_spec=pltpu.PrefetchScalarGridSpec(
            num_scalar_prefetch=1,
            grid=(count,),
            in_specs=[whole] * 4
            + [weights, weights]
            + [pl.BlockSpec(memory_space=pl.ANY)] * len(after),
            out_specs=pl.BlockSpec((2, tokens, tile), lambda i, place_ref: (0, 0, i)),
        ),
        flops=8 * tokens * width * tile * count,
        moved=8 * width * tile * count,
        vmem=38,
    )(place, same[0], other[0], same[1], other[1], gate, up, *after)


def pick_kernel(counts, tile, instead, bases_ref, picks_ref, *refs):
    out_ref = refs[-1]
    tokens, picked = out_ref.shape[1:]

    @pl.when(bases_ref[len(counts)] == 0)
    def _():
        total = jnp.zeros((2 * tokens, picked), jnp.float32)
        for part, (ref, count) in enumerate(zip(refs[: len(counts)], counts)):
            for i in range(count):
                base = bases_ref[part] + i * tile
                unit = lax.broadcasted_iota(jnp.int32, (tile, picked), 0) + base
                chosen = jnp.where(unit == picks_ref[...], 1.0, 0.0).astype(jnp.bfloat16)
                block = ref[:, :, i * tile : (i + 1) * tile].reshape(2 * tokens, tile)
                total += jnp.dot(block, chosen, preferred_element_type=jnp.float32)
        out_ref[...] = total.astype(jnp.bfloat16).reshape(2, tokens, picked)

    @pl.when(bases_ref[len(counts)] == 1)
    def _():
        if instead is None:
            out_ref[...] = jnp.zeros_like(out_ref)
        else:
            part, start = instead
            out_ref[...] = refs[part][:, :, start : start + picked]


def pick(bases, picks, parts, instead, tile, after):
    tokens = parts[0].shape[1]
    picked = picks.shape[1]
    counts = [part.shape[2] // tile for part in parts]
    vmem = pl.BlockSpec(memory_space=pltpu.VMEM)
    return call(
        functools.partial(pick_kernel, counts, tile, instead),
        out_shape=jax.ShapeDtypeStruct((2, tokens, picked), jnp.bfloat16),
        in_specs=[pl.BlockSpec(memory_space=pltpu.SMEM), vmem]
        + [vmem] * len(parts)
        + [pl.BlockSpec(memory_space=pl.ANY)] * len(after),
        out_specs=vmem,
        flops=4 * tokens * picked * tile * sum(counts),
        moved=4 * tokens * tile * sum(counts),
        vmem=16,
    )(bases, picks, *parts, *after)


def zscore(mine, theirs):
    tokens = mine.shape[1]
    gate = mine[0].astype(jnp.float32) + theirs[0].astype(jnp.float32)
    up = mine[1].astype(jnp.float32) + theirs[1].astype(jnp.float32)
    hidden = (gate / (1.0 + jnp.exp(-gate)) * up).astype(jnp.bfloat16).astype(jnp.float32)
    mean = jnp.sum(hidden, axis=0, keepdims=True) / tokens
    var = jnp.sum(hidden * hidden, axis=0, keepdims=True) / tokens - mean * mean
    return (hidden - mean) * lax.rsqrt(var + epsilon)


def unit_kernel(bounds, mine_ref, *refs):
    out_ref = refs[-1]
    for (start, stop), theirs_ref in zip(bounds, refs):
        out_ref[:, start - bounds[0][0] : stop - bounds[0][0]] = zscore(
            mine_ref[:, :, start:stop], theirs_ref[...]
        ).astype(jnp.bfloat16)


def unit_scores(mine, theirs, start):
    tokens = mine.shape[1]
    bounds = []
    for part in theirs:
        bounds.append((start, start + part.shape[2]))
        start = bounds[-1][1]
    count = start - bounds[0][0]
    vmem = pl.BlockSpec(memory_space=pltpu.VMEM)
    return call(
        functools.partial(unit_kernel, bounds),
        out_shape=jax.ShapeDtypeStruct((tokens, count), jnp.bfloat16),
        in_specs=[vmem] * (1 + len(theirs)),
        out_specs=vmem,
        flops=20 * tokens * count,
        moved=10 * tokens * count,
        vmem=16,
    )(mine, *theirs)


def panel_kernel(mine_ref, theirs_ref, out_ref):
    out_ref[...] = zscore(mine_ref[...], theirs_ref[...]).T.astype(jnp.bfloat16)


def panel_kernel_or(model_ref, mine_ref, theirs_ref, given_ref, out_ref):
    @pl.when(model_ref[0] == 0)
    def _():
        panel_kernel(mine_ref, theirs_ref, out_ref)

    @pl.when(model_ref[0] == 1)
    def _():
        out_ref[...] = given_ref[...]


def panel_scores(mine, theirs, first, given=()):
    _, tokens, count = theirs.shape
    rows = pl.BlockSpec((count, tokens), lambda i: (0, 0))
    units = [
        pl.BlockSpec((2, tokens, count), lambda i: (0, 0, first)),
        pl.BlockSpec((2, tokens, count), lambda i: (0, 0, 0)),
    ]
    return call(
        panel_kernel_or if given else panel_kernel,
        out_shape=jax.ShapeDtypeStruct((count, tokens), jnp.bfloat16),
        grid=(1,),
        in_specs=[pl.BlockSpec(memory_space=pltpu.SMEM), *units, rows] if given else units,
        out_specs=rows,
        flops=20 * tokens * count,
        moved=10 * tokens * count,
        vmem=16,
    )(*given[:1], mine, theirs, *given[1:])


def score_kernel(scale, tile, n_pieces, has_before, where_ref, panel_ref, *refs):
    pieces = refs[: 4 * n_pieces]
    out_ref, near_ref, far_ref, block_ref, sems = refs[4 * n_pieces + has_before :]
    model, near_column, far_column = (where_ref[i] for i in range(3))
    rows, columns = block_ref.shape[1:]

    def assemble(at, into):
        start = 0
        for piece in range(n_pieces):
            ref = pieces[4 * piece + at]
            into[:, start : start + ref.shape[1]] = ref[...]
            start += ref.shape[1]

    for holder in range(2):

        @pl.when(model == holder)
        def _():
            assemble(2 * holder, near_ref)
            assemble(2 * holder + 1, far_ref)

    def copy(slot, row, column):
        return pltpu.make_async_copy(
            block_ref.at[slot],
            out_ref.at[
                pl.ds(pl.multiple_of(row, rows), rows), pl.ds(pl.multiple_of(column, 128), columns)
            ],
            sems.at[slot],
        )

    def step(index, carry):
        for which in range(2):
            row = (2 * index + which) * rows
            for far, units_ref in enumerate((near_ref, far_ref)):
                slot = 2 * which + far
                column = far_column if far else near_column

                @pl.when(index > 0)
                def _():
                    copy(slot, row, column).wait()

                for start in range(0, columns, tile):
                    total = jnp.dot(
                        panel_ref[pl.ds(pl.multiple_of(row, rows), rows), :],
                        units_ref[:, start : start + tile],
                        preferred_element_type=jnp.float32,
                    )
                    block_ref[slot, :, start : start + tile] = (total * scale).astype(jnp.bfloat16)
                copy(slot, row, column).start()
        return carry

    lax.fori_loop(0, panel_ref.shape[0] // (2 * rows), step, 0)
    for slot in range(4):
        copy(slot, 0, 0).wait()


def scores(where, panel, pieces, tile, half, before):
    rows, tokens = panel.shape
    columns = sum(piece[0].shape[1] for piece in pieces)
    vmem = pl.BlockSpec(memory_space=pltpu.VMEM)
    anywhere = pl.BlockSpec(memory_space=pl.ANY)
    flat = [array for piece in pieces for array in piece]
    return call(
        functools.partial(score_kernel, 1.0 / math.sqrt(tokens), tile, len(pieces), len(before)),
        out_shape=jax.ShapeDtypeStruct((rows, 2 * half * tile), jnp.bfloat16),
        in_specs=[pl.BlockSpec(memory_space=pltpu.SMEM), vmem]
        + [vmem] * len(flat)
        + [anywhere] * len(before),
        out_specs=anywhere,
        scratch_shapes=[
            pltpu.VMEM((tokens, columns), jnp.bfloat16),
            pltpu.VMEM((tokens, columns), jnp.bfloat16),
            pltpu.VMEM((4, rows // 4, columns), jnp.bfloat16),
            pltpu.SemaphoreType.DMA((4,)),
        ],
        input_output_aliases={2 + len(flat): 0} if before else {},
        flops=4 * rows * tokens * columns,
        moved=4 * rows * columns,
        vmem=16,
    )(where, panel, *flat, *before)


def paired_body(acts, gate_w, up_w, panel_units):
    model = lax.axis_index("mp")
    block = lax.axis_index("dp")
    side = lax.axis_index("tensor")
    sizes = tuple(lax.axis_size(name) for name in AXES)
    chip, core = block // 2, block % 2
    gate, up = gate_w[0], up_w[0]
    units = gate.shape[1]
    picks = panel_units.reshape(2, 2, sizes[1], -1)
    tile = picks.shape[3]
    half = units // 2 // tile
    large = (half - 1) // 2
    chunks = [large, half - 2 - large, 2]
    starts = [0, large, half - 2]

    def b_sides(m, d, t):
        return (m, d, 1 - t) if m == 1 else None

    def both_sides(m, d, t):
        return m, d, 1 - t

    def a_sides(m, d, t):
        return (m, d, 1 - t) if m == 0 else None

    def b_to_a(m, d, t):
        return (0, d, t) if m == 1 else None

    def b_to_far_a(m, d, t):
        return (0, d, 1 - t) if m == 1 else None

    def a_to_b(m, d, t):
        return (1, d, t) if m == 0 else None

    middle = acts.shape[2] // 2
    same = [join(shifts(acts[0][:, :middle], sizes), [])]
    other = [send(same[0], sizes, other_core)]
    last = shifts(acts[0][:, middle:], sizes)

    picks = lax.dynamic_index_in_dim(picks, block, axis=2, keepdims=False) - block * units
    picks_far = lax.dynamic_index_in_dim(picks, 1 - side, axis=1, keepdims=False)
    picks_b, picks_a = picks_far[1:], picks_far[:1]
    picks_own = lax.dynamic_index_in_dim(picks, side, axis=1, keepdims=False).reshape(1, -1)
    bases = [((1 - side) * half + first) * tile for first in starts] + [side * half * tile, model]
    bases = jnp.stack(bases).astype(jnp.int32)
    model_number = jnp.reshape(model, (1,)).astype(jnp.int32)
    targets = [
        jnp.stack([model, (side * half + first) * tile, ((1 - side) * half + first) * tile])
        for first in (0, starts[2])
    ]
    targets = [target.astype(jnp.int32) for target in targets]

    to_side = jnp.stack([(1 - side) * half, chip, core]).astype(jnp.int32)
    own_side = jnp.stack([side * half, chip, core]).astype(jnp.int32)
    early = early_products(
        to_side,
        same[0],
        other[0],
        gate,
        up,
        tile,
        half,
        [own_side, picks_b, picks_a, picks_own, bases, model_number, *targets],
    )
    same.append(join(last, [early]))
    other.append(send(same[1], sizes, other_core))
    sent = []
    for first, count in zip(starts, chunks):
        sent.append(
            late_products(
                to_side, early, same[1], other[1], gate, up, tile, first, count, sent[-1:]
            )
        )
    kept = kept_products(own_side, same, other, gate, up, tile, half, sent[-1:])

    parts = sent + [kept]
    shared_b = pick(bases, picks_b, parts, (2, 0), tile, [])
    shared_a = pick(bases, picks_a, parts, (2, tile), tile, [shared_b])
    picked_own = pick(bases, picks_own, parts, None, tile, [shared_a])
    came = [send(part, sizes, b_sides) for part in sent[:2]]
    came += [send(part, sizes, both_sides) for part in (shared_b, shared_a)]

    rows_b = send(panel_scores(picked_own, came[2], 1), sizes, a_to_b)
    rows = panel_scores(picked_own, came[3], 0, (model_number, rows_b))
    panel = lax.all_gather(rows, "dp", axis=0, tiled=True)

    z = unit_scores(kept, came[:1], 0)
    a_mine = send(z, sizes, b_to_a)
    a_far = send(a_mine, sizes, a_sides)
    pieces = [(a_mine, a_far, z, send(a_far, sizes, a_to_b))]

    z = unit_scores(kept, came[1:2], starts[1] * tile)
    a_mine = send(z, sizes, b_to_a)
    far = send(choose(model_number, a_mine, z), sizes, both_sides)
    pieces.append((a_mine, far, z, far))

    z = unit_scores(kept, came[2:], starts[2] * tile)
    pieces.append(
        (send(z, sizes, b_to_a), send(z, sizes, b_to_far_a), z, send(z, sizes, b_sides))
    )

    result = scores(targets[0], panel, pieces[:2], tile, half, [])
    return scores(targets[1], panel, pieces[2:], tile, half, [result])


def solution(mesh):
    in_specs = (P("mp", "dp", "tensor"), P("mp", "tensor", "dp"), P("mp", "tensor", "dp"), P())
    out_specs = P(("mp", "tensor"), "dp")
    paired = mesh.shape["mp"] == 2 and mesh.shape["tensor"] == 2 and mesh.shape["dp"] == 2 * CHIPS

    def body(acts, gate_w, up_w, panel_units):
        picked = panel_units.shape[0] // (4 * 2 * CHIPS)
        units = gate_w.shape[2]
        fits = picked % 128 == 0 and units % (2 * picked) == 0 and units % 512 == 0
        fits = fits and units >= 8 * picked and acts.shape[2] % 512 == 0
        if paired and fits and acts.shape[1] % 16 == 0:
            return paired_body(acts, gate_w, up_w, panel_units)
        return general_body(acts, gate_w, up_w, panel_units)

    return jax.shard_map(body, mesh=mesh, in_specs=in_specs, out_specs=out_specs, check_vma=False)
```

```python
import functools
import math

import jax
import jax.numpy as jnp
from jax import lax
from jax.experimental import pallas as pl
from jax.experimental.pallas import tpu as pltpu
from jax.sharding import PartitionSpec as P

epsilon = 1e-05
AXES = ("mp", "dp", "tensor")
MIB = 1 << 20


def from_partner(block, axis, distance):
    count = lax.axis_size(axis)
    route = []
    for low in range(count):
        high = low | 1 << distance
        if high != low and high < count:
            route += [(low, high), (high, low)]
    return lax.ppermute(block, axis, route)


def cross_models(full_units, panel_own, panel_next, model_index):
    other_units, other_panel = from_partner((full_units, panel_next), "mp", 0)
    is_first = model_index == 0
    return (
        jnp.where(is_first, panel_own, other_panel),
        jnp.where(is_first, other_units, full_units),
    )


def general_body(acts, gate_w, up_w, panel_units):
    model_index = lax.axis_index("mp")
    unit_block = lax.axis_index("dp")
    n_model = lax.axis_size("mp")
    n_data = lax.axis_size("dp")
    n_width = lax.axis_size("tensor")
    weight_gate = gate_w[0]
    weight_up = up_w[0]
    units = weight_gate.shape[1]
    gathered = lax.all_gather(acts[0], "dp", axis=0, tiled=True)
    tokens = gathered.shape[0]
    token_share = tokens // n_width
    score_scale = 1.0 / math.sqrt(tokens)
    panel_picks = panel_units.reshape(n_model, n_width, n_data, -1)
    panel_picks = (
        lax.dynamic_index_in_dim(panel_picks, unit_block, axis=2, keepdims=False)
        - unit_block * units
    )
    gate_part = jnp.dot(gathered, weight_gate, preferred_element_type=jnp.float32)
    up_part = jnp.dot(gathered, weight_up, preferred_element_type=jnp.float32)
    summed = lax.psum_scatter(
        jnp.concatenate([gate_part, up_part], axis=1).astype(jnp.bfloat16),
        "tensor",
        scatter_dimension=0,
        tiled=True,
    ).astype(jnp.float32)
    hidden = (jax.nn.silu(summed[:, :units]) * summed[:, units:]).astype(jnp.bfloat16)
    wide_hidden = hidden.astype(jnp.float32)
    totals = lax.psum(
        (jnp.sum(wide_hidden, axis=0), jnp.sum(wide_hidden * wide_hidden, axis=0)), "tensor"
    )
    unit_mean = totals[0] / tokens
    unit_var = totals[1] / tokens - unit_mean * unit_mean
    scored = ((wide_hidden - unit_mean) * lax.rsqrt(unit_var + epsilon)).astype(jnp.bfloat16)
    full_units = lax.all_gather(scored, "tensor", axis=0, tiled=True)
    order_list = panel_picks.transpose(1, 0, 2).reshape(-1)
    chosen = jnp.take(scored, order_list, axis=1).reshape(token_share, n_width, -1)
    moved_rows = lax.all_to_all(chosen, "tensor", split_axis=1, concat_axis=0, tiled=True)
    moved_rows = moved_rows.reshape(tokens, n_model, -1)
    panel_cols = lax.all_gather(moved_rows, "dp", axis=2, tiled=True)
    mine_a, mine_b = cross_models(full_units, panel_cols[:, 0], panel_cols[:, 1], model_index)
    result = lax.dot_general(
        mine_a, mine_b, (((0,), (0,)), ((), ())), preferred_element_type=jnp.float32
    )
    return (result * score_scale).astype(jnp.bfloat16)


CHIPS = 4


def routes(sizes, move):
    n_model, n_data, n_width = sizes
    pairs = []
    for m in range(n_model):
        for d in range(n_data):
            for t in range(n_width):
                to = move(m, d, t)
                if to is not None:
                    source = (m * n_data + d) * n_width + t
                    pairs.append((source, (to[0] * n_data + to[1]) * n_width + to[2]))
    return pairs


def send(block, sizes, move):
    return lax.ppermute(block, AXES, routes(sizes, move))


def other_core(m, d, t):
    return m, d ^ 1, t


def shifted(step):
    def move(m, d, t):
        return m, (d + 2 * step) % (2 * CHIPS), t

    return move


def shifts(block, sizes):
    came = [send(block, sizes, shifted(step)) for step in (1, CHIPS - 1, 2)]
    return [block, came[0], came[2], came[1]]


def join_kernel(count, *refs):
    rows = refs[0].shape[0]
    for i in range(count):
        refs[-1][i * rows : (i + 1) * rows, :] = refs[i][...]


def join(blocks, after):
    rows, width = blocks[0].shape
    count = len(blocks)
    vmem = pl.BlockSpec(memory_space=pltpu.VMEM)
    return call(
        functools.partial(join_kernel, count),
        out_shape=jax.ShapeDtypeStruct((count * rows, width), blocks[0].dtype),
        in_specs=[vmem] * count + [pl.BlockSpec(memory_space=pl.ANY)] * len(after),
        out_specs=vmem,
        flops=0,
        moved=4 * count * rows * width,
        vmem=16,
    )(*blocks, *after)


def swapped(block, sizes, distance):
    return send(block, sizes, lambda m, d, t: (m, d ^ (2 * distance), t))


SWAPS = (0, 2, 1, 3)


def canonical(index, chip, core):
    line = lax.rem(chip + CHIPS - index % CHIPS, CHIPS)
    return line * 2 + (core if index < CHIPS else 1 - core)


def call(kernel, *, flops, moved, vmem, **rest):
    return pl.pallas_call(
        kernel,
        compiler_params=pltpu.CompilerParams(vmem_limit_bytes=vmem * MIB),
        cost_estimate=pl.CostEstimate(flops=flops, bytes_accessed=moved, transcendentals=0),
        **rest,
    )


def choose_kernel(model_ref, first_ref, second_ref, out_ref):
    for holder, ref in enumerate((first_ref, second_ref)):

        @pl.when(model_ref[0] == holder)
        def _():
            out_ref[...] = ref[...]


def choose(model_number, first, second):
    vmem = pl.BlockSpec(memory_space=pltpu.VMEM)
    return call(
        choose_kernel,
        out_shape=jax.ShapeDtypeStruct(first.shape, first.dtype),
        in_specs=[pl.BlockSpec(memory_space=pltpu.SMEM), vmem, vmem],
        out_specs=vmem,
        flops=0,
        moved=4 * first.size,
        vmem=16,
    )(model_number, first, second)


def products_kernel(place_ref, same_ref, other_ref, gate_ref, up_ref, *refs):
    out_ref = refs[-1]
    rows = same_ref.shape[0] // CHIPS
    x = jnp.concatenate([same_ref[...], other_ref[...]], axis=0)
    for which, weight_ref in enumerate((gate_ref, up_ref)):
        total = jnp.dot(x, weight_ref[...], preferred_element_type=jnp.float32)
        total = total.astype(jnp.bfloat16)
        for i in range(2 * CHIPS):
            start = pl.multiple_of(canonical(i, place_ref[1], place_ref[2]) * rows, rows)
            out_ref[which, pl.ds(start, rows), :] = total[i * rows : (i + 1) * rows]


def products(place, same, other, gate, up, tile, first, count, after):
    tokens, width = 2 * same.shape[0], same.shape[1]
    weights = pl.BlockSpec((width, tile), lambda i, place_ref: (0, place_ref[0] + first + i))
    whole = pl.BlockSpec(same.shape, lambda i, place_ref: (0, 0))
    return call(
        products_kernel,
        out_shape=jax.ShapeDtypeStruct((2, tokens, tile * count), jnp.bfloat16),
        grid_spec=pltpu.PrefetchScalarGridSpec(
            num_scalar_prefetch=1,
            grid=(count,),
            in_specs=[whole, whole, weights, weights]
            + [pl.BlockSpec(memory_space=pl.ANY)] * len(after),
            out_specs=pl.BlockSpec((2, tokens, tile), lambda i, place_ref: (0, 0, i)),
        ),
        flops=4 * tokens * width * tile * count,
        moved=4 * width * tile * count,
        vmem=38,
    )(place, same, other, gate, up, *after)


def pick_kernel(counts, tile, bases_ref, picks_ref, *refs):
    out_ref = refs[-1]
    tokens, picked = out_ref.shape[1:]

    @pl.when(bases_ref[len(counts)] == 0)
    def _():
        total = jnp.zeros((2 * tokens, picked), jnp.float32)
        for part, (ref, count) in enumerate(zip(refs[: len(counts)], counts)):
            for i in range(count):
                base = bases_ref[part] + i * tile
                unit = lax.broadcasted_iota(jnp.int32, (tile, picked), 0) + base
                chosen = jnp.where(unit == picks_ref[...], 1.0, 0.0).astype(jnp.bfloat16)
                block = ref[:, :, i * tile : (i + 1) * tile].reshape(2 * tokens, tile)
                total += jnp.dot(block, chosen, preferred_element_type=jnp.float32)
        out_ref[...] = total.astype(jnp.bfloat16).reshape(2, tokens, picked)

    @pl.when(bases_ref[len(counts)] == 1)
    def _():
        out_ref[...] = jnp.zeros_like(out_ref)


def pick(bases, picks, parts, tile, after):
    tokens = parts[0].shape[1]
    picked = picks.shape[1]
    counts = [part.shape[2] // tile for part in parts]
    vmem = pl.BlockSpec(memory_space=pltpu.VMEM)
    return call(
        functools.partial(pick_kernel, counts, tile),
        out_shape=jax.ShapeDtypeStruct((2, tokens, picked), jnp.bfloat16),
        in_specs=[pl.BlockSpec(memory_space=pltpu.SMEM), vmem]
        + [vmem] * len(parts)
        + [pl.BlockSpec(memory_space=pl.ANY)] * len(after),
        out_specs=vmem,
        flops=4 * tokens * picked * tile * sum(counts),
        moved=4 * tokens * tile * sum(counts),
        vmem=16,
    )(bases, picks, *parts, *after)


def zscore(mine, theirs):
    tokens = mine.shape[1]
    gate = mine[0].astype(jnp.float32) + theirs[0].astype(jnp.float32)
    up = mine[1].astype(jnp.float32) + theirs[1].astype(jnp.float32)
    hidden = (gate / (1.0 + jnp.exp(-gate)) * up).astype(jnp.bfloat16).astype(jnp.float32)
    mean = jnp.sum(hidden, axis=0, keepdims=True) / tokens
    var = jnp.sum(hidden * hidden, axis=0, keepdims=True) / tokens - mean * mean
    return (hidden - mean) * lax.rsqrt(var + epsilon)


def unit_kernel(mine_ref, theirs_ref, *refs):
    refs[-1][...] = zscore(mine_ref[...], theirs_ref[...]).astype(jnp.bfloat16)


def unit_scores(mine, theirs, tile, first, after):
    _, tokens, count = theirs.shape
    return call(
        unit_kernel,
        out_shape=jax.ShapeDtypeStruct((tokens, count), jnp.bfloat16),
        grid=(count // tile,),
        in_specs=[
            pl.BlockSpec((2, tokens, tile), lambda i: (0, 0, first + i)),
            pl.BlockSpec((2, tokens, tile), lambda i: (0, 0, i)),
        ]
        + [pl.BlockSpec(memory_space=pl.ANY)] * len(after),
        out_specs=pl.BlockSpec((tokens, tile), lambda i: (0, i)),
        flops=20 * tokens * count,
        moved=10 * tokens * count,
        vmem=16,
    )(mine, theirs, *after)


def panel_kernel(mine_ref, theirs_ref, out_ref):
    out_ref[...] = zscore(mine_ref[...], theirs_ref[...]).T.astype(jnp.bfloat16)


def panel_kernel_or(model_ref, mine_ref, theirs_ref, given_ref, *refs):
    out_ref = refs[-1]

    @pl.when(model_ref[0] == 0)
    def _():
        panel_kernel(mine_ref, theirs_ref, out_ref)

    @pl.when(model_ref[0] == 1)
    def _():
        out_ref[...] = given_ref[...]


def panel_scores(mine, theirs, first, given=(), after=()):
    _, tokens, count = theirs.shape
    rows = pl.BlockSpec((count, tokens), lambda i: (0, 0))
    units = [
        pl.BlockSpec((2, tokens, count), lambda i: (0, 0, first)),
        pl.BlockSpec((2, tokens, count), lambda i: (0, 0, 0)),
    ]
    return call(
        panel_kernel_or if given else panel_kernel,
        out_shape=jax.ShapeDtypeStruct((count, tokens), jnp.bfloat16),
        grid=(1,),
        in_specs=(
            [pl.BlockSpec(memory_space=pltpu.SMEM), *units, rows]
            + [pl.BlockSpec(memory_space=pl.ANY)] * len(after)
            if given
            else units
        ),
        out_specs=rows,
        flops=20 * tokens * count,
        moved=10 * tokens * count,
        vmem=16,
    )(*given[:1], mine, theirs, *given[1:], *after)


def score_kernel(scale, tile, cores, n_pieces, has_before, where_ref, *refs):
    panels, refs = refs[: len(cores)], refs[len(cores) :]
    pieces = refs[: 4 * n_pieces]
    out_ref, panel_ref, near_ref, far_ref, block_ref, in_sems, out_sems = refs[
        4 * n_pieces + has_before :
    ]
    model, chip, core, near_column, far_column = (where_ref[i] for i in range(5))
    rows = block_ref.shape[2]
    columns = block_ref.shape[3]

    def fetch(at):
        copies = [
            pltpu.make_async_copy(ref, panel_ref.at[i], in_sems.at[i])
            for i, ref in enumerate(panels)
        ]
        for far, into in enumerate((near_ref, far_ref)):
            start = 0
            for piece in range(n_pieces):
                ref = pieces[4 * piece + at + far]
                stop = start + ref.shape[1]
                copies.append(
                    pltpu.make_async_copy(
                        ref, into.at[:, start:stop], in_sems.at[len(cores) + 2 * piece + far]
                    )
                )
                start = stop
        for copy in copies:
            copy.start()
        for copy in copies:
            copy.wait()

    for holder in range(2):

        @pl.when(model == holder)
        def _():
            fetch(2 * holder)

    copies = []
    for which, other in enumerate(cores):
        for pair in range(CHIPS // 2):
            panel = panel_ref[which, 2 * pair * rows : (2 * pair + 2) * rows, :]
            for units_ref, column in ((near_ref, near_column), (far_ref, far_column)):
                slot = len(copies) // 2
                for start in range(0, columns, tile):
                    total = jnp.dot(
                        panel,
                        units_ref[:, start : start + tile],
                        preferred_element_type=jnp.float32,
                    )
                    block_ref[slot, :, :, start : start + tile] = (
                        (total * scale).astype(jnp.bfloat16).reshape(2, rows, tile)
                    )
                for i in range(2):
                    line = lax.bitwise_xor(chip, SWAPS[2 * pair + i])
                    place = line * 2 + (1 - core if other else core)
                    copies.append(
                        pltpu.make_async_copy(
                            block_ref.at[slot, i],
                            out_ref.at[
                                pl.ds(pl.multiple_of(place * rows, rows), rows),
                                pl.ds(pl.multiple_of(column, 128), columns),
                            ],
                            out_sems.at[slot, i],
                        )
                    )
                    copies[-1].start()
    for copy in copies:
        copy.wait()


def scores(where, panels, cores, pieces, tile, shape, before, after):
    rows, tokens = panels[0].shape
    columns = sum(piece[0].shape[1] for piece in pieces)
    slots = len(panels) * CHIPS
    anywhere = pl.BlockSpec(memory_space=pl.ANY)
    flat = [array for piece in pieces for array in piece]
    return call(
        functools.partial(
            score_kernel,
            1.0 / math.sqrt(tokens),
            tile,
            cores,
            len(pieces),
            len(before) + len(after),
        ),
        out_shape=jax.ShapeDtypeStruct(shape, jnp.bfloat16),
        in_specs=[pl.BlockSpec(memory_space=pltpu.SMEM)]
        + [anywhere] * (len(panels) + len(flat) + len(before) + len(after)),
        out_specs=anywhere,
        scratch_shapes=[
            pltpu.VMEM((len(panels), rows, tokens), jnp.bfloat16),
            pltpu.VMEM((tokens, columns), jnp.bfloat16),
            pltpu.VMEM((tokens, columns), jnp.bfloat16),
            pltpu.VMEM((slots, 2, rows // CHIPS, columns), jnp.bfloat16),
            pltpu.SemaphoreType.DMA((len(panels) + 2 * len(pieces),)),
            pltpu.SemaphoreType.DMA((slots, 2)),
        ],
        input_output_aliases={1 + len(panels) + len(flat): 0} if before else {},
        flops=4 * len(panels) * rows * tokens * columns,
        moved=4 * len(panels) * rows * columns,
        vmem=24,
    )(where, *panels, *flat, *before, *after)


def paired_body(acts, gate_w, up_w, panel_units):
    model = lax.axis_index("mp")
    block = lax.axis_index("dp")
    side = lax.axis_index("tensor")
    sizes = tuple(lax.axis_size(name) for name in AXES)
    chip, core = block // 2, block % 2
    gate, up = gate_w[0], up_w[0]
    units = gate.shape[1]
    picks = panel_units.reshape(2, 2, sizes[1], -1)
    tile = picks.shape[3]
    half = units // 2 // tile
    chunks = [2, half - 4, 2]
    starts = [0, 2, half - 2]

    def b_sides(m, d, t):
        return (m, d, 1 - t) if m == 1 else None

    def both_sides(m, d, t):
        return m, d, 1 - t

    def a_sides(m, d, t):
        return (m, d, 1 - t) if m == 0 else None

    def b_to_a(m, d, t):
        return (0, d, t) if m == 1 else None

    def b_to_far_a(m, d, t):
        return (0, d, 1 - t) if m == 1 else None

    def a_to_b(m, d, t):
        return (1, d, t) if m == 0 else None

    same = join(shifts(acts[0], sizes), [])
    other = send(same, sizes, other_core)

    picks = lax.dynamic_index_in_dim(picks, block, axis=2, keepdims=False) - block * units
    picks_far = lax.dynamic_index_in_dim(picks, 1 - side, axis=1, keepdims=False)
    picks_b, picks_a = picks_far[1:], picks_far[:1]
    picks_own = lax.dynamic_index_in_dim(picks, side, axis=1, keepdims=False).reshape(1, -1)
    bases = [((1 - side) * half + first) * tile for first in starts] + [side * half * tile, model]
    bases = jnp.stack(bases).astype(jnp.int32)
    model_number = jnp.reshape(model, (1,)).astype(jnp.int32)
    targets = [
        jnp.stack(
            [model, chip, core, (side * half + first) * tile, ((1 - side) * half + first) * tile]
        )
        for first in (0, starts[2])
    ]
    targets = [target.astype(jnp.int32) for target in targets]

    to_side = jnp.stack([(1 - side) * half, chip, core]).astype(jnp.int32)
    own_side = jnp.stack([side * half, chip, core]).astype(jnp.int32)
    ready = [own_side, picks_b, picks_a, picks_own, bases, model_number, *targets]
    sent, came = [], []
    for first, count in zip(starts, chunks):
        sent.append(
            products(to_side, same, other, gate, up, tile, first, count, sent[-1:] or ready)
        )
        came.append(send(sent[-1], sizes, b_sides))
    kept = products(own_side, same, other, gate, up, tile, 0, half, sent[-1:])

    z = [unit_scores(kept, came[0], tile, starts[0], [])]

    parts = sent + [kept]
    picked_b = pick(bases, picks_b, parts, tile, [came[1], z[0]])
    picked_own = pick(bases, picks_own, parts, tile, [picked_b])
    picked_a = pick(bases, picks_a, parts, tile, [picked_own])
    rows_b = panel_scores(picked_own, send(picked_b, sizes, a_sides), 1)
    rows_b = send(rows_b, sizes, a_to_b)
    a_mine = send(z[0], sizes, b_to_a)
    rows = panel_scores(
        picked_own, send(picked_a, sizes, a_sides), 0, (model_number, rows_b), (a_mine,)
    )

    z.append(unit_scores(kept, came[1], tile, starts[1], [picked_a]))
    z.append(unit_scores(kept, came[2], tile, starts[2], []))
    a_far = send(a_mine, sizes, a_sides)
    pieces = [(a_mine, a_far, z[0], send(a_far, sizes, a_to_b))]
    a_mine = send(z[1], sizes, b_to_a)
    far = send(choose(model_number, a_mine, z[1]), sizes, both_sides)
    pieces.append((a_mine, far, z[1], far))
    pieces.append(
        (
            send(z[2], sizes, b_to_a),
            send(z[2], sizes, b_to_far_a),
            z[2],
            send(z[2], sizes, b_sides),
        )
    )

    panel = join([rows, swapped(rows, sizes, 2)], [z[2], a_far])
    arrived = [pieces[0][3], far, pieces[2][0], pieces[2][1], pieces[2][3]]
    panel = join([panel, swapped(panel, sizes, 1)], arrived)
    panel_other = send(panel, sizes, other_core)
    shape = (2 * CHIPS * rows.shape[0], units)
    result = scores(targets[0], [panel], (0,), pieces[:2], tile, shape, [], [])
    result = scores(targets[0], [panel_other], (1,), pieces[:2], tile, shape, [result], [])
    return scores(
        targets[1], [panel, panel_other], (0, 1), pieces[2:], tile, shape, [result], []
    )


def solution(mesh):
    in_specs = (P("mp", "dp", "tensor"), P("mp", "tensor", "dp"), P("mp", "tensor", "dp"), P())
    out_specs = P(("mp", "tensor"), "dp")
    paired = mesh.shape["mp"] == 2 and mesh.shape["tensor"] == 2 and mesh.shape["dp"] == 2 * CHIPS

    def body(acts, gate_w, up_w, panel_units):
        picked = panel_units.shape[0] // (4 * 2 * CHIPS)
        units = gate_w.shape[2]
        fits = picked % 128 == 0 and units % (2 * picked) == 0 and units % 512 == 0
        fits = fits and units >= 10 * picked
        if paired and fits and acts.shape[1] % 16 == 0:
            return paired_body(acts, gate_w, up_w, panel_units)
        return general_body(acts, gate_w, up_w, panel_units)

    return jax.shard_map(body, mesh=mesh, in_specs=in_specs, out_specs=out_specs, check_vma=False)
```

```python
import functools
import math

import jax
import jax.numpy as jnp
from jax import lax
from jax.experimental import pallas as pl
from jax.experimental.pallas import tpu as pltpu
from jax.sharding import PartitionSpec as P

epsilon = 1e-05
AXES = ("mp", "dp", "tensor")
MIB = 1 << 20


def from_partner(block, axis, distance):
    count = lax.axis_size(axis)
    route = []
    for low in range(count):
        high = low | 1 << distance
        if high != low and high < count:
            route += [(low, high), (high, low)]
    return lax.ppermute(block, axis, route)


def cross_models(full_units, panel_own, panel_next, model_index):
    other_units, other_panel = from_partner((full_units, panel_next), "mp", 0)
    is_first = model_index == 0
    return (
        jnp.where(is_first, panel_own, other_panel),
        jnp.where(is_first, other_units, full_units),
    )


def general_body(acts, gate_w, up_w, panel_units):
    model_index = lax.axis_index("mp")
    unit_block = lax.axis_index("dp")
    n_model = lax.axis_size("mp")
    n_data = lax.axis_size("dp")
    n_width = lax.axis_size("tensor")
    weight_gate = gate_w[0]
    weight_up = up_w[0]
    units = weight_gate.shape[1]
    gathered = lax.all_gather(acts[0], "dp", axis=0, tiled=True)
    tokens = gathered.shape[0]
    token_share = tokens // n_width
    score_scale = 1.0 / math.sqrt(tokens)
    panel_picks = panel_units.reshape(n_model, n_width, n_data, -1)
    panel_picks = (
        lax.dynamic_index_in_dim(panel_picks, unit_block, axis=2, keepdims=False)
        - unit_block * units
    )
    gate_part = jnp.dot(gathered, weight_gate, preferred_element_type=jnp.float32)
    up_part = jnp.dot(gathered, weight_up, preferred_element_type=jnp.float32)
    summed = lax.psum_scatter(
        jnp.concatenate([gate_part, up_part], axis=1).astype(jnp.bfloat16),
        "tensor",
        scatter_dimension=0,
        tiled=True,
    ).astype(jnp.float32)
    hidden = (jax.nn.silu(summed[:, :units]) * summed[:, units:]).astype(jnp.bfloat16)
    wide_hidden = hidden.astype(jnp.float32)
    totals = lax.psum(
        (jnp.sum(wide_hidden, axis=0), jnp.sum(wide_hidden * wide_hidden, axis=0)), "tensor"
    )
    unit_mean = totals[0] / tokens
    unit_var = totals[1] / tokens - unit_mean * unit_mean
    scored = ((wide_hidden - unit_mean) * lax.rsqrt(unit_var + epsilon)).astype(jnp.bfloat16)
    full_units = lax.all_gather(scored, "tensor", axis=0, tiled=True)
    order_list = panel_picks.transpose(1, 0, 2).reshape(-1)
    chosen = jnp.take(scored, order_list, axis=1).reshape(token_share, n_width, -1)
    moved_rows = lax.all_to_all(chosen, "tensor", split_axis=1, concat_axis=0, tiled=True)
    moved_rows = moved_rows.reshape(tokens, n_model, -1)
    panel_cols = lax.all_gather(moved_rows, "dp", axis=2, tiled=True)
    mine_a, mine_b = cross_models(full_units, panel_cols[:, 0], panel_cols[:, 1], model_index)
    result = lax.dot_general(
        mine_a, mine_b, (((0,), (0,)), ((), ())), preferred_element_type=jnp.float32
    )
    return (result * score_scale).astype(jnp.bfloat16)


CHIPS = 4


def routes(sizes, move):
    n_model, n_data, n_width = sizes
    pairs = []
    for m in range(n_model):
        for d in range(n_data):
            for t in range(n_width):
                to = move(m, d, t)
                if to is not None:
                    source = (m * n_data + d) * n_width + t
                    pairs.append((source, (to[0] * n_data + to[1]) * n_width + to[2]))
    return pairs


def send(block, sizes, move):
    return lax.ppermute(block, AXES, routes(sizes, move))


def other_core(m, d, t):
    return m, d ^ 1, t


def shifted(step):
    def move(m, d, t):
        return m, (d + 2 * step) % (2 * CHIPS), t

    return move


def shifts(block, sizes):
    came = [send(block, sizes, shifted(step)) for step in (1, CHIPS - 1, 2)]
    return [block, came[0], came[2], came[1]]


def join_kernel(count, *refs):
    out_ref, sems = refs[-2:]
    rows = refs[0].shape[0]
    copies = [
        pltpu.make_async_copy(refs[i], out_ref.at[i * rows : (i + 1) * rows, :], sems.at[i])
        for i in range(count)
    ]
    for copy in copies:
        copy.start()
    for copy in copies:
        copy.wait()


def join(blocks, after):
    rows, width = blocks[0].shape
    count = len(blocks)
    return call(
        functools.partial(join_kernel, count),
        out_shape=jax.ShapeDtypeStruct((count * rows, width), blocks[0].dtype),
        in_specs=[pl.BlockSpec(memory_space=pl.ANY)] * (count + len(after)),
        out_specs=pl.BlockSpec(memory_space=pltpu.VMEM),
        scratch_shapes=[pltpu.SemaphoreType.DMA((count,))],
        flops=0,
        moved=4 * count * rows * width,
        vmem=16,
    )(*blocks, *after)


def swapped(block, sizes, distance):
    return send(block, sizes, lambda m, d, t: (m, d ^ (2 * distance), t))


SWAPS = (0, 2, 1, 3)


def canonical(index, chip, core):
    line = lax.rem(chip + CHIPS - index % CHIPS, CHIPS)
    return line * 2 + (core if index < CHIPS else 1 - core)


def call(kernel, *, flops, moved, vmem, **rest):
    return pl.pallas_call(
        kernel,
        compiler_params=pltpu.CompilerParams(vmem_limit_bytes=vmem * MIB),
        cost_estimate=pl.CostEstimate(flops=flops, bytes_accessed=moved, transcendentals=0),
        **rest,
    )


def choose_kernel(model_ref, first_ref, second_ref, out_ref):
    for holder, ref in enumerate((first_ref, second_ref)):

        @pl.when(model_ref[0] == holder)
        def _():
            out_ref[...] = ref[...]


def choose(model_number, first, second):
    vmem = pl.BlockSpec(memory_space=pltpu.VMEM)
    return call(
        choose_kernel,
        out_shape=jax.ShapeDtypeStruct(first.shape, first.dtype),
        in_specs=[pl.BlockSpec(memory_space=pltpu.SMEM), vmem, vmem],
        out_specs=vmem,
        flops=0,
        moved=4 * first.size,
        vmem=16,
    )(model_number, first, second)


def products_kernel(counts, n_after, place_ref, same_ref, other_ref, gate_ref, up_ref, *refs):
    rows = same_ref.shape[0] // CHIPS
    step = pl.program_id(0)

    def write(out_ref):
        x = jnp.concatenate([same_ref[...], other_ref[...]], axis=0)
        for which, weight_ref in enumerate((gate_ref, up_ref)):
            total = jnp.dot(x, weight_ref[...], preferred_element_type=jnp.float32)
            total = total.astype(jnp.bfloat16)
            for i in range(2 * CHIPS):
                start = pl.multiple_of(canonical(i, place_ref[0], place_ref[1]) * rows, rows)
                out_ref[which, pl.ds(start, rows), :] = total[i * rows : (i + 1) * rows]

    first = 0
    for count, out_ref in zip(counts, refs[n_after:]):

        @pl.when((step >= first) & (step < first + count))
        def _():
            write(out_ref)

        first += count


def products(place, same, other, gate, up, tile, counts, after):
    tokens, width = 2 * same.shape[0], same.shape[1]
    firsts = [sum(counts[:i]) for i in range(len(counts))]

    def weight_tile(i, place_ref):
        column = place_ref[2] + i
        for run in range(1, len(counts)):
            column = jnp.where(i >= firsts[run], place_ref[2 + run] + i - firsts[run], column)
        return 0, column

    def out_tile(run):
        return lambda i, place_ref: (0, 0, jnp.clip(i - firsts[run], 0, counts[run] - 1))

    weights = pl.BlockSpec((width, tile), weight_tile)
    whole = pl.BlockSpec(same.shape, lambda i, place_ref: (0, 0))
    return call(
        functools.partial(products_kernel, counts, len(after)),
        out_shape=[
            jax.ShapeDtypeStruct((2, tokens, tile * count), jnp.bfloat16) for count in counts
        ],
        grid_spec=pltpu.PrefetchScalarGridSpec(
            num_scalar_prefetch=1,
            grid=(sum(counts),),
            in_specs=[whole, whole, weights, weights]
            + [pl.BlockSpec(memory_space=pl.ANY)] * len(after),
            out_specs=[
                pl.BlockSpec((2, tokens, tile), out_tile(run)) for run in range(len(counts))
            ],
        ),
        flops=4 * tokens * width * tile * sum(counts),
        moved=4 * width * tile * sum(counts),
        vmem=38,
    )(place, same, other, gate, up, *after)


def pick_kernel(counts, tile, bases_ref, picks_ref, *refs):
    out_ref = refs[-1]
    tokens, picked = out_ref.shape[1:]

    @pl.when(bases_ref[len(counts)] == 0)
    def _():
        total = jnp.zeros((2 * tokens, picked), jnp.float32)
        for part, (ref, count) in enumerate(zip(refs[: len(counts)], counts)):
            for i in range(count):
                base = bases_ref[part] + i * tile
                unit = lax.broadcasted_iota(jnp.int32, (tile, picked), 0) + base
                chosen = jnp.where(unit == picks_ref[...], 1.0, 0.0).astype(jnp.bfloat16)
                block = ref[:, :, i * tile : (i + 1) * tile].reshape(2 * tokens, tile)
                total += jnp.dot(block, chosen, preferred_element_type=jnp.float32)
        out_ref[...] = total.astype(jnp.bfloat16).reshape(2, tokens, picked)

    @pl.when(bases_ref[len(counts)] == 1)
    def _():
        out_ref[...] = jnp.zeros_like(out_ref)


def pick(bases, picks, parts, tile, after):
    tokens = parts[0].shape[1]
    picked = picks.shape[1]
    counts = [part.shape[2] // tile for part in parts]
    vmem = pl.BlockSpec(memory_space=pltpu.VMEM)
    return call(
        functools.partial(pick_kernel, counts, tile),
        out_shape=jax.ShapeDtypeStruct((2, tokens, picked), jnp.bfloat16),
        in_specs=[pl.BlockSpec(memory_space=pltpu.SMEM), vmem]
        + [vmem] * len(parts)
        + [pl.BlockSpec(memory_space=pl.ANY)] * len(after),
        out_specs=vmem,
        flops=4 * tokens * picked * tile * sum(counts),
        moved=4 * tokens * tile * sum(counts),
        vmem=16,
    )(bases, picks, *parts, *after)


def zscore(mine, theirs):
    tokens = mine.shape[1]
    gate = mine[0].astype(jnp.float32) + theirs[0].astype(jnp.float32)
    up = mine[1].astype(jnp.float32) + theirs[1].astype(jnp.float32)
    hidden = (gate / (1.0 + jnp.exp(-gate)) * up).astype(jnp.bfloat16).astype(jnp.float32)
    mean = jnp.sum(hidden, axis=0, keepdims=True) / tokens
    var = jnp.sum(hidden * hidden, axis=0, keepdims=True) / tokens - mean * mean
    return (hidden - mean) * lax.rsqrt(var + epsilon)


def unit_kernel(counts, mine_ref, *refs):
    first = 0
    for count, theirs_ref in zip(counts, refs):

        @pl.when((pl.program_id(0) >= first) & (pl.program_id(0) < first + count))
        def _():
            refs[-1][...] = zscore(mine_ref[...], theirs_ref[...]).astype(jnp.bfloat16)

        first += count


def unit_scores(mine, theirs, tile, first, after):
    tokens = mine.shape[1]
    counts = [part.shape[2] // tile for part in theirs]
    firsts = [sum(counts[:i]) for i in range(len(counts))]

    def their_tile(run):
        return lambda i: (0, 0, jnp.clip(i - firsts[run], 0, counts[run] - 1))

    units = tile * sum(counts)
    return call(
        functools.partial(unit_kernel, counts),
        out_shape=jax.ShapeDtypeStruct((tokens, units), jnp.bfloat16),
        grid=(sum(counts),),
        in_specs=[pl.BlockSpec((2, tokens, tile), lambda i: (0, 0, first + i))]
        + [pl.BlockSpec((2, tokens, tile), their_tile(run)) for run in range(len(theirs))]
        + [pl.BlockSpec(memory_space=pl.ANY)] * len(after),
        out_specs=pl.BlockSpec((tokens, tile), lambda i: (0, i)),
        flops=20 * tokens * units,
        moved=10 * tokens * units,
        vmem=16,
    )(mine, *theirs, *after)


def panel_kernel(mine_ref, theirs_ref, out_ref):
    out_ref[...] = zscore(mine_ref[...], theirs_ref[...]).T.astype(jnp.bfloat16)


def panel_kernel_or(model_ref, mine_ref, theirs_ref, given_ref, *refs):
    out_ref = refs[-1]

    @pl.when(model_ref[0] == 0)
    def _():
        panel_kernel(mine_ref, theirs_ref, out_ref)

    @pl.when(model_ref[0] == 1)
    def _():
        out_ref[...] = given_ref[...]


def panel_scores(mine, theirs, first, given=(), after=()):
    _, tokens, count = theirs.shape
    rows = pl.BlockSpec((count, tokens), lambda i: (0, 0))
    units = [
        pl.BlockSpec((2, tokens, count), lambda i: (0, 0, first)),
        pl.BlockSpec((2, tokens, count), lambda i: (0, 0, 0)),
    ]
    return call(
        panel_kernel_or if given else panel_kernel,
        out_shape=jax.ShapeDtypeStruct((count, tokens), jnp.bfloat16),
        grid=(1,),
        in_specs=(
            [pl.BlockSpec(memory_space=pltpu.SMEM), *units, rows]
            + [pl.BlockSpec(memory_space=pl.ANY)] * len(after)
            if given
            else units
        ),
        out_specs=rows,
        flops=20 * tokens * count,
        moved=10 * tokens * count,
        vmem=16,
    )(*given[:1], mine, theirs, *given[1:], *after)


def score_kernel(scale, tile, cores, n_pieces, has_before, where_ref, *refs):
    panels, refs = refs[: len(cores)], refs[len(cores) :]
    pieces = refs[: 4 * n_pieces]
    out_ref, panel_ref, near_ref, far_ref, block_ref, in_sems, out_sems = refs[
        4 * n_pieces + has_before :
    ]
    model, chip, core, near_column, far_column = (where_ref[i] for i in range(5))
    rows = block_ref.shape[2]
    columns = block_ref.shape[3]

    def fetch(at):
        copies = [
            pltpu.make_async_copy(ref, panel_ref.at[i], in_sems.at[i])
            for i, ref in enumerate(panels)
        ]
        for far, into in enumerate((near_ref, far_ref)):
            start = 0
            for piece in range(n_pieces):
                ref = pieces[4 * piece + at + far]
                stop = start + ref.shape[1]
                copies.append(
                    pltpu.make_async_copy(
                        ref, into.at[:, start:stop], in_sems.at[len(cores) + 2 * piece + far]
                    )
                )
                start = stop
        for copy in copies:
            copy.start()
        for copy in copies:
            copy.wait()

    for holder in range(2):

        @pl.when(model == holder)
        def _():
            fetch(2 * holder)

    copies = []
    for which, other in enumerate(cores):
        for pair in range(CHIPS // 2):
            panel = panel_ref[which, 2 * pair * rows : (2 * pair + 2) * rows, :]
            for units_ref, column in ((near_ref, near_column), (far_ref, far_column)):
                slot = len(copies) // 2
                for start in range(0, columns, tile):
                    total = jnp.dot(
                        panel,
                        units_ref[:, start : start + tile],
                        preferred_element_type=jnp.float32,
                    )
                    block_ref[slot, :, :, start : start + tile] = (
                        (total * scale).astype(jnp.bfloat16).reshape(2, rows, tile)
                    )
                for i in range(2):
                    line = lax.bitwise_xor(chip, SWAPS[2 * pair + i])
                    place = line * 2 + (1 - core if other else core)
                    copies.append(
                        pltpu.make_async_copy(
                            block_ref.at[slot, i],
                            out_ref.at[
                                pl.ds(pl.multiple_of(place * rows, rows), rows),
                                pl.ds(pl.multiple_of(column, 128), columns),
                            ],
                            out_sems.at[slot, i],
                        )
                    )
                    copies[-1].start()
    for copy in copies:
        copy.wait()


def scores(where, panels, cores, pieces, tile, shape, before, after):
    rows, tokens = panels[0].shape
    columns = sum(piece[0].shape[1] for piece in pieces)
    slots = len(panels) * CHIPS
    anywhere = pl.BlockSpec(memory_space=pl.ANY)
    flat = [array for piece in pieces for array in piece]
    return call(
        functools.partial(
            score_kernel,
            1.0 / math.sqrt(tokens),
            tile,
            cores,
            len(pieces),
            len(before) + len(after),
        ),
        out_shape=jax.ShapeDtypeStruct(shape, jnp.bfloat16),
        in_specs=[pl.BlockSpec(memory_space=pltpu.SMEM)]
        + [anywhere] * (len(panels) + len(flat) + len(before) + len(after)),
        out_specs=anywhere,
        scratch_shapes=[
            pltpu.VMEM((len(panels), rows, tokens), jnp.bfloat16),
            pltpu.VMEM((tokens, columns), jnp.bfloat16),
            pltpu.VMEM((tokens, columns), jnp.bfloat16),
            pltpu.VMEM((slots, 2, rows // CHIPS, columns), jnp.bfloat16),
            pltpu.SemaphoreType.DMA((len(panels) + 2 * len(pieces),)),
            pltpu.SemaphoreType.DMA((slots, 2)),
        ],
        input_output_aliases={1 + len(panels) + len(flat): 0} if before else {},
        flops=4 * len(panels) * rows * tokens * columns,
        moved=4 * len(panels) * rows * columns,
        vmem=24,
    )(where, *panels, *flat, *before, *after)


def paired_body(acts, gate_w, up_w, panel_units):
    model = lax.axis_index("mp")
    block = lax.axis_index("dp")
    side = lax.axis_index("tensor")
    sizes = tuple(lax.axis_size(name) for name in AXES)
    chip, core = block // 2, block % 2
    gate, up = gate_w[0], up_w[0]
    units = gate.shape[1]
    picks = panel_units.reshape(2, 2, sizes[1], -1)
    tile = picks.shape[3]
    half = units // 2 // tile
    chunks = [2, half - 4, 2]
    starts = [0, 2, half - 2]

    def b_sides(m, d, t):
        return (m, d, 1 - t) if m == 1 else None

    def both_sides(m, d, t):
        return m, d, 1 - t

    def a_sides(m, d, t):
        return (m, d, 1 - t) if m == 0 else None

    def b_to_a(m, d, t):
        return (0, d, t) if m == 1 else None

    def b_to_far_a(m, d, t):
        return (0, d, 1 - t) if m == 1 else None

    def a_to_b(m, d, t):
        return (1, d, t) if m == 0 else None

    same = join(shifts(acts[0], sizes), [])
    other = send(same, sizes, other_core)

    picks = lax.dynamic_index_in_dim(picks, block, axis=2, keepdims=False) - block * units
    picks_far = lax.dynamic_index_in_dim(picks, 1 - side, axis=1, keepdims=False)
    picks_b, picks_a = picks_far[1:], picks_far[:1]
    picks_own = lax.dynamic_index_in_dim(picks, side, axis=1, keepdims=False).reshape(1, -1)
    bases = [((1 - side) * half + first) * tile for first in starts] + [side * half * tile, model]
    bases = jnp.stack(bases).astype(jnp.int32)
    model_number = jnp.reshape(model, (1,)).astype(jnp.int32)
    target = [model, chip, core, side * half * tile, (1 - side) * half * tile]
    target = jnp.stack(target).astype(jnp.int32)

    to_side, own_side = (1 - side) * half, side * half
    places = [
        [chip, core, to_side],
        [chip, core, to_side + starts[1]],
        [chip, core, to_side + starts[2], own_side],
    ]
    places = [jnp.stack(place).astype(jnp.int32) for place in places]
    ready = [picks_b, picks_a, picks_own, bases, model_number, *places, target]
    sent = products(places[0], same, other, gate, up, tile, chunks[:1], ready)
    sent += products(places[1], same, other, gate, up, tile, chunks[1:2], sent)
    sent += products(places[2], same, other, gate, up, tile, [chunks[2], half], sent[1:])
    kept = sent[-1]
    came = [send(part, sizes, b_sides) for part in sent[:3]]

    z = [unit_scores(kept, came[:2], tile, 0, [])]
    picked_b = pick(bases, picks_b, sent, tile, [z[0]])
    picked_own = pick(bases, picks_own, sent, tile, [picked_b])
    picked_a = pick(bases, picks_a, sent, tile, [picked_own])
    rows_b = panel_scores(picked_own, send(picked_b, sizes, a_sides), 1)
    rows_b = send(rows_b, sizes, a_to_b)
    rows = panel_scores(
        picked_own, send(picked_a, sizes, a_sides), 0, (model_number, rows_b)
    )

    a_mine = send(z[0], sizes, b_to_a)
    chosen = choose(model_number, a_mine, z[0])
    far = send(chosen, sizes, both_sides)
    pieces = [(a_mine, far, z[0], far)]
    z.append(unit_scores(kept, came[2:], tile, starts[2], [rows]))
    direct = [send(z[1], sizes, move) for move in (b_to_a, b_to_far_a, b_sides)]
    pieces.append((direct[0], direct[1], z[1], direct[2]))

    panel = join([rows, swapped(rows, sizes, 2)], [z[1], chosen])
    panel = join([panel, swapped(panel, sizes, 1)], direct)
    panel_other = send(panel, sizes, other_core)
    shape = (2 * CHIPS * rows.shape[0], units)
    result = scores(target, [panel], (0,), pieces, tile, shape, [], [])
    return scores(target, [panel_other], (1,), pieces, tile, shape, [result], [])


def solution(mesh):
    in_specs = (P("mp", "dp", "tensor"), P("mp", "tensor", "dp"), P("mp", "tensor", "dp"), P())
    out_specs = P(("mp", "tensor"), "dp")
    paired = mesh.shape["mp"] == 2 and mesh.shape["tensor"] == 2 and mesh.shape["dp"] == 2 * CHIPS

    def body(acts, gate_w, up_w, panel_units):
        picked = panel_units.shape[0] // (4 * 2 * CHIPS)
        units = gate_w.shape[2]
        fits = picked % 128 == 0 and units % (2 * picked) == 0 and units % 512 == 0
        fits = fits and units >= 10 * picked
        if paired and fits and acts.shape[1] % 16 == 0:
            return paired_body(acts, gate_w, up_w, panel_units)
        return general_body(acts, gate_w, up_w, panel_units)

    return jax.shard_map(body, mesh=mesh, in_specs=in_specs, out_specs=out_specs, check_vma=False)
```

```python
import functools
import math

import jax
import jax.numpy as jnp
from jax import lax
from jax.experimental import pallas as pl
from jax.experimental.pallas import tpu as pltpu
from jax.sharding import PartitionSpec as P

epsilon = 1e-05
AXES = ("mp", "dp", "tensor")
MIB = 1 << 20


def from_partner(block, axis, distance):
    count = lax.axis_size(axis)
    route = []
    for low in range(count):
        high = low | 1 << distance
        if high != low and high < count:
            route += [(low, high), (high, low)]
    return lax.ppermute(block, axis, route)


def cross_models(full_units, panel_own, panel_next, model_index):
    other_units, other_panel = from_partner((full_units, panel_next), "mp", 0)
    is_first = model_index == 0
    return (
        jnp.where(is_first, panel_own, other_panel),
        jnp.where(is_first, other_units, full_units),
    )


def general_body(acts, gate_w, up_w, panel_units):
    model_index = lax.axis_index("mp")
    unit_block = lax.axis_index("dp")
    n_model = lax.axis_size("mp")
    n_data = lax.axis_size("dp")
    n_width = lax.axis_size("tensor")
    weight_gate = gate_w[0]
    weight_up = up_w[0]
    units = weight_gate.shape[1]
    gathered = lax.all_gather(acts[0], "dp", axis=0, tiled=True)
    tokens = gathered.shape[0]
    token_share = tokens // n_width
    score_scale = 1.0 / math.sqrt(tokens)
    panel_picks = panel_units.reshape(n_model, n_width, n_data, -1)
    panel_picks = (
        lax.dynamic_index_in_dim(panel_picks, unit_block, axis=2, keepdims=False)
        - unit_block * units
    )
    gate_part = jnp.dot(gathered, weight_gate, preferred_element_type=jnp.float32)
    up_part = jnp.dot(gathered, weight_up, preferred_element_type=jnp.float32)
    summed = lax.psum_scatter(
        jnp.concatenate([gate_part, up_part], axis=1).astype(jnp.bfloat16),
        "tensor",
        scatter_dimension=0,
        tiled=True,
    ).astype(jnp.float32)
    hidden = (jax.nn.silu(summed[:, :units]) * summed[:, units:]).astype(jnp.bfloat16)
    wide_hidden = hidden.astype(jnp.float32)
    totals = lax.psum(
        (jnp.sum(wide_hidden, axis=0), jnp.sum(wide_hidden * wide_hidden, axis=0)), "tensor"
    )
    unit_mean = totals[0] / tokens
    unit_var = totals[1] / tokens - unit_mean * unit_mean
    scored = ((wide_hidden - unit_mean) * lax.rsqrt(unit_var + epsilon)).astype(jnp.bfloat16)
    full_units = lax.all_gather(scored, "tensor", axis=0, tiled=True)
    order_list = panel_picks.transpose(1, 0, 2).reshape(-1)
    chosen = jnp.take(scored, order_list, axis=1).reshape(token_share, n_width, -1)
    moved_rows = lax.all_to_all(chosen, "tensor", split_axis=1, concat_axis=0, tiled=True)
    moved_rows = moved_rows.reshape(tokens, n_model, -1)
    panel_cols = lax.all_gather(moved_rows, "dp", axis=2, tiled=True)
    mine_a, mine_b = cross_models(full_units, panel_cols[:, 0], panel_cols[:, 1], model_index)
    result = lax.dot_general(
        mine_a, mine_b, (((0,), (0,)), ((), ())), preferred_element_type=jnp.float32
    )
    return (result * score_scale).astype(jnp.bfloat16)


CHIPS = 4


def routes(sizes, move):
    n_model, n_data, n_width = sizes
    pairs = []
    for m in range(n_model):
        for d in range(n_data):
            for t in range(n_width):
                to = move(m, d, t)
                if to is not None:
                    source = (m * n_data + d) * n_width + t
                    pairs.append((source, (to[0] * n_data + to[1]) * n_width + to[2]))
    return pairs


def send(block, sizes, move):
    return lax.ppermute(block, AXES, routes(sizes, move))


def other_core(m, d, t):
    return m, d ^ 1, t


def shifted(step):
    def move(m, d, t):
        return m, (d + 2 * step) % (2 * CHIPS), t

    return move


def shifts(block, sizes):
    came = [send(block, sizes, shifted(step)) for step in (1, CHIPS - 1, 2)]
    return [block, came[0], came[2], came[1]]


def join_kernel(count, *refs):
    out_ref, sems = refs[-2:]
    rows = refs[0].shape[0]
    copies = [
        pltpu.make_async_copy(refs[i], out_ref.at[i * rows : (i + 1) * rows, :], sems.at[i])
        for i in range(count)
    ]
    for copy in copies:
        copy.start()
    for copy in copies:
        copy.wait()


def join(blocks, after):
    rows, width = blocks[0].shape
    count = len(blocks)
    return call(
        functools.partial(join_kernel, count),
        out_shape=jax.ShapeDtypeStruct((count * rows, width), blocks[0].dtype),
        in_specs=[pl.BlockSpec(memory_space=pl.ANY)] * (count + len(after)),
        out_specs=pl.BlockSpec(memory_space=pltpu.VMEM),
        scratch_shapes=[pltpu.SemaphoreType.DMA((count,))],
        flops=0,
        moved=0,
        vmem=16,
    )(*blocks, *after)


def swapped(block, sizes, distance):
    return send(block, sizes, lambda m, d, t: (m, d ^ (2 * distance), t))


SWAPS = (0, 2, 1, 3)


def canonical(index, chip, core):
    line = lax.rem(chip + CHIPS - index % CHIPS, CHIPS)
    return line * 2 + (core if index < CHIPS else 1 - core)


def call(kernel, *, flops, moved, vmem, **rest):
    return pl.pallas_call(
        kernel,
        compiler_params=pltpu.CompilerParams(vmem_limit_bytes=vmem * MIB),
        cost_estimate=pl.CostEstimate(flops=flops, bytes_accessed=moved, transcendentals=0),
        **rest,
    )


def products_kernel(counts, n_after, place_ref, same_ref, other_ref, gate_ref, up_ref, *refs):
    rows = same_ref.shape[0] // CHIPS
    step = pl.program_id(0)

    def write(out_ref):
        x = jnp.concatenate([same_ref[...], other_ref[...]], axis=0)
        for which, weight_ref in enumerate((gate_ref, up_ref)):
            total = jnp.dot(x, weight_ref[...], preferred_element_type=jnp.float32)
            total = total.astype(jnp.bfloat16)
            for i in range(2 * CHIPS):
                start = pl.multiple_of(canonical(i, place_ref[0], place_ref[1]) * rows, rows)
                out_ref[which, pl.ds(start, rows), :] = total[i * rows : (i + 1) * rows]

    first = 0
    for count, out_ref in zip(counts, refs[n_after:]):

        @pl.when((step >= first) & (step < first + count))
        def _():
            write(out_ref)

        first += count


def products(place, same, other, gate, up, tile, counts, after):
    tokens, width = 2 * same.shape[0], same.shape[1]
    firsts = [sum(counts[:i]) for i in range(len(counts))]

    def weight_tile(i, place_ref):
        column = place_ref[2] + i
        for run in range(1, len(counts)):
            column = jnp.where(i >= firsts[run], place_ref[2 + run] + i - firsts[run], column)
        return 0, column

    def out_tile(run):
        return lambda i, place_ref: (0, 0, jnp.clip(i - firsts[run], 0, counts[run] - 1))

    weights = pl.BlockSpec((width, tile), weight_tile)
    whole = pl.BlockSpec(same.shape, lambda i, place_ref: (0, 0))
    return call(
        functools.partial(products_kernel, counts, len(after)),
        out_shape=[
            jax.ShapeDtypeStruct((2, tokens, tile * count), jnp.bfloat16) for count in counts
        ],
        grid_spec=pltpu.PrefetchScalarGridSpec(
            num_scalar_prefetch=1,
            grid=(sum(counts),),
            in_specs=[whole, whole, weights, weights]
            + [pl.BlockSpec(memory_space=pl.ANY)] * len(after),
            out_specs=[
                pl.BlockSpec((2, tokens, tile), out_tile(run)) for run in range(len(counts))
            ],
        ),
        flops=4 * tokens * width * tile * sum(counts),
        moved=4 * width * tile * sum(counts),
        vmem=38,
    )(place, same, other, gate, up, *after)


def pick_kernel(counts, tile, bases_ref, picks_ref, *refs):
    out_ref = refs[-1]
    tokens, picked = out_ref.shape[1:]

    @pl.when(bases_ref[len(counts)] == 0)
    def _():
        total = jnp.zeros((2 * tokens, picked), jnp.float32)
        for part, (ref, count) in enumerate(zip(refs[: len(counts)], counts)):
            for i in range(count):
                base = bases_ref[part] + i * tile
                unit = lax.broadcasted_iota(jnp.int32, (tile, picked), 0) + base
                chosen = jnp.where(unit == picks_ref[...], 1.0, 0.0).astype(jnp.bfloat16)
                block = ref[:, :, i * tile : (i + 1) * tile].reshape(2 * tokens, tile)
                total += jnp.dot(block, chosen, preferred_element_type=jnp.float32)
        out_ref[...] = total.astype(jnp.bfloat16).reshape(2, tokens, picked)

    @pl.when(bases_ref[len(counts)] == 1)
    def _():
        out_ref[...] = jnp.zeros_like(out_ref)


def pick(bases, picks, parts, tile, after):
    tokens = parts[0].shape[1]
    picked = picks.shape[1]
    counts = [part.shape[2] // tile for part in parts]
    vmem = pl.BlockSpec(memory_space=pltpu.VMEM)
    return call(
        functools.partial(pick_kernel, counts, tile),
        out_shape=jax.ShapeDtypeStruct((2, tokens, picked), jnp.bfloat16),
        in_specs=[pl.BlockSpec(memory_space=pltpu.SMEM), vmem]
        + [vmem] * len(parts)
        + [pl.BlockSpec(memory_space=pl.ANY)] * len(after),
        out_specs=vmem,
        flops=0,
        moved=0,
        vmem=16,
    )(bases, picks, *parts, *after)


def zscore(mine, theirs):
    tokens = mine.shape[1]
    gate = mine[0].astype(jnp.float32) + theirs[0].astype(jnp.float32)
    up = mine[1].astype(jnp.float32) + theirs[1].astype(jnp.float32)
    hidden = (gate / (1.0 + jnp.exp(-gate)) * up).astype(jnp.bfloat16).astype(jnp.float32)
    mean = jnp.sum(hidden, axis=0, keepdims=True) / tokens
    var = jnp.sum(hidden * hidden, axis=0, keepdims=True) / tokens - mean * mean
    return (hidden - mean) * lax.rsqrt(var + epsilon)


def unit_kernel(model_ref, mine_ref, theirs_ref, *refs):
    @pl.when(model_ref[0] == 1)
    def _():
        refs[-1][...] = zscore(mine_ref[...], theirs_ref[...]).astype(jnp.bfloat16)

    @pl.when(model_ref[0] == 0)
    def _():
        refs[-1][...] = jnp.zeros_like(refs[-1])


def unit_scores(model_number, mine, theirs, tile, first, after):
    _, tokens, units = theirs.shape
    return call(
        unit_kernel,
        out_shape=jax.ShapeDtypeStruct((tokens, units), jnp.bfloat16),
        grid_spec=pltpu.PrefetchScalarGridSpec(
            num_scalar_prefetch=1,
            grid=(units // tile,),
            in_specs=[
                pl.BlockSpec((2, tokens, tile), lambda i, model: (0, 0, (first + i) * model[0])),
                pl.BlockSpec((2, tokens, tile), lambda i, model: (0, 0, i * model[0])),
            ]
            + [pl.BlockSpec(memory_space=pl.ANY)] * len(after),
            out_specs=pl.BlockSpec((tokens, tile), lambda i, model: (0, i)),
        ),
        flops=0,
        moved=0,
        vmem=16,
    )(model_number, mine, theirs, *after)


def panel_kernel(mine_ref, theirs_ref, out_ref):
    out_ref[...] = zscore(mine_ref[...], theirs_ref[...]).T.astype(jnp.bfloat16)


def panel_kernel_or(model_ref, mine_ref, theirs_ref, given_ref, *refs):
    out_ref = refs[-1]

    @pl.when(model_ref[0] == 0)
    def _():
        panel_kernel(mine_ref, theirs_ref, out_ref)

    @pl.when(model_ref[0] == 1)
    def _():
        out_ref[...] = given_ref[...]


def panel_scores(mine, theirs, first, given=(), after=()):
    _, tokens, count = theirs.shape
    rows = pl.BlockSpec((count, tokens), lambda i: (0, 0))
    units = [
        pl.BlockSpec((2, tokens, count), lambda i: (0, 0, first)),
        pl.BlockSpec((2, tokens, count), lambda i: (0, 0, 0)),
    ]
    return call(
        panel_kernel_or if given else panel_kernel,
        out_shape=jax.ShapeDtypeStruct((count, tokens), jnp.bfloat16),
        grid=(1,),
        in_specs=(
            [pl.BlockSpec(memory_space=pltpu.SMEM), *units, rows]
            + [pl.BlockSpec(memory_space=pl.ANY)] * len(after)
            if given
            else units
        ),
        out_specs=rows,
        flops=0,
        moved=0,
        vmem=16,
    )(*given[:1], mine, theirs, *given[1:], *after)


def score_kernel(scale, tile, cores, widths, n_after, where_ref, *refs):
    panels, refs = refs[: len(cores)], refs[len(cores) :]
    pieces = []
    for side in widths:
        pieces.append(refs[: 2 * len(side)])
        refs = refs[2 * len(side) :]
    out_ref, panel_ref, refs = refs[n_after], refs[n_after + 1], refs[n_after + 2 :]
    units_refs, block_refs = refs[: len(widths)], refs[len(widths) : 2 * len(widths)]
    in_sems, out_sems = refs[2 * len(widths) :]
    model, chip, core = (where_ref[i] for i in range(3))
    rows = panel_ref.shape[1] // CHIPS

    def fetch(holder):
        pairs = [(ref, panel_ref.at[i]) for i, ref in enumerate(panels)]
        for side, into in zip(pieces, units_refs):
            start = 0
            for ref in side[holder::2]:
                pairs.append((ref, into.at[:, start : start + ref.shape[1]]))
                start += ref.shape[1]
        copies = [
            pltpu.make_async_copy(source, into, in_sems.at[i])
            for i, (source, into) in enumerate(pairs)
        ]
        for copy in copies:
            copy.start()
        for copy in copies:
            copy.wait()

    for holder in range(2):

        @pl.when(model == holder)
        def _():
            fetch(holder)

    copies = []
    for which, other in enumerate(cores):
        for pair in range(CHIPS // 2):
            panel = panel_ref[which, 2 * pair * rows : (2 * pair + 2) * rows, :]
            slot = which * (CHIPS // 2) + pair
            for side, (units_ref, block_ref) in enumerate(zip(units_refs, block_refs)):
                columns = units_ref.shape[1]
                for start in range(0, columns, tile):
                    total = jnp.dot(
                        panel,
                        units_ref[:, start : start + tile],
                        preferred_element_type=jnp.float32,
                    )
                    block_ref[slot, :, :, start : start + tile] = (
                        (total * scale).astype(jnp.bfloat16).reshape(2, rows, tile)
                    )
                for i in range(2):
                    line = lax.bitwise_xor(chip, SWAPS[2 * pair + i])
                    place = line * 2 + (1 - core if other else core)
                    copies.append(
                        pltpu.make_async_copy(
                            block_ref.at[slot, i],
                            out_ref.at[
                                pl.ds(pl.multiple_of(place * rows, rows), rows),
                                pl.ds(pl.multiple_of(where_ref[3 + side], 128), columns),
                            ],
                            out_sems.at[slot, side, i],
                        )
                    )
                    copies[-1].start()
    for copy in copies:
        copy.wait()


def scores(where, panels, cores, sides, tile, shape, before):
    rows, tokens = panels[0].shape
    widths = [[piece[0].shape[1] for piece in side] for side in sides]
    slots = len(panels) * CHIPS // 2
    anywhere = pl.BlockSpec(memory_space=pl.ANY)
    flat = [array for side in sides for piece in side for array in piece]
    columns = [sum(side) for side in widths]
    return call(
        functools.partial(
            score_kernel, 1.0 / math.sqrt(tokens), tile, cores, widths, len(before)
        ),
        out_shape=jax.ShapeDtypeStruct(shape, jnp.bfloat16),
        in_specs=[pl.BlockSpec(memory_space=pltpu.SMEM)]
        + [anywhere] * (len(panels) + len(flat) + len(before)),
        out_specs=anywhere,
        scratch_shapes=[pltpu.VMEM((len(panels), rows, tokens), jnp.bfloat16)]
        + [pltpu.VMEM((tokens, count), jnp.bfloat16) for count in columns]
        + [pltpu.VMEM((slots, 2, rows // CHIPS, count), jnp.bfloat16) for count in columns]
        + [
            pltpu.SemaphoreType.DMA((len(panels) + sum(map(len, widths)),)),
            pltpu.SemaphoreType.DMA((slots, len(sides), 2)),
        ],
        input_output_aliases={1 + len(panels) + len(flat): 0} if before else {},
        flops=2 * len(panels) * rows * tokens * sum(columns),
        moved=2 * len(panels) * rows * sum(columns),
        vmem=24,
    )(where, *panels, *flat, *before)


def paired_body(acts, gate_w, up_w, panel_units):
    model = lax.axis_index("mp")
    block = lax.axis_index("dp")
    side = lax.axis_index("tensor")
    sizes = tuple(lax.axis_size(name) for name in AXES)
    chip, core = block // 2, block % 2
    gate, up = gate_w[0], up_w[0]
    units = gate.shape[1]
    picks = panel_units.reshape(2, 2, sizes[1], -1)
    tile = picks.shape[3]
    half = units // 2 // tile
    chunks = [half - half // 2, half // 2]

    def b_sides(m, d, t):
        return (m, d, 1 - t) if m == 1 else None

    def both_sides(m, d, t):
        return m, d, 1 - t

    def a_sides(m, d, t):
        return (m, d, 1 - t) if m == 0 else None

    def b_to_a(m, d, t):
        return (0, d, t) if m == 1 else None

    def b_to_far_a(m, d, t):
        return (0, d, 1 - t) if m == 1 else None

    def a_to_b(m, d, t):
        return (1, d, t) if m == 0 else None

    same = join(shifts(acts[0], sizes), [])
    other = send(same, sizes, other_core)

    picks = lax.dynamic_index_in_dim(picks, block, axis=2, keepdims=False) - block * units
    picks_far = lax.dynamic_index_in_dim(picks, 1 - side, axis=1, keepdims=False)
    picks_b, picks_a = picks_far[1:], picks_far[:1]
    picks_own = lax.dynamic_index_in_dim(picks, side, axis=1, keepdims=False).reshape(1, -1)
    bases = [((1 - side) * half + first) * tile for first in (0, chunks[0])]
    bases += [side * half * tile, model]
    bases = jnp.stack(bases).astype(jnp.int32)
    model_number = jnp.reshape(model, (1,)).astype(jnp.int32)
    near, far = side * half * tile, (1 - side) * half * tile
    targets = [[model, chip, core, near, far], [model, chip, core, far + chunks[0] * tile]]
    targets = [jnp.stack(target).astype(jnp.int32) for target in targets]

    to_side, own_side = (1 - side) * half, side * half
    places = [[chip, core, to_side], [chip, core, to_side + chunks[0], own_side]]
    places = [jnp.stack(place).astype(jnp.int32) for place in places]
    ready = [picks_b, picks_a, picks_own, bases, model_number, *places, *targets]
    sent = products(places[0], same, other, gate, up, tile, chunks[:1], ready)
    sent += products(places[1], same, other, gate, up, tile, [chunks[1], half], sent)
    kept = sent[-1]
    came = [send(part, sizes, b_sides) for part in sent[:2]]

    z = unit_scores(model_number, kept, came[0], tile, 0, [])
    a_mine = send(z, sizes, b_to_a)
    nears, fars = [(a_mine, z)], [(send(a_mine, sizes, a_sides), send(z, sizes, b_sides))]

    picked_b = pick(bases, picks_b, sent, tile, [z])
    picked_a = pick(bases, picks_a, sent, tile, [picked_b])
    picked_own = pick(bases, picks_own, sent, tile, [picked_a])
    rows_b = panel_scores(picked_own, send(picked_b, sizes, a_sides), 1)
    rows_b = send(rows_b, sizes, a_to_b)
    rows = panel_scores(
        picked_own, send(picked_a, sizes, a_sides), 0, (model_number, rows_b), (a_mine,)
    )

    z = unit_scores(model_number, kept, came[1], tile, chunks[0], [rows])
    nears.append((send(z, sizes, b_to_a), z))
    fars.append((send(z, sizes, b_to_far_a), send(z, sizes, b_sides)))

    panel = join([rows, swapped(rows, sizes, 2)], [z])
    panel = join([panel, swapped(panel, sizes, 1)], [*fars[0], nears[1][0], fars[1][1]])
    panel_other = send(panel, sizes, other_core)
    shape = (2 * CHIPS * rows.shape[0], units)
    sides = [nears, fars[:1]]
    result = scores(targets[0], [panel], (0,), sides, tile, shape, [])
    result = scores(targets[0], [panel_other], (1,), sides, tile, shape, [result])
    return scores(
        targets[1], [panel, panel_other], (0, 1), [fars[1:]], tile, shape, [result]
    )


def solution(mesh):
    in_specs = (P("mp", "dp", "tensor"), P("mp", "tensor", "dp"), P("mp", "tensor", "dp"), P())
    out_specs = P(("mp", "tensor"), "dp")
    paired = mesh.shape["mp"] == 2 and mesh.shape["tensor"] == 2 and mesh.shape["dp"] == 2 * CHIPS

    def body(acts, gate_w, up_w, panel_units):
        picked = panel_units.shape[0] // (4 * 2 * CHIPS)
        units = gate_w.shape[2]
        fits = picked % 128 == 0 and units % (2 * picked) == 0 and units % 512 == 0
        fits = fits and units >= 10 * picked
        if paired and fits and acts.shape[1] % 16 == 0:
            return paired_body(acts, gate_w, up_w, panel_units)
        return general_body(acts, gate_w, up_w, panel_units)

    return jax.shard_map(body, mesh=mesh, in_specs=in_specs, out_specs=out_specs, check_vma=False)
```

```python
import functools
import math

import jax
import jax.numpy as jnp
from jax import lax
from jax.experimental import pallas as pl
from jax.experimental.pallas import tpu as pltpu
from jax.sharding import PartitionSpec as P

epsilon = 1e-05
AXES = ("mp", "dp", "tensor")
MIB = 1 << 20


def from_partner(block, axis, distance):
    count = lax.axis_size(axis)
    route = []
    for low in range(count):
        high = low | 1 << distance
        if high != low and high < count:
            route += [(low, high), (high, low)]
    return lax.ppermute(block, axis, route)


def cross_models(full_units, panel_own, panel_next, model_index):
    other_units, other_panel = from_partner((full_units, panel_next), "mp", 0)
    is_first = model_index == 0
    return (
        jnp.where(is_first, panel_own, other_panel),
        jnp.where(is_first, other_units, full_units),
    )


def general_body(acts, gate_w, up_w, panel_units):
    model_index = lax.axis_index("mp")
    unit_block = lax.axis_index("dp")
    n_model = lax.axis_size("mp")
    n_data = lax.axis_size("dp")
    n_width = lax.axis_size("tensor")
    weight_gate = gate_w[0]
    weight_up = up_w[0]
    units = weight_gate.shape[1]
    gathered = lax.all_gather(acts[0], "dp", axis=0, tiled=True)
    tokens = gathered.shape[0]
    token_share = tokens // n_width
    score_scale = 1.0 / math.sqrt(tokens)
    panel_picks = panel_units.reshape(n_model, n_width, n_data, -1)
    panel_picks = (
        lax.dynamic_index_in_dim(panel_picks, unit_block, axis=2, keepdims=False)
        - unit_block * units
    )
    gate_part = jnp.dot(gathered, weight_gate, preferred_element_type=jnp.float32)
    up_part = jnp.dot(gathered, weight_up, preferred_element_type=jnp.float32)
    summed = lax.psum_scatter(
        jnp.concatenate([gate_part, up_part], axis=1).astype(jnp.bfloat16),
        "tensor",
        scatter_dimension=0,
        tiled=True,
    ).astype(jnp.float32)
    hidden = (jax.nn.silu(summed[:, :units]) * summed[:, units:]).astype(jnp.bfloat16)
    wide_hidden = hidden.astype(jnp.float32)
    totals = lax.psum(
        (jnp.sum(wide_hidden, axis=0), jnp.sum(wide_hidden * wide_hidden, axis=0)), "tensor"
    )
    unit_mean = totals[0] / tokens
    unit_var = totals[1] / tokens - unit_mean * unit_mean
    scored = ((wide_hidden - unit_mean) * lax.rsqrt(unit_var + epsilon)).astype(jnp.bfloat16)
    full_units = lax.all_gather(scored, "tensor", axis=0, tiled=True)
    order_list = panel_picks.transpose(1, 0, 2).reshape(-1)
    chosen = jnp.take(scored, order_list, axis=1).reshape(token_share, n_width, -1)
    moved_rows = lax.all_to_all(chosen, "tensor", split_axis=1, concat_axis=0, tiled=True)
    moved_rows = moved_rows.reshape(tokens, n_model, -1)
    panel_cols = lax.all_gather(moved_rows, "dp", axis=2, tiled=True)
    mine_a, mine_b = cross_models(full_units, panel_cols[:, 0], panel_cols[:, 1], model_index)
    result = lax.dot_general(
        mine_a, mine_b, (((0,), (0,)), ((), ())), preferred_element_type=jnp.float32
    )
    return (result * score_scale).astype(jnp.bfloat16)


CHIPS = 4


def routes(sizes, move):
    n_model, n_data, n_width = sizes
    pairs = []
    for m in range(n_model):
        for d in range(n_data):
            for t in range(n_width):
                to = move(m, d, t)
                if to is not None:
                    source = (m * n_data + d) * n_width + t
                    pairs.append((source, (to[0] * n_data + to[1]) * n_width + to[2]))
    return pairs


def send(block, sizes, move):
    return lax.ppermute(block, AXES, routes(sizes, move))


def other_core(m, d, t):
    return m, d ^ 1, t


def shifted(step):
    def move(m, d, t):
        return m, (d + 2 * step) % (2 * CHIPS), t

    return move


def shifts(block, sizes):
    came = [send(block, sizes, shifted(step)) for step in (1, CHIPS - 1, 2)]
    return [block, came[0], came[2], came[1]]


def join_kernel(count, *refs):
    out_ref, sems = refs[-2:]
    rows = refs[0].shape[0]
    copies = [
        pltpu.make_async_copy(refs[i], out_ref.at[i * rows : (i + 1) * rows, :], sems.at[i])
        for i in range(count)
    ]
    for copy in copies:
        copy.start()
    for copy in copies:
        copy.wait()


def join(blocks, after):
    rows, width = blocks[0].shape
    count = len(blocks)
    return call(
        functools.partial(join_kernel, count),
        out_shape=jax.ShapeDtypeStruct((count * rows, width), blocks[0].dtype),
        in_specs=[pl.BlockSpec(memory_space=pl.ANY)] * (count + len(after)),
        out_specs=pl.BlockSpec(memory_space=pltpu.VMEM),
        scratch_shapes=[pltpu.SemaphoreType.DMA((count,))],
        flops=0,
        moved=0,
        vmem=16,
    )(*blocks, *after)


def swapped(block, sizes, distance):
    return send(block, sizes, lambda m, d, t: (m, d ^ (2 * distance), t))


SWAPS = (0, 2, 1, 3)


def canonical(index, chip, core):
    line = lax.rem(chip + CHIPS - index % CHIPS, CHIPS)
    return line * 2 + (core if index < CHIPS else 1 - core)


def call(kernel, *, flops, moved, vmem, **rest):
    return pl.pallas_call(
        kernel,
        compiler_params=pltpu.CompilerParams(vmem_limit_bytes=vmem * MIB),
        cost_estimate=pl.CostEstimate(flops=flops, bytes_accessed=moved, transcendentals=0),
        **rest,
    )


def products_kernel(counts, n_after, place_ref, gate_ref, up_ref, *refs):
    x_refs, refs = refs[: 2 * CHIPS], refs[2 * CHIPS :]
    rows = x_refs[0].shape[0]
    step = pl.program_id(0)

    def write(out_ref):
        x = jnp.concatenate([x_ref[...] for x_ref in x_refs], axis=0)
        for which, weight_ref in enumerate((gate_ref, up_ref)):
            total = jnp.dot(x, weight_ref[...], preferred_element_type=jnp.float32)
            total = total.astype(jnp.bfloat16)
            for i in range(2 * CHIPS):
                start = pl.multiple_of(canonical(i, place_ref[0], place_ref[1]) * rows, rows)
                out_ref[which, pl.ds(start, rows), :] = total[i * rows : (i + 1) * rows]

    first = 0
    for count, out_ref in zip(counts, refs[n_after:]):

        @pl.when((step >= first) & (step < first + count))
        def _():
            write(out_ref)

        first += count


def products(place, blocks, gate, up, tile, counts, after):
    rows, width = blocks[0].shape
    tokens = len(blocks) * rows
    firsts = [sum(counts[:i]) for i in range(len(counts))]

    def weight_tile(i, place_ref):
        column = place_ref[2] + i
        for run in range(1, len(counts)):
            column = jnp.where(i >= firsts[run], place_ref[2 + run] + i - firsts[run], column)
        return 0, column

    def out_tile(run):
        return lambda i, place_ref: (0, 0, jnp.clip(i - firsts[run], 0, counts[run] - 1))

    weights = pl.BlockSpec((width, tile), weight_tile)
    whole = pl.BlockSpec((rows, width), lambda i, place_ref: (0, 0))
    return call(
        functools.partial(products_kernel, counts, len(after)),
        out_shape=[
            jax.ShapeDtypeStruct((2, tokens, tile * count), jnp.bfloat16) for count in counts
        ],
        grid_spec=pltpu.PrefetchScalarGridSpec(
            num_scalar_prefetch=1,
            grid=(sum(counts),),
            in_specs=[weights, weights]
            + [whole] * len(blocks)
            + [pl.BlockSpec(memory_space=pl.ANY)] * len(after),
            out_specs=[
                pl.BlockSpec((2, tokens, tile), out_tile(run)) for run in range(len(counts))
            ],
        ),
        flops=4 * tokens * width * tile * sum(counts),
        moved=4 * width * tile * sum(counts),
        vmem=38,
    )(place, gate, up, *blocks, *after)


def pick_kernel(counts, tile, bases_ref, picks_ref, *refs):
    out_ref = refs[-1]
    tokens, picked = out_ref.shape[1:]

    @pl.when(bases_ref[len(counts)] == 0)
    def _():
        total = jnp.zeros((2 * tokens, picked), jnp.float32)
        for part, (ref, count) in enumerate(zip(refs[: len(counts)], counts)):
            for i in range(count):
                base = bases_ref[part] + i * tile
                unit = lax.broadcasted_iota(jnp.int32, (tile, picked), 0) + base
                chosen = jnp.where(unit == picks_ref[...], 1.0, 0.0).astype(jnp.bfloat16)
                block = ref[:, :, i * tile : (i + 1) * tile].reshape(2 * tokens, tile)
                total += jnp.dot(block, chosen, preferred_element_type=jnp.float32)
        out_ref[...] = total.astype(jnp.bfloat16).reshape(2, tokens, picked)

    @pl.when(bases_ref[len(counts)] == 1)
    def _():
        out_ref[...] = jnp.zeros_like(out_ref)


def pick(bases, picks, parts, tile, after):
    tokens = parts[0].shape[1]
    picked = picks.shape[1]
    counts = [part.shape[2] // tile for part in parts]
    vmem = pl.BlockSpec(memory_space=pltpu.VMEM)
    return call(
        functools.partial(pick_kernel, counts, tile),
        out_shape=jax.ShapeDtypeStruct((2, tokens, picked), jnp.bfloat16),
        in_specs=[pl.BlockSpec(memory_space=pltpu.SMEM), vmem]
        + [vmem] * len(parts)
        + [pl.BlockSpec(memory_space=pl.ANY)] * len(after),
        out_specs=vmem,
        flops=0,
        moved=0,
        vmem=16,
    )(bases, picks, *parts, *after)


def zscore(mine, theirs):
    tokens = mine.shape[1]
    gate = mine[0].astype(jnp.float32) + theirs[0].astype(jnp.float32)
    up = mine[1].astype(jnp.float32) + theirs[1].astype(jnp.float32)
    hidden = (gate / (1.0 + jnp.exp(-gate)) * up).astype(jnp.bfloat16).astype(jnp.float32)
    mean = jnp.sum(hidden, axis=0, keepdims=True) / tokens
    var = jnp.sum(hidden * hidden, axis=0, keepdims=True) / tokens - mean * mean
    return (hidden - mean) * lax.rsqrt(var + epsilon)


def unit_kernel(model_ref, mine_ref, theirs_ref, *refs):
    @pl.when(model_ref[0] == 1)
    def _():
        refs[-1][...] = zscore(mine_ref[...], theirs_ref[...]).astype(jnp.bfloat16)

    @pl.when(model_ref[0] == 0)
    def _():
        refs[-1][...] = jnp.zeros_like(refs[-1])


def unit_scores(model_number, mine, theirs, tile, first, after):
    _, tokens, units = theirs.shape
    return call(
        unit_kernel,
        out_shape=jax.ShapeDtypeStruct((tokens, units), jnp.bfloat16),
        grid_spec=pltpu.PrefetchScalarGridSpec(
            num_scalar_prefetch=1,
            grid=(units // tile,),
            in_specs=[
                pl.BlockSpec((2, tokens, tile), lambda i, model: (0, 0, (first + i) * model[0])),
                pl.BlockSpec((2, tokens, tile), lambda i, model: (0, 0, i * model[0])),
            ]
            + [pl.BlockSpec(memory_space=pl.ANY)] * len(after),
            out_specs=pl.BlockSpec((tokens, tile), lambda i, model: (0, i)),
        ),
        flops=0,
        moved=0,
        vmem=16,
    )(model_number, mine, theirs, *after)


def panel_kernel(mine_ref, theirs_ref, out_ref):
    out_ref[...] = zscore(mine_ref[...], theirs_ref[...]).T.astype(jnp.bfloat16)


def panel_kernel_or(model_ref, mine_ref, theirs_ref, given_ref, *refs):
    out_ref = refs[-1]

    @pl.when(model_ref[0] == 0)
    def _():
        panel_kernel(mine_ref, theirs_ref, out_ref)

    @pl.when(model_ref[0] == 1)
    def _():
        out_ref[...] = given_ref[...]


def panel_scores(mine, theirs, first, given=(), after=()):
    _, tokens, count = theirs.shape
    rows = pl.BlockSpec((count, tokens), lambda i: (0, 0))
    units = [
        pl.BlockSpec((2, tokens, count), lambda i: (0, 0, first)),
        pl.BlockSpec((2, tokens, count), lambda i: (0, 0, 0)),
    ]
    return call(
        panel_kernel_or if given else panel_kernel,
        out_shape=jax.ShapeDtypeStruct((count, tokens), jnp.bfloat16),
        grid=(1,),
        in_specs=(
            [pl.BlockSpec(memory_space=pltpu.SMEM), *units, rows]
            + [pl.BlockSpec(memory_space=pl.ANY)] * len(after)
            if given
            else units
        ),
        out_specs=rows,
        flops=0,
        moved=0,
        vmem=16,
    )(*given[:1], mine, theirs, *given[1:], *after)


def score_kernel(scale, tile, cores, widths, n_after, where_ref, *refs):
    panels, refs = refs[: len(cores)], refs[len(cores) :]
    pieces = []
    for side in widths:
        pieces.append(refs[: 2 * len(side)])
        refs = refs[2 * len(side) :]
    out_ref, panel_ref, refs = refs[n_after], refs[n_after + 1], refs[n_after + 2 :]
    units_refs, block_refs = refs[: len(widths)], refs[len(widths) : 2 * len(widths)]
    in_sems, out_sems = refs[2 * len(widths) :]
    model, chip, core = (where_ref[i] for i in range(3))
    rows = panel_ref.shape[1] // CHIPS

    def fetch(holder):
        pairs = [(ref, panel_ref.at[i]) for i, ref in enumerate(panels)]
        for side, into in zip(pieces, units_refs):
            start = 0
            for ref in side[holder::2]:
                pairs.append((ref, into.at[:, start : start + ref.shape[1]]))
                start += ref.shape[1]
        copies = [
            pltpu.make_async_copy(source, into, in_sems.at[i])
            for i, (source, into) in enumerate(pairs)
        ]
        for copy in copies:
            copy.start()
        for copy in copies:
            copy.wait()

    for holder in range(2):

        @pl.when(model == holder)
        def _():
            fetch(holder)

    copies = []
    for which, other in enumerate(cores):
        for pair in range(CHIPS // 2):
            panel = panel_ref[which, 2 * pair * rows : (2 * pair + 2) * rows, :]
            slot = which * (CHIPS // 2) + pair
            for side, (units_ref, block_ref) in enumerate(zip(units_refs, block_refs)):
                columns = units_ref.shape[1]
                for start in range(0, columns, tile):
                    total = jnp.dot(
                        panel,
                        units_ref[:, start : start + tile],
                        preferred_element_type=jnp.float32,
                    )
                    block_ref[slot, :, :, start : start + tile] = (
                        (total * scale).astype(jnp.bfloat16).reshape(2, rows, tile)
                    )
                for i in range(2):
                    line = lax.bitwise_xor(chip, SWAPS[2 * pair + i])
                    place = line * 2 + (1 - core if other else core)
                    copies.append(
                        pltpu.make_async_copy(
                            block_ref.at[slot, i],
                            out_ref.at[
                                pl.ds(pl.multiple_of(place * rows, rows), rows),
                                pl.ds(pl.multiple_of(where_ref[3 + side], 128), columns),
                            ],
                            out_sems.at[slot, side, i],
                        )
                    )
                    copies[-1].start()
    for copy in copies:
        copy.wait()


def scores(where, panels, cores, sides, tile, shape, before):
    rows, tokens = panels[0].shape
    widths = [[piece[0].shape[1] for piece in side] for side in sides]
    slots = len(panels) * CHIPS // 2
    anywhere = pl.BlockSpec(memory_space=pl.ANY)
    flat = [array for side in sides for piece in side for array in piece]
    columns = [sum(side) for side in widths]
    return call(
        functools.partial(
            score_kernel, 1.0 / math.sqrt(tokens), tile, cores, widths, len(before)
        ),
        out_shape=jax.ShapeDtypeStruct(shape, jnp.bfloat16),
        in_specs=[pl.BlockSpec(memory_space=pltpu.SMEM)]
        + [anywhere] * (len(panels) + len(flat) + len(before)),
        out_specs=anywhere,
        scratch_shapes=[pltpu.VMEM((len(panels), rows, tokens), jnp.bfloat16)]
        + [pltpu.VMEM((tokens, count), jnp.bfloat16) for count in columns]
        + [pltpu.VMEM((slots, 2, rows // CHIPS, count), jnp.bfloat16) for count in columns]
        + [
            pltpu.SemaphoreType.DMA((len(panels) + sum(map(len, widths)),)),
            pltpu.SemaphoreType.DMA((slots, len(sides), 2)),
        ],
        input_output_aliases={1 + len(panels) + len(flat): 0} if before else {},
        flops=2 * len(panels) * rows * tokens * sum(columns),
        moved=2 * len(panels) * rows * sum(columns),
        vmem=24,
    )(where, *panels, *flat, *before)


def paired_body(acts, gate_w, up_w, panel_units):
    model = lax.axis_index("mp")
    block = lax.axis_index("dp")
    side = lax.axis_index("tensor")
    sizes = tuple(lax.axis_size(name) for name in AXES)
    chip, core = block // 2, block % 2
    gate, up = gate_w[0], up_w[0]
    units = gate.shape[1]
    picks = panel_units.reshape(2, 2, sizes[1], -1)
    tile = picks.shape[3]
    half = units // 2 // tile
    chunks = [half - half // 2, half // 2]

    def b_sides(m, d, t):
        return (m, d, 1 - t) if m == 1 else None

    def both_sides(m, d, t):
        return m, d, 1 - t

    def a_sides(m, d, t):
        return (m, d, 1 - t) if m == 0 else None

    def b_to_a(m, d, t):
        return (0, d, t) if m == 1 else None

    def a_to_b(m, d, t):
        return (1, d, t) if m == 0 else None

    own = join([acts[0]], [])
    blocks = [own, *shifts(acts[0], sizes)[1:]]
    blocks += [send(part, sizes, other_core) for part in blocks]

    picks = lax.dynamic_index_in_dim(picks, block, axis=2, keepdims=False) - block * units
    picks_far = lax.dynamic_index_in_dim(picks, 1 - side, axis=1, keepdims=False)
    picks_b, picks_a = picks_far[1:], picks_far[:1]
    picks_own = lax.dynamic_index_in_dim(picks, side, axis=1, keepdims=False).reshape(1, -1)
    bases = [((1 - side) * half + first) * tile for first in (0, chunks[0])]
    bases += [side * half * tile, model]
    bases = jnp.stack(bases).astype(jnp.int32)
    model_number = jnp.reshape(model, (1,)).astype(jnp.int32)
    near, far = side * half * tile, (1 - side) * half * tile
    targets = [[model, chip, core, near, far], [model, chip, core, far + chunks[0] * tile]]
    targets = [jnp.stack(target).astype(jnp.int32) for target in targets]

    to_side, own_side = (1 - side) * half, side * half
    places = [[chip, core, to_side], [chip, core, to_side + chunks[0], own_side]]
    places = [jnp.stack(place).astype(jnp.int32) for place in places]
    ready = [picks_b, picks_a, picks_own, bases, model_number, *places, *targets]
    sent = products(places[0], blocks, gate, up, tile, chunks[:1], ready)
    sent += products(places[1], blocks, gate, up, tile, [chunks[1], half], sent)
    kept = sent[-1]
    came = [send(part, sizes, b_sides) for part in sent[:2]]

    z = unit_scores(model_number, kept, came[0], tile, 0, [])
    a_mine = send(z, sizes, b_to_a)
    nears, fars = [(a_mine, z)], [(send(a_mine, sizes, a_sides), send(z, sizes, b_sides))]

    picked_b = pick(bases, picks_b, sent, tile, [z])
    picked_a = pick(bases, picks_a, sent, tile, [picked_b])
    picked_own = pick(bases, picks_own, sent, tile, [picked_a])
    rows_b = panel_scores(picked_own, send(picked_b, sizes, a_sides), 1)
    rows_b = send(rows_b, sizes, a_to_b)
    rows = panel_scores(
        picked_own, send(picked_a, sizes, a_sides), 0, (model_number, rows_b)
    )

    z = unit_scores(model_number, kept, came[1], tile, chunks[0], [rows])
    nears.append((send(z, sizes, b_to_a), z))
    fars.append((send(nears[1][0], sizes, a_sides), send(z, sizes, b_sides)))

    panel = join([rows, swapped(rows, sizes, 2)], [z])
    panel = join([panel, swapped(panel, sizes, 1)], [*fars[0], nears[1][0], fars[1][1]])
    panel_other = send(panel, sizes, other_core)
    shape = (2 * CHIPS * rows.shape[0], units)
    sides = [nears, fars[:1]]
    result = scores(targets[0], [panel], (0,), sides, tile, shape, [])
    result = scores(targets[0], [panel_other], (1,), sides, tile, shape, [result])
    return scores(
        targets[1], [panel, panel_other], (0, 1), [fars[1:]], tile, shape, [result]
    )


def solution(mesh):
    in_specs = (P("mp", "dp", "tensor"), P("mp", "tensor", "dp"), P("mp", "tensor", "dp"), P())
    out_specs = P(("mp", "tensor"), "dp")
    paired = mesh.shape["mp"] == 2 and mesh.shape["tensor"] == 2 and mesh.shape["dp"] == 2 * CHIPS

    def body(acts, gate_w, up_w, panel_units):
        picked = panel_units.shape[0] // (4 * 2 * CHIPS)
        units = gate_w.shape[2]
        fits = picked % 128 == 0 and units % (2 * picked) == 0 and units % 512 == 0
        fits = fits and units >= 10 * picked
        if paired and fits and acts.shape[1] % 16 == 0:
            return paired_body(acts, gate_w, up_w, panel_units)
        return general_body(acts, gate_w, up_w, panel_units)

    return jax.shard_map(body, mesh=mesh, in_specs=in_specs, out_specs=out_specs, check_vma=False)
```

```python
import functools
import math

import jax
import jax.numpy as jnp
from jax import lax
from jax.experimental import pallas as pl
from jax.experimental.pallas import tpu as pltpu
from jax.sharding import PartitionSpec as P

epsilon = 1e-05
AXES = ("mp", "dp", "tensor")
MIB = 1 << 20


def from_partner(block, axis, distance):
    count = lax.axis_size(axis)
    route = []
    for low in range(count):
        high = low | 1 << distance
        if high != low and high < count:
            route += [(low, high), (high, low)]
    return lax.ppermute(block, axis, route)


def cross_models(full_units, panel_own, panel_next, model_index):
    other_units, other_panel = from_partner((full_units, panel_next), "mp", 0)
    is_first = model_index == 0
    return (
        jnp.where(is_first, panel_own, other_panel),
        jnp.where(is_first, other_units, full_units),
    )


def general_body(acts, gate_w, up_w, panel_units):
    model_index = lax.axis_index("mp")
    unit_block = lax.axis_index("dp")
    n_model = lax.axis_size("mp")
    n_data = lax.axis_size("dp")
    n_width = lax.axis_size("tensor")
    weight_gate = gate_w[0]
    weight_up = up_w[0]
    units = weight_gate.shape[1]
    gathered = lax.all_gather(acts[0], "dp", axis=0, tiled=True)
    tokens = gathered.shape[0]
    token_share = tokens // n_width
    score_scale = 1.0 / math.sqrt(tokens)
    panel_picks = panel_units.reshape(n_model, n_width, n_data, -1)
    panel_picks = (
        lax.dynamic_index_in_dim(panel_picks, unit_block, axis=2, keepdims=False)
        - unit_block * units
    )
    gate_part = jnp.dot(gathered, weight_gate, preferred_element_type=jnp.float32)
    up_part = jnp.dot(gathered, weight_up, preferred_element_type=jnp.float32)
    summed = lax.psum_scatter(
        jnp.concatenate([gate_part, up_part], axis=1).astype(jnp.bfloat16),
        "tensor",
        scatter_dimension=0,
        tiled=True,
    ).astype(jnp.float32)
    hidden = (jax.nn.silu(summed[:, :units]) * summed[:, units:]).astype(jnp.bfloat16)
    wide_hidden = hidden.astype(jnp.float32)
    totals = lax.psum(
        (jnp.sum(wide_hidden, axis=0), jnp.sum(wide_hidden * wide_hidden, axis=0)), "tensor"
    )
    unit_mean = totals[0] / tokens
    unit_var = totals[1] / tokens - unit_mean * unit_mean
    scored = ((wide_hidden - unit_mean) * lax.rsqrt(unit_var + epsilon)).astype(jnp.bfloat16)
    full_units = lax.all_gather(scored, "tensor", axis=0, tiled=True)
    order_list = panel_picks.transpose(1, 0, 2).reshape(-1)
    chosen = jnp.take(scored, order_list, axis=1).reshape(token_share, n_width, -1)
    moved_rows = lax.all_to_all(chosen, "tensor", split_axis=1, concat_axis=0, tiled=True)
    moved_rows = moved_rows.reshape(tokens, n_model, -1)
    panel_cols = lax.all_gather(moved_rows, "dp", axis=2, tiled=True)
    mine_a, mine_b = cross_models(full_units, panel_cols[:, 0], panel_cols[:, 1], model_index)
    result = lax.dot_general(
        mine_a, mine_b, (((0,), (0,)), ((), ())), preferred_element_type=jnp.float32
    )
    return (result * score_scale).astype(jnp.bfloat16)


CHIPS = 4


def routes(sizes, move):
    n_model, n_data, n_width = sizes
    pairs = []
    for m in range(n_model):
        for d in range(n_data):
            for t in range(n_width):
                to = move(m, d, t)
                if to is not None:
                    source = (m * n_data + d) * n_width + t
                    pairs.append((source, (to[0] * n_data + to[1]) * n_width + to[2]))
    return pairs


def send(block, sizes, move):
    return lax.ppermute(block, AXES, routes(sizes, move))


def other_core(m, d, t):
    return m, d ^ 1, t


def shifted(step):
    def move(m, d, t):
        return m, (d + 2 * step) % (2 * CHIPS), t

    return move


def shifts(block, sizes):
    came = [send(block, sizes, shifted(step)) for step in (1, CHIPS - 1, 2)]
    return [block, came[0], came[2], came[1]]


def join_kernel(count, *refs):
    out_ref, sems = refs[-2:]
    rows = refs[0].shape[0]
    copies = [
        pltpu.make_async_copy(refs[i], out_ref.at[i * rows : (i + 1) * rows, :], sems.at[i])
        for i in range(count)
    ]
    for copy in copies:
        copy.start()
    for copy in copies:
        copy.wait()


def join(blocks, after, flops=0):
    rows, width = blocks[0].shape
    count = len(blocks)
    return call(
        functools.partial(join_kernel, count),
        out_shape=jax.ShapeDtypeStruct((count * rows, width), blocks[0].dtype),
        in_specs=[pl.BlockSpec(memory_space=pl.ANY)] * (count + len(after)),
        out_specs=pl.BlockSpec(memory_space=pltpu.VMEM),
        scratch_shapes=[pltpu.SemaphoreType.DMA((count,))],
        flops=flops,
        moved=0,
        vmem=16,
    )(*blocks, *after)


def swapped(block, sizes, distance):
    return send(block, sizes, lambda m, d, t: (m, d ^ (2 * distance), t))


SWAPS = (0, 2, 1, 3)


def canonical(index, chip, core):
    line = lax.rem(chip + CHIPS - index % CHIPS, CHIPS)
    return line * 2 + (core if index < CHIPS else 1 - core)


def call(kernel, *, flops, moved, vmem, **rest):
    return pl.pallas_call(
        kernel,
        compiler_params=pltpu.CompilerParams(vmem_limit_bytes=vmem * MIB),
        cost_estimate=pl.CostEstimate(flops=flops, bytes_accessed=moved, transcendentals=0),
        **rest,
    )


def products_kernel(counts, n_after, place_ref, gate_ref, up_ref, *refs):
    x_refs, refs = refs[: 2 * CHIPS], refs[2 * CHIPS :]
    rows = x_refs[0].shape[0]
    step = pl.program_id(0)

    def write(out_ref):
        x = jnp.concatenate([x_ref[...] for x_ref in x_refs], axis=0)
        for which, weight_ref in enumerate((gate_ref, up_ref)):
            total = jnp.dot(x, weight_ref[...], preferred_element_type=jnp.float32)
            total = total.astype(jnp.bfloat16)
            for i in range(2 * CHIPS):
                start = pl.multiple_of(canonical(i, place_ref[0], place_ref[1]) * rows, rows)
                out_ref[which, pl.ds(start, rows), :] = total[i * rows : (i + 1) * rows]

    first = 0
    for count, out_ref in zip(counts, refs[n_after:]):

        @pl.when((step >= first) & (step < first + count))
        def _():
            write(out_ref)

        first += count


def products(place, blocks, gate, up, tile, counts, after):
    rows, width = blocks[0].shape
    tokens = len(blocks) * rows
    firsts = [sum(counts[:i]) for i in range(len(counts))]

    def weight_tile(i, place_ref):
        column = place_ref[2] + i
        for run in range(1, len(counts)):
            column = jnp.where(i >= firsts[run], place_ref[2 + run] + i - firsts[run], column)
        return 0, column

    def out_tile(run):
        return lambda i, place_ref: (0, 0, jnp.clip(i - firsts[run], 0, counts[run] - 1))

    weights = pl.BlockSpec((width, tile), weight_tile)
    whole = pl.BlockSpec((rows, width), lambda i, place_ref: (0, 0))
    return call(
        functools.partial(products_kernel, counts, len(after)),
        out_shape=[
            jax.ShapeDtypeStruct((2, tokens, tile * count), jnp.bfloat16) for count in counts
        ],
        grid_spec=pltpu.PrefetchScalarGridSpec(
            num_scalar_prefetch=1,
            grid=(sum(counts),),
            in_specs=[weights, weights]
            + [whole] * len(blocks)
            + [pl.BlockSpec(memory_space=pl.ANY)] * len(after),
            out_specs=[
                pl.BlockSpec((2, tokens, tile), out_tile(run)) for run in range(len(counts))
            ],
        ),
        flops=4 * tokens * width * tile * sum(counts),
        moved=4 * width * tile * sum(counts),
        vmem=38,
    )(place, gate, up, *blocks, *after)


def pick_kernel(counts, tile, bases_ref, picks_ref, *refs):
    out_ref = refs[-1]
    tokens, picked = out_ref.shape[1:]

    @pl.when(bases_ref[len(counts)] == 0)
    def _():
        total = jnp.zeros((2 * tokens, picked), jnp.float32)
        for part, (ref, count) in enumerate(zip(refs[: len(counts)], counts)):
            for i in range(count):
                base = bases_ref[part] + i * tile
                unit = lax.broadcasted_iota(jnp.int32, (tile, picked), 0) + base
                chosen = jnp.where(unit == picks_ref[...], 1.0, 0.0).astype(jnp.bfloat16)
                block = ref[:, :, i * tile : (i + 1) * tile].reshape(2 * tokens, tile)
                total += jnp.dot(block, chosen, preferred_element_type=jnp.float32)
        out_ref[...] = total.astype(jnp.bfloat16).reshape(2, tokens, picked)

    @pl.when(bases_ref[len(counts)] == 1)
    def _():
        out_ref[...] = jnp.zeros_like(out_ref)


def pick(bases, picks, parts, tile, after):
    tokens = parts[0].shape[1]
    picked = picks.shape[1]
    counts = [part.shape[2] // tile for part in parts]
    vmem = pl.BlockSpec(memory_space=pltpu.VMEM)
    return call(
        functools.partial(pick_kernel, counts, tile),
        out_shape=jax.ShapeDtypeStruct((2, tokens, picked), jnp.bfloat16),
        in_specs=[pl.BlockSpec(memory_space=pltpu.SMEM), vmem]
        + [vmem] * len(parts)
        + [pl.BlockSpec(memory_space=pl.ANY)] * len(after),
        out_specs=vmem,
        flops=0,
        moved=0,
        vmem=16,
    )(bases, picks, *parts, *after)


def zscore(mine, theirs):
    tokens = mine.shape[1]
    gate = mine[0].astype(jnp.float32) + theirs[0].astype(jnp.float32)
    up = mine[1].astype(jnp.float32) + theirs[1].astype(jnp.float32)
    hidden = (gate / (1.0 + jnp.exp(-gate)) * up).astype(jnp.bfloat16).astype(jnp.float32)
    mean = jnp.sum(hidden, axis=0, keepdims=True) / tokens
    var = jnp.sum(hidden * hidden, axis=0, keepdims=True) / tokens - mean * mean
    return (hidden - mean) * lax.rsqrt(var + epsilon)


def unit_kernel(model_ref, mine_ref, theirs_ref, *refs):
    @pl.when(model_ref[0] == 1)
    def _():
        refs[-1][...] = zscore(mine_ref[...], theirs_ref[...]).astype(jnp.bfloat16)

    @pl.when(model_ref[0] == 0)
    def _():
        refs[-1][...] = jnp.zeros_like(refs[-1])


def unit_scores(model_number, mine, theirs, tile, first, after):
    _, tokens, units = theirs.shape
    return call(
        unit_kernel,
        out_shape=jax.ShapeDtypeStruct((tokens, units), jnp.bfloat16),
        grid_spec=pltpu.PrefetchScalarGridSpec(
            num_scalar_prefetch=1,
            grid=(units // tile,),
            in_specs=[
                pl.BlockSpec((2, tokens, tile), lambda i, model: (0, 0, (first + i) * model[0])),
                pl.BlockSpec((2, tokens, tile), lambda i, model: (0, 0, i * model[0])),
            ]
            + [pl.BlockSpec(memory_space=pl.ANY)] * len(after),
            out_specs=pl.BlockSpec((tokens, tile), lambda i, model: (0, i)),
        ),
        flops=0,
        moved=0,
        vmem=16,
    )(model_number, mine, theirs, *after)


def panel_kernel(mine_ref, theirs_ref, out_ref):
    out_ref[...] = zscore(mine_ref[...], theirs_ref[...]).T.astype(jnp.bfloat16)


def panel_kernel_or(model_ref, mine_ref, theirs_ref, given_ref, *refs):
    out_ref = refs[-1]

    @pl.when(model_ref[0] == 0)
    def _():
        panel_kernel(mine_ref, theirs_ref, out_ref)

    @pl.when(model_ref[0] == 1)
    def _():
        out_ref[...] = given_ref[...]


def panel_scores(mine, theirs, first, given=(), after=()):
    _, tokens, count = theirs.shape
    rows = pl.BlockSpec((count, tokens), lambda i: (0, 0))
    units = [
        pl.BlockSpec((2, tokens, count), lambda i: (0, 0, first)),
        pl.BlockSpec((2, tokens, count), lambda i: (0, 0, 0)),
    ]
    return call(
        panel_kernel_or if given else panel_kernel,
        out_shape=jax.ShapeDtypeStruct((count, tokens), jnp.bfloat16),
        grid=(1,),
        in_specs=(
            [pl.BlockSpec(memory_space=pltpu.SMEM), *units, rows]
            + [pl.BlockSpec(memory_space=pl.ANY)] * len(after)
            if given
            else units
        ),
        out_specs=rows,
        flops=0,
        moved=0,
        vmem=16,
    )(*given[:1], mine, theirs, *given[1:], *after)


def score_kernel(scale, tile, cores, widths, n_after, where_ref, *refs):
    panels, refs = refs[: len(cores)], refs[len(cores) :]
    pieces = []
    for side in widths:
        pieces.append(refs[: 2 * len(side)])
        refs = refs[2 * len(side) :]
    out_ref, panel_ref, refs = refs[n_after], refs[n_after + 1], refs[n_after + 2 :]
    units_refs, block_refs = refs[: len(widths)], refs[len(widths) : 2 * len(widths)]
    in_sems, out_sems = refs[2 * len(widths) :]
    model, chip, core = (where_ref[i] for i in range(3))
    rows = panel_ref.shape[1] // CHIPS

    def fetch(holder):
        pairs = [(ref, panel_ref.at[i]) for i, ref in enumerate(panels)]
        for side, into in zip(pieces, units_refs):
            start = 0
            for ref in side[holder::2]:
                pairs.append((ref, into.at[:, start : start + ref.shape[1]]))
                start += ref.shape[1]
        copies = [
            pltpu.make_async_copy(source, into, in_sems.at[i])
            for i, (source, into) in enumerate(pairs)
        ]
        for copy in copies:
            copy.start()
        for copy in copies:
            copy.wait()

    for holder in range(2):

        @pl.when(model == holder)
        def _():
            fetch(holder)

    copies = []
    for which, other in enumerate(cores):
        for pair in range(CHIPS // 2):
            panel = panel_ref[which, 2 * pair * rows : (2 * pair + 2) * rows, :]
            slot = which * (CHIPS // 2) + pair
            for side, (units_ref, block_ref) in enumerate(zip(units_refs, block_refs)):
                columns = units_ref.shape[1]
                for start in range(0, columns, tile):
                    total = jnp.dot(
                        panel,
                        units_ref[:, start : start + tile],
                        preferred_element_type=jnp.float32,
                    )
                    block_ref[slot, :, :, start : start + tile] = (
                        (total * scale).astype(jnp.bfloat16).reshape(2, rows, tile)
                    )
                for i in range(2):
                    line = lax.bitwise_xor(chip, SWAPS[2 * pair + i])
                    place = line * 2 + (1 - core if other else core)
                    copies.append(
                        pltpu.make_async_copy(
                            block_ref.at[slot, i],
                            out_ref.at[
                                pl.ds(pl.multiple_of(place * rows, rows), rows),
                                pl.ds(pl.multiple_of(where_ref[3 + side], 128), columns),
                            ],
                            out_sems.at[slot, side, i],
                        )
                    )
                    copies[-1].start()
    for copy in copies:
        copy.wait()


def scores(where, panels, cores, sides, tile, shape, before):
    rows, tokens = panels[0].shape
    widths = [[piece[0].shape[1] for piece in side] for side in sides]
    slots = len(panels) * CHIPS // 2
    anywhere = pl.BlockSpec(memory_space=pl.ANY)
    flat = [array for side in sides for piece in side for array in piece]
    columns = [sum(side) for side in widths]
    return call(
        functools.partial(
            score_kernel, 1.0 / math.sqrt(tokens), tile, cores, widths, len(before)
        ),
        out_shape=jax.ShapeDtypeStruct(shape, jnp.bfloat16),
        in_specs=[pl.BlockSpec(memory_space=pltpu.SMEM)]
        + [anywhere] * (len(panels) + len(flat) + len(before)),
        out_specs=anywhere,
        scratch_shapes=[pltpu.VMEM((len(panels), rows, tokens), jnp.bfloat16)]
        + [pltpu.VMEM((tokens, count), jnp.bfloat16) for count in columns]
        + [pltpu.VMEM((slots, 2, rows // CHIPS, count), jnp.bfloat16) for count in columns]
        + [
            pltpu.SemaphoreType.DMA((len(panels) + sum(map(len, widths)),)),
            pltpu.SemaphoreType.DMA((slots, len(sides), 2)),
        ],
        input_output_aliases={1 + len(panels) + len(flat): 0} if before else {},
        flops=2 * len(panels) * rows * tokens * sum(columns),
        moved=2 * len(panels) * rows * sum(columns),
        vmem=24,
    )(where, *panels, *flat, *before)


def paired_body(acts, gate_w, up_w, panel_units):
    model = lax.axis_index("mp")
    block = lax.axis_index("dp")
    side = lax.axis_index("tensor")
    sizes = tuple(lax.axis_size(name) for name in AXES)
    chip, core = block // 2, block % 2
    gate, up = gate_w[0], up_w[0]
    units = gate.shape[1]
    picks = panel_units.reshape(2, 2, sizes[1], -1)
    tile = picks.shape[3]
    half = units // 2 // tile
    chunks = [half - half // 2, half // 2]

    def b_sides(m, d, t):
        return (m, d, 1 - t) if m == 1 else None

    def both_sides(m, d, t):
        return m, d, 1 - t

    def a_sides(m, d, t):
        return (m, d, 1 - t) if m == 0 else None

    def b_to_a(m, d, t):
        return (0, d, t) if m == 1 else None

    def a_to_b(m, d, t):
        return (1, d, t) if m == 0 else None

    own = join([acts[0]], [])
    blocks = [own, *shifts(acts[0], sizes)[1:]]
    blocks += [send(part, sizes, other_core) for part in blocks]

    picks = lax.dynamic_index_in_dim(picks, block, axis=2, keepdims=False) - block * units
    picks_far = lax.dynamic_index_in_dim(picks, 1 - side, axis=1, keepdims=False)
    picks_b, picks_a = picks_far[1:], picks_far[:1]
    picks_own = lax.dynamic_index_in_dim(picks, side, axis=1, keepdims=False).reshape(1, -1)
    bases = [((1 - side) * half + first) * tile for first in (0, chunks[0])]
    bases += [side * half * tile, model]
    bases = jnp.stack(bases).astype(jnp.int32)
    model_number = jnp.reshape(model, (1,)).astype(jnp.int32)
    near, far = side * half * tile, (1 - side) * half * tile
    targets = [[model, chip, core, near, far], [model, chip, core, far + chunks[0] * tile]]
    targets = [jnp.stack(target).astype(jnp.int32) for target in targets]

    to_side, own_side = (1 - side) * half, side * half
    places = [[chip, core, to_side], [chip, core, to_side + chunks[0], own_side]]
    places = [jnp.stack(place).astype(jnp.int32) for place in places]
    ready = [picks_b, picks_a, picks_own, bases, model_number, *places, *targets]
    sent = products(places[0], blocks, gate, up, tile, chunks[:1], ready)
    sent += products(places[1], blocks, gate, up, tile, [chunks[1], half], sent)
    kept = sent[-1]
    came = [send(part, sizes, b_sides) for part in sent[:2]]

    z = unit_scores(model_number, kept, came[0], tile, 0, [])
    a_mine = send(z, sizes, b_to_a)
    nears, fars = [(a_mine, z)], [(send(a_mine, sizes, a_sides), send(z, sizes, b_sides))]

    picked_b = pick(bases, picks_b, sent, tile, [z])
    picked_a = pick(bases, picks_a, sent, tile, [picked_b])
    picked_own = pick(bases, picks_own, sent, tile, [picked_a])
    rows_b = panel_scores(picked_own, send(picked_b, sizes, a_sides), 1)
    rows_b = send(rows_b, sizes, a_to_b)
    rows = panel_scores(
        picked_own, send(picked_a, sizes, a_sides), 0, (model_number, rows_b)
    )

    z = unit_scores(model_number, kept, came[1], tile, chunks[0], [rows])
    nears.append((send(z, sizes, b_to_a), z))
    fars.append((send(nears[1][0], sizes, a_sides), send(z, sizes, b_sides)))

    panel = join([rows, swapped(rows, sizes, 2)], [z], 1 << 33)
    panel = join([panel, swapped(panel, sizes, 1)], [*fars[0], nears[1][0], fars[1][1]])
    panel_other = send(panel, sizes, other_core)
    shape = (2 * CHIPS * rows.shape[0], units)
    sides = [nears, fars[:1]]
    result = scores(targets[0], [panel], (0,), sides, tile, shape, [])
    result = scores(targets[0], [panel_other], (1,), sides, tile, shape, [result])
    return scores(
        targets[1], [panel, panel_other], (0, 1), [fars[1:]], tile, shape, [result]
    )


def solution(mesh):
    in_specs = (P("mp", "dp", "tensor"), P("mp", "tensor", "dp"), P("mp", "tensor", "dp"), P())
    out_specs = P(("mp", "tensor"), "dp")
    paired = mesh.shape["mp"] == 2 and mesh.shape["tensor"] == 2 and mesh.shape["dp"] == 2 * CHIPS

    def body(acts, gate_w, up_w, panel_units):
        picked = panel_units.shape[0] // (4 * 2 * CHIPS)
        units = gate_w.shape[2]
        fits = picked % 128 == 0 and units % (2 * picked) == 0 and units % 512 == 0
        fits = fits and units >= 10 * picked
        if paired and fits and acts.shape[1] % 16 == 0:
            return paired_body(acts, gate_w, up_w, panel_units)
        return general_body(acts, gate_w, up_w, panel_units)

    return jax.shard_map(body, mesh=mesh, in_specs=in_specs, out_specs=out_specs, check_vma=False)
```

```python
import functools
import math

import jax
import jax.numpy as jnp
from jax import lax
from jax.experimental import pallas as pl
from jax.experimental.pallas import tpu as pltpu
from jax.sharding import PartitionSpec as P

epsilon = 1e-05
AXES = ("mp", "dp", "tensor")
MIB = 1 << 20


def from_partner(block, axis, distance):
    count = lax.axis_size(axis)
    route = []
    for low in range(count):
        high = low | 1 << distance
        if high != low and high < count:
            route += [(low, high), (high, low)]
    return lax.ppermute(block, axis, route)


def cross_models(full_units, panel_own, panel_next, model_index):
    other_units, other_panel = from_partner((full_units, panel_next), "mp", 0)
    is_first = model_index == 0
    return (
        jnp.where(is_first, panel_own, other_panel),
        jnp.where(is_first, other_units, full_units),
    )


def general_body(acts, gate_w, up_w, panel_units):
    model_index = lax.axis_index("mp")
    unit_block = lax.axis_index("dp")
    n_model = lax.axis_size("mp")
    n_data = lax.axis_size("dp")
    n_width = lax.axis_size("tensor")
    weight_gate = gate_w[0]
    weight_up = up_w[0]
    units = weight_gate.shape[1]
    gathered = lax.all_gather(acts[0], "dp", axis=0, tiled=True)
    tokens = gathered.shape[0]
    token_share = tokens // n_width
    score_scale = 1.0 / math.sqrt(tokens)
    panel_picks = panel_units.reshape(n_model, n_width, n_data, -1)
    panel_picks = (
        lax.dynamic_index_in_dim(panel_picks, unit_block, axis=2, keepdims=False)
        - unit_block * units
    )
    gate_part = jnp.dot(gathered, weight_gate, preferred_element_type=jnp.float32)
    up_part = jnp.dot(gathered, weight_up, preferred_element_type=jnp.float32)
    summed = lax.psum_scatter(
        jnp.concatenate([gate_part, up_part], axis=1).astype(jnp.bfloat16),
        "tensor",
        scatter_dimension=0,
        tiled=True,
    ).astype(jnp.float32)
    hidden = (jax.nn.silu(summed[:, :units]) * summed[:, units:]).astype(jnp.bfloat16)
    wide_hidden = hidden.astype(jnp.float32)
    totals = lax.psum(
        (jnp.sum(wide_hidden, axis=0), jnp.sum(wide_hidden * wide_hidden, axis=0)), "tensor"
    )
    unit_mean = totals[0] / tokens
    unit_var = totals[1] / tokens - unit_mean * unit_mean
    scored = ((wide_hidden - unit_mean) * lax.rsqrt(unit_var + epsilon)).astype(jnp.bfloat16)
    full_units = lax.all_gather(scored, "tensor", axis=0, tiled=True)
    order_list = panel_picks.transpose(1, 0, 2).reshape(-1)
    chosen = jnp.take(scored, order_list, axis=1).reshape(token_share, n_width, -1)
    moved_rows = lax.all_to_all(chosen, "tensor", split_axis=1, concat_axis=0, tiled=True)
    moved_rows = moved_rows.reshape(tokens, n_model, -1)
    panel_cols = lax.all_gather(moved_rows, "dp", axis=2, tiled=True)
    mine_a, mine_b = cross_models(full_units, panel_cols[:, 0], panel_cols[:, 1], model_index)
    result = lax.dot_general(
        mine_a, mine_b, (((0,), (0,)), ((), ())), preferred_element_type=jnp.float32
    )
    return (result * score_scale).astype(jnp.bfloat16)


CHIPS = 4


def routes(sizes, move):
    n_model, n_data, n_width = sizes
    pairs = []
    for m in range(n_model):
        for d in range(n_data):
            for t in range(n_width):
                to = move(m, d, t)
                if to is not None:
                    source = (m * n_data + d) * n_width + t
                    pairs.append((source, (to[0] * n_data + to[1]) * n_width + to[2]))
    return pairs


def send(block, sizes, move):
    return lax.ppermute(block, AXES, routes(sizes, move))


def other_core(m, d, t):
    return m, d ^ 1, t


def shifted(step):
    def move(m, d, t):
        return m, (d + 2 * step) % (2 * CHIPS), t

    return move


def shifts(block, sizes):
    came = [send(block, sizes, shifted(step)) for step in (1, CHIPS - 1, 2)]
    return [block, came[0], came[2], came[1]]


def join_kernel(count, *refs):
    out_ref, sems = refs[-2:]
    rows = refs[0].shape[0]
    copies = [
        pltpu.make_async_copy(refs[i], out_ref.at[i * rows : (i + 1) * rows, :], sems.at[i])
        for i in range(count)
    ]
    for copy in copies:
        copy.start()
    for copy in copies:
        copy.wait()


def join(blocks, after, flops=0):
    rows, width = blocks[0].shape
    count = len(blocks)
    return call(
        functools.partial(join_kernel, count),
        out_shape=jax.ShapeDtypeStruct((count * rows, width), blocks[0].dtype),
        in_specs=[pl.BlockSpec(memory_space=pl.ANY)] * (count + len(after)),
        out_specs=pl.BlockSpec(memory_space=pltpu.VMEM),
        scratch_shapes=[pltpu.SemaphoreType.DMA((count,))],
        flops=flops,
        moved=0,
        vmem=16,
    )(*blocks, *after)


def swapped(block, sizes, distance):
    return send(block, sizes, lambda m, d, t: (m, d ^ (2 * distance), t))


SWAPS = (0, 2, 1, 3)


def canonical(index, chip, core):
    line = lax.rem(chip + CHIPS - index % CHIPS, CHIPS)
    return line * 2 + (core if index < CHIPS else 1 - core)


def call(kernel, *, flops, moved, vmem, **rest):
    return pl.pallas_call(
        kernel,
        compiler_params=pltpu.CompilerParams(vmem_limit_bytes=vmem * MIB),
        cost_estimate=pl.CostEstimate(flops=flops, bytes_accessed=moved, transcendentals=0),
        **rest,
    )


def products_kernel(counts, n_after, place_ref, gate_ref, up_ref, *refs):
    x_refs, refs = refs[: 2 * CHIPS], refs[2 * CHIPS :]
    rows = x_refs[0].shape[0]
    step = pl.program_id(0)

    def write(out_ref):
        x = jnp.concatenate([x_ref[...] for x_ref in x_refs], axis=0)
        for which, weight_ref in enumerate((gate_ref, up_ref)):
            total = jnp.dot(x, weight_ref[...], preferred_element_type=jnp.float32)
            total = total.astype(jnp.bfloat16)
            for i in range(2 * CHIPS):
                start = pl.multiple_of(canonical(i, place_ref[0], place_ref[1]) * rows, rows)
                out_ref[which, pl.ds(start, rows), :] = total[i * rows : (i + 1) * rows]

    first = 0
    for count, out_ref in zip(counts, refs[n_after:]):

        @pl.when((step >= first) & (step < first + count))
        def _():
            write(out_ref)

        first += count


def products(place, blocks, gate, up, tile, counts, after):
    rows, width = blocks[0].shape
    tokens = len(blocks) * rows
    firsts = [sum(counts[:i]) for i in range(len(counts))]

    def weight_tile(i, place_ref):
        column = place_ref[2] + i
        for run in range(1, len(counts)):
            column = jnp.where(i >= firsts[run], place_ref[2 + run] + i - firsts[run], column)
        return 0, column

    def out_tile(run):
        return lambda i, place_ref: (0, 0, jnp.clip(i - firsts[run], 0, counts[run] - 1))

    weights = pl.BlockSpec((width, tile), weight_tile)
    whole = pl.BlockSpec((rows, width), lambda i, place_ref: (0, 0))
    return call(
        functools.partial(products_kernel, counts, len(after)),
        out_shape=[
            jax.ShapeDtypeStruct((2, tokens, tile * count), jnp.bfloat16) for count in counts
        ],
        grid_spec=pltpu.PrefetchScalarGridSpec(
            num_scalar_prefetch=1,
            grid=(sum(counts),),
            in_specs=[weights, weights]
            + [whole] * len(blocks)
            + [pl.BlockSpec(memory_space=pl.ANY)] * len(after),
            out_specs=[
                pl.BlockSpec((2, tokens, tile), out_tile(run)) for run in range(len(counts))
            ],
        ),
        flops=4 * tokens * width * tile * sum(counts),
        moved=4 * width * tile * sum(counts),
        vmem=38,
    )(place, gate, up, *blocks, *after)


def pick_kernel(counts, tile, bases_ref, picks_ref, *refs):
    out_ref = refs[-1]
    tokens, picked = out_ref.shape[1:]

    @pl.when(bases_ref[len(counts)] == 0)
    def _():
        total = jnp.zeros((2 * tokens, picked), jnp.float32)
        for part, (ref, count) in enumerate(zip(refs[: len(counts)], counts)):
            for i in range(count):
                base = bases_ref[part] + i * tile
                unit = lax.broadcasted_iota(jnp.int32, (tile, picked), 0) + base
                chosen = jnp.where(unit == picks_ref[...], 1.0, 0.0).astype(jnp.bfloat16)
                block = ref[:, :, i * tile : (i + 1) * tile].reshape(2 * tokens, tile)
                total += jnp.dot(block, chosen, preferred_element_type=jnp.float32)
        out_ref[...] = total.astype(jnp.bfloat16).reshape(2, tokens, picked)

    @pl.when(bases_ref[len(counts)] == 1)
    def _():
        out_ref[...] = jnp.zeros_like(out_ref)


def pick(bases, picks, parts, tile, after):
    tokens = parts[0].shape[1]
    picked = picks.shape[1]
    counts = [part.shape[2] // tile for part in parts]
    vmem = pl.BlockSpec(memory_space=pltpu.VMEM)
    return call(
        functools.partial(pick_kernel, counts, tile),
        out_shape=jax.ShapeDtypeStruct((2, tokens, picked), jnp.bfloat16),
        in_specs=[pl.BlockSpec(memory_space=pltpu.SMEM), vmem]
        + [vmem] * len(parts)
        + [pl.BlockSpec(memory_space=pl.ANY)] * len(after),
        out_specs=vmem,
        flops=0,
        moved=0,
        vmem=16,
    )(bases, picks, *parts, *after)


def zscore(mine, theirs):
    tokens = mine.shape[1]
    gate = mine[0].astype(jnp.float32) + theirs[0].astype(jnp.float32)
    up = mine[1].astype(jnp.float32) + theirs[1].astype(jnp.float32)
    hidden = (gate / (1.0 + jnp.exp(-gate)) * up).astype(jnp.bfloat16).astype(jnp.float32)
    mean = jnp.sum(hidden, axis=0, keepdims=True) / tokens
    var = jnp.sum(hidden * hidden, axis=0, keepdims=True) / tokens - mean * mean
    return (hidden - mean) * lax.rsqrt(var + epsilon)


def unit_kernel(model_ref, mine_ref, theirs_ref, *refs):
    @pl.when(model_ref[0] == 1)
    def _():
        refs[-1][...] = zscore(mine_ref[...], theirs_ref[...]).astype(jnp.bfloat16)

    @pl.when(model_ref[0] == 0)
    def _():
        refs[-1][...] = jnp.zeros_like(refs[-1])


def unit_scores(model_number, mine, theirs, tile, first, after):
    _, tokens, units = theirs.shape
    return call(
        unit_kernel,
        out_shape=jax.ShapeDtypeStruct((tokens, units), jnp.bfloat16),
        grid_spec=pltpu.PrefetchScalarGridSpec(
            num_scalar_prefetch=1,
            grid=(units // tile,),
            in_specs=[
                pl.BlockSpec((2, tokens, tile), lambda i, model: (0, 0, (first + i) * model[0])),
                pl.BlockSpec((2, tokens, tile), lambda i, model: (0, 0, i * model[0])),
            ]
            + [pl.BlockSpec(memory_space=pl.ANY)] * len(after),
            out_specs=pl.BlockSpec((tokens, tile), lambda i, model: (0, i)),
        ),
        flops=0,
        moved=0,
        vmem=16,
    )(model_number, mine, theirs, *after)


def panel_kernel(mine_ref, theirs_ref, out_ref):
    out_ref[...] = zscore(mine_ref[...], theirs_ref[...]).T.astype(jnp.bfloat16)


def panel_kernel_or(model_ref, mine_ref, theirs_ref, given_ref, *refs):
    out_ref = refs[-1]

    @pl.when(model_ref[0] == 0)
    def _():
        panel_kernel(mine_ref, theirs_ref, out_ref)

    @pl.when(model_ref[0] == 1)
    def _():
        out_ref[...] = given_ref[...]


def panel_scores(mine, theirs, first, given=(), after=()):
    _, tokens, count = theirs.shape
    rows = pl.BlockSpec((count, tokens), lambda i: (0, 0))
    units = [
        pl.BlockSpec((2, tokens, count), lambda i: (0, 0, first)),
        pl.BlockSpec((2, tokens, count), lambda i: (0, 0, 0)),
    ]
    return call(
        panel_kernel_or if given else panel_kernel,
        out_shape=jax.ShapeDtypeStruct((count, tokens), jnp.bfloat16),
        grid=(1,),
        in_specs=(
            [pl.BlockSpec(memory_space=pltpu.SMEM), *units, rows]
            + [pl.BlockSpec(memory_space=pl.ANY)] * len(after)
            if given
            else units
        ),
        out_specs=rows,
        flops=0,
        moved=0,
        vmem=16,
    )(*given[:1], mine, theirs, *given[1:], *after)


def score_kernel(scale, tile, cores, widths, n_after, where_ref, *refs):
    panels, refs = refs[: len(cores)], refs[len(cores) :]
    pieces = []
    for side in widths:
        pieces.append(refs[: 2 * len(side)])
        refs = refs[2 * len(side) :]
    out_ref, panel_ref, refs = refs[n_after], refs[n_after + 1], refs[n_after + 2 :]
    units_refs, block_refs = refs[: len(widths)], refs[len(widths) : 2 * len(widths)]
    in_sems, out_sems = refs[2 * len(widths) :]
    model, chip, core = (where_ref[i] for i in range(3))
    rows = panel_ref.shape[1] // CHIPS

    def fetch(holder):
        pairs = [(ref, panel_ref.at[i]) for i, ref in enumerate(panels)]
        for side, into in zip(pieces, units_refs):
            start = 0
            for ref in side[holder::2]:
                pairs.append((ref, into.at[:, start : start + ref.shape[1]]))
                start += ref.shape[1]
        copies = [
            pltpu.make_async_copy(source, into, in_sems.at[i])
            for i, (source, into) in enumerate(pairs)
        ]
        for copy in copies:
            copy.start()
        for copy in copies:
            copy.wait()

    for holder in range(2):

        @pl.when(model == holder)
        def _():
            fetch(holder)

    copies = []
    for which, other in enumerate(cores):
        for pair in range(CHIPS // 2):
            panel = panel_ref[which, 2 * pair * rows : (2 * pair + 2) * rows, :]
            slot = which * (CHIPS // 2) + pair
            for side, (units_ref, block_ref) in enumerate(zip(units_refs, block_refs)):
                columns = units_ref.shape[1]
                for start in range(0, columns, tile):
                    total = jnp.dot(
                        panel,
                        units_ref[:, start : start + tile],
                        preferred_element_type=jnp.float32,
                    )
                    block_ref[slot, :, :, start : start + tile] = (
                        (total * scale).astype(jnp.bfloat16).reshape(2, rows, tile)
                    )
                for i in range(2):
                    line = lax.bitwise_xor(chip, SWAPS[2 * pair + i])
                    place = line * 2 + (1 - core if other else core)
                    copies.append(
                        pltpu.make_async_copy(
                            block_ref.at[slot, i],
                            out_ref.at[
                                pl.ds(pl.multiple_of(place * rows, rows), rows),
                                pl.ds(pl.multiple_of(where_ref[3 + side], 128), columns),
                            ],
                            out_sems.at[slot, side, i],
                        )
                    )
                    copies[-1].start()
    for copy in copies:
        copy.wait()


def scores(where, panels, cores, sides, tile, shape, before):
    rows, tokens = panels[0].shape
    widths = [[piece[0].shape[1] for piece in side] for side in sides]
    slots = len(panels) * CHIPS // 2
    anywhere = pl.BlockSpec(memory_space=pl.ANY)
    flat = [array for side in sides for piece in side for array in piece]
    columns = [sum(side) for side in widths]
    return call(
        functools.partial(
            score_kernel, 1.0 / math.sqrt(tokens), tile, cores, widths, len(before)
        ),
        out_shape=jax.ShapeDtypeStruct(shape, jnp.bfloat16),
        in_specs=[pl.BlockSpec(memory_space=pltpu.SMEM)]
        + [anywhere] * (len(panels) + len(flat) + len(before)),
        out_specs=anywhere,
        scratch_shapes=[pltpu.VMEM((len(panels), rows, tokens), jnp.bfloat16)]
        + [pltpu.VMEM((tokens, count), jnp.bfloat16) for count in columns]
        + [pltpu.VMEM((slots, 2, rows // CHIPS, count), jnp.bfloat16) for count in columns]
        + [
            pltpu.SemaphoreType.DMA((len(panels) + sum(map(len, widths)),)),
            pltpu.SemaphoreType.DMA((slots, len(sides), 2)),
        ],
        input_output_aliases={1 + len(panels) + len(flat): 0} if before else {},
        flops=2 * len(panels) * rows * tokens * sum(columns),
        moved=2 * len(panels) * rows * sum(columns),
        vmem=24,
    )(where, *panels, *flat, *before)


def paired_body(acts, gate_w, up_w, panel_units):
    model = lax.axis_index("mp")
    block = lax.axis_index("dp")
    side = lax.axis_index("tensor")
    sizes = tuple(lax.axis_size(name) for name in AXES)
    chip, core = block // 2, block % 2
    gate, up = gate_w[0], up_w[0]
    units = gate.shape[1]
    picks = panel_units.reshape(2, 2, sizes[1], -1)
    tile = picks.shape[3]
    half = units // 2 // tile
    chunks = [half - half // 2, half // 2]

    def b_sides(m, d, t):
        return (m, d, 1 - t) if m == 1 else None

    def both_sides(m, d, t):
        return m, d, 1 - t

    def a_sides(m, d, t):
        return (m, d, 1 - t) if m == 0 else None

    def b_to_a(m, d, t):
        return (0, d, t) if m == 1 else None

    def a_to_b(m, d, t):
        return (1, d, t) if m == 0 else None

    own = join([acts[0]], [])
    blocks = [own, *shifts(acts[0], sizes)[1:]]
    blocks += [send(part, sizes, other_core) for part in blocks]

    picks = lax.dynamic_index_in_dim(picks, block, axis=2, keepdims=False) - block * units
    picks_far = lax.dynamic_index_in_dim(picks, 1 - side, axis=1, keepdims=False)
    picks_b, picks_a = picks_far[1:], picks_far[:1]
    picks_own = lax.dynamic_index_in_dim(picks, side, axis=1, keepdims=False).reshape(1, -1)
    bases = [((1 - side) * half + first) * tile for first in (0, chunks[0])]
    bases += [side * half * tile, model]
    bases = jnp.stack(bases).astype(jnp.int32)
    model_number = jnp.reshape(model, (1,)).astype(jnp.int32)
    near, far = side * half * tile, (1 - side) * half * tile
    targets = [[model, chip, core, near, far], [model, chip, core, far + chunks[0] * tile]]
    targets = [jnp.stack(target).astype(jnp.int32) for target in targets]

    to_side, own_side = (1 - side) * half, side * half
    places = [[chip, core, to_side], [chip, core, to_side + chunks[0], own_side]]
    places = [jnp.stack(place).astype(jnp.int32) for place in places]
    ready = [picks_b, picks_a, picks_own, bases, model_number, *places, *targets]
    sent = products(places[0], blocks, gate, up, tile, chunks[:1], ready)
    sent += products(places[1], blocks, gate, up, tile, [chunks[1], half], sent)
    kept = sent[-1]
    came = [send(part, sizes, b_sides) for part in sent[:2]]

    z = unit_scores(model_number, kept, came[0], tile, 0, [])
    a_mine = send(z, sizes, b_to_a)
    nears, fars = [(a_mine, z)], [(send(a_mine, sizes, a_sides), send(z, sizes, b_sides))]

    picked_b = pick(bases, picks_b, sent, tile, [z])
    picked_a = pick(bases, picks_a, sent, tile, [picked_b])
    picked_own = pick(bases, picks_own, sent, tile, [picked_a])
    rows_b = panel_scores(picked_own, send(picked_b, sizes, a_sides), 1)
    rows_b = send(rows_b, sizes, a_to_b)
    rows = panel_scores(
        picked_own, send(picked_a, sizes, a_sides), 0, (model_number, rows_b)
    )

    z = unit_scores(model_number, kept, came[1], tile, chunks[0], [rows, a_mine])
    nears.append((send(z, sizes, b_to_a), z))
    fars.append((send(nears[1][0], sizes, a_sides), send(z, sizes, b_sides)))

    panel = join([rows, swapped(rows, sizes, 2)], [z], 1 << 33)
    panel = join([panel, swapped(panel, sizes, 1)], [*fars[0], nears[1][0]])
    panel_other = send(panel, sizes, other_core)
    shape = (2 * CHIPS * rows.shape[0], units)
    sides = [nears, fars[:1]]
    result = scores(targets[0], [panel], (0,), sides, tile, shape, [])
    result = scores(targets[0], [panel_other], (1,), sides, tile, shape, [result])
    return scores(
        targets[1], [panel, panel_other], (0, 1), [fars[1:]], tile, shape, [result]
    )


def solution(mesh):
    in_specs = (P("mp", "dp", "tensor"), P("mp", "tensor", "dp"), P("mp", "tensor", "dp"), P())
    out_specs = P(("mp", "tensor"), "dp")
    paired = mesh.shape["mp"] == 2 and mesh.shape["tensor"] == 2 and mesh.shape["dp"] == 2 * CHIPS

    def body(acts, gate_w, up_w, panel_units):
        picked = panel_units.shape[0] // (4 * 2 * CHIPS)
        units = gate_w.shape[2]
        fits = picked % 128 == 0 and units % (2 * picked) == 0 and units % 512 == 0
        fits = fits and units >= 10 * picked
        if paired and fits and acts.shape[1] % 16 == 0:
            return paired_body(acts, gate_w, up_w, panel_units)
        return general_body(acts, gate_w, up_w, panel_units)

    return jax.shard_map(body, mesh=mesh, in_specs=in_specs, out_specs=out_specs, check_vma=False)
```

```python
import functools
import math

import jax
import jax.numpy as jnp
from jax import lax
from jax.experimental import pallas as pl
from jax.experimental.pallas import tpu as pltpu
from jax.sharding import PartitionSpec as P

epsilon = 1e-05
AXES = ("mp", "dp", "tensor")
MIB = 1 << 20


def from_partner(block, axis, distance):
    count = lax.axis_size(axis)
    route = []
    for low in range(count):
        high = low | 1 << distance
        if high != low and high < count:
            route += [(low, high), (high, low)]
    return lax.ppermute(block, axis, route)


def cross_models(full_units, panel_own, panel_next, model_index):
    other_units, other_panel = from_partner((full_units, panel_next), "mp", 0)
    is_first = model_index == 0
    return (
        jnp.where(is_first, panel_own, other_panel),
        jnp.where(is_first, other_units, full_units),
    )


def general_body(acts, gate_w, up_w, panel_units):
    model_index = lax.axis_index("mp")
    unit_block = lax.axis_index("dp")
    n_model = lax.axis_size("mp")
    n_data = lax.axis_size("dp")
    n_width = lax.axis_size("tensor")
    weight_gate = gate_w[0]
    weight_up = up_w[0]
    units = weight_gate.shape[1]
    gathered = lax.all_gather(acts[0], "dp", axis=0, tiled=True)
    tokens = gathered.shape[0]
    token_share = tokens // n_width
    score_scale = 1.0 / math.sqrt(tokens)
    panel_picks = panel_units.reshape(n_model, n_width, n_data, -1)
    panel_picks = (
        lax.dynamic_index_in_dim(panel_picks, unit_block, axis=2, keepdims=False)
        - unit_block * units
    )
    gate_part = jnp.dot(gathered, weight_gate, preferred_element_type=jnp.float32)
    up_part = jnp.dot(gathered, weight_up, preferred_element_type=jnp.float32)
    summed = lax.psum_scatter(
        jnp.concatenate([gate_part, up_part], axis=1).astype(jnp.bfloat16),
        "tensor",
        scatter_dimension=0,
        tiled=True,
    ).astype(jnp.float32)
    hidden = (jax.nn.silu(summed[:, :units]) * summed[:, units:]).astype(jnp.bfloat16)
    wide_hidden = hidden.astype(jnp.float32)
    totals = lax.psum(
        (jnp.sum(wide_hidden, axis=0), jnp.sum(wide_hidden * wide_hidden, axis=0)), "tensor"
    )
    unit_mean = totals[0] / tokens
    unit_var = totals[1] / tokens - unit_mean * unit_mean
    scored = ((wide_hidden - unit_mean) * lax.rsqrt(unit_var + epsilon)).astype(jnp.bfloat16)
    full_units = lax.all_gather(scored, "tensor", axis=0, tiled=True)
    order_list = panel_picks.transpose(1, 0, 2).reshape(-1)
    chosen = jnp.take(scored, order_list, axis=1).reshape(token_share, n_width, -1)
    moved_rows = lax.all_to_all(chosen, "tensor", split_axis=1, concat_axis=0, tiled=True)
    moved_rows = moved_rows.reshape(tokens, n_model, -1)
    panel_cols = lax.all_gather(moved_rows, "dp", axis=2, tiled=True)
    mine_a, mine_b = cross_models(full_units, panel_cols[:, 0], panel_cols[:, 1], model_index)
    result = lax.dot_general(
        mine_a, mine_b, (((0,), (0,)), ((), ())), preferred_element_type=jnp.float32
    )
    return (result * score_scale).astype(jnp.bfloat16)


CHIPS = 4


def routes(sizes, move):
    n_model, n_data, n_width = sizes
    pairs = []
    for m in range(n_model):
        for d in range(n_data):
            for t in range(n_width):
                to = move(m, d, t)
                if to is not None:
                    source = (m * n_data + d) * n_width + t
                    pairs.append((source, (to[0] * n_data + to[1]) * n_width + to[2]))
    return pairs


def send(block, sizes, move):
    return lax.ppermute(block, AXES, routes(sizes, move))


def other_core(m, d, t):
    return m, d ^ 1, t


def shifted(step):
    def move(m, d, t):
        return m, (d + 2 * step) % (2 * CHIPS), t

    return move


def shifts(block, sizes):
    came = [send(block, sizes, shifted(step)) for step in (1, CHIPS - 1, 2)]
    return [block, came[0], came[2], came[1]]


def join_kernel(count, *refs):
    out_ref, sems = refs[-2:]
    rows = refs[0].shape[0]
    copies = [
        pltpu.make_async_copy(refs[i], out_ref.at[i * rows : (i + 1) * rows, :], sems.at[i])
        for i in range(count)
    ]
    for copy in copies:
        copy.start()
    for copy in copies:
        copy.wait()


def join(blocks, after):
    rows, width = blocks[0].shape
    count = len(blocks)
    return call(
        functools.partial(join_kernel, count),
        out_shape=jax.ShapeDtypeStruct((count * rows, width), blocks[0].dtype),
        in_specs=[pl.BlockSpec(memory_space=pl.ANY)] * (count + len(after)),
        out_specs=pl.BlockSpec(memory_space=pltpu.VMEM),
        scratch_shapes=[pltpu.SemaphoreType.DMA((count,))],
        flops=0,
        moved=0,
        vmem=16,
    )(*blocks, *after)


def swapped(block, sizes, distance):
    return send(block, sizes, lambda m, d, t: (m, d ^ (2 * distance), t))


SWAPS = (0, 2, 1, 3)


def canonical(index, chip, core):
    line = lax.rem(chip + CHIPS - index % CHIPS, CHIPS)
    return line * 2 + (core if index < CHIPS else 1 - core)


def call(kernel, *, flops, moved, vmem, **rest):
    return pl.pallas_call(
        kernel,
        compiler_params=pltpu.CompilerParams(vmem_limit_bytes=vmem * MIB),
        cost_estimate=pl.CostEstimate(flops=flops, bytes_accessed=moved, transcendentals=0),
        **rest,
    )


def products_kernel(counts, n_after, place_ref, gate_ref, up_ref, *refs):
    x_refs, refs = refs[: 2 * CHIPS], refs[2 * CHIPS :]
    rows = x_refs[0].shape[0]
    step = pl.program_id(0)

    def write(out_ref):
        x = jnp.concatenate([x_ref[...] for x_ref in x_refs], axis=0)
        for which, weight_ref in enumerate((gate_ref, up_ref)):
            total = jnp.dot(x, weight_ref[...], preferred_element_type=jnp.float32)
            total = total.astype(jnp.bfloat16)
            for i in range(2 * CHIPS):
                start = pl.multiple_of(canonical(i, place_ref[0], place_ref[1]) * rows, rows)
                out_ref[which, pl.ds(start, rows), :] = total[i * rows : (i + 1) * rows]

    first = 0
    for count, out_ref in zip(counts, refs[n_after:]):

        @pl.when((step >= first) & (step < first + count))
        def _():
            write(out_ref)

        first += count


def products(place, blocks, gate, up, tile, counts, after):
    rows, width = blocks[0].shape
    tokens = len(blocks) * rows
    firsts = [sum(counts[:i]) for i in range(len(counts))]

    def weight_tile(i, place_ref):
        column = place_ref[2] + i
        for run in range(1, len(counts)):
            column = jnp.where(i >= firsts[run], place_ref[2 + run] + i - firsts[run], column)
        return 0, column

    def out_tile(run):
        return lambda i, place_ref: (0, 0, jnp.clip(i - firsts[run], 0, counts[run] - 1))

    weights = pl.BlockSpec((width, tile), weight_tile)
    whole = pl.BlockSpec((rows, width), lambda i, place_ref: (0, 0))
    return call(
        functools.partial(products_kernel, counts, len(after)),
        out_shape=[
            jax.ShapeDtypeStruct((2, tokens, tile * count), jnp.bfloat16) for count in counts
        ],
        grid_spec=pltpu.PrefetchScalarGridSpec(
            num_scalar_prefetch=1,
            grid=(sum(counts),),
            in_specs=[weights, weights]
            + [whole] * len(blocks)
            + [pl.BlockSpec(memory_space=pl.ANY)] * len(after),
            out_specs=[
                pl.BlockSpec((2, tokens, tile), out_tile(run)) for run in range(len(counts))
            ],
        ),
        flops=4 * tokens * width * tile * sum(counts),
        moved=4 * width * tile * sum(counts),
        vmem=38,
    )(place, gate, up, *blocks, *after)


def pick_kernel(counts, tile, bases_ref, picks_ref, *refs):
    out_ref = refs[-1]
    tokens, picked = out_ref.shape[1:]

    @pl.when(bases_ref[len(counts)] == 0)
    def _():
        total = jnp.zeros((2 * tokens, picked), jnp.float32)
        for part, (ref, count) in enumerate(zip(refs[: len(counts)], counts)):
            for i in range(count):
                base = bases_ref[part] + i * tile
                unit = lax.broadcasted_iota(jnp.int32, (tile, picked), 0) + base
                chosen = jnp.where(unit == picks_ref[...], 1.0, 0.0).astype(jnp.bfloat16)
                block = ref[:, :, i * tile : (i + 1) * tile].reshape(2 * tokens, tile)
                total += jnp.dot(block, chosen, preferred_element_type=jnp.float32)
        out_ref[...] = total.astype(jnp.bfloat16).reshape(2, tokens, picked)

    @pl.when(bases_ref[len(counts)] == 1)
    def _():
        out_ref[...] = jnp.zeros_like(out_ref)


def pick(bases, picks, parts, tile, after):
    tokens = parts[0].shape[1]
    picked = picks.shape[1]
    counts = [part.shape[2] // tile for part in parts]
    vmem = pl.BlockSpec(memory_space=pltpu.VMEM)
    return call(
        functools.partial(pick_kernel, counts, tile),
        out_shape=jax.ShapeDtypeStruct((2, tokens, picked), jnp.bfloat16),
        in_specs=[pl.BlockSpec(memory_space=pltpu.SMEM), vmem]
        + [vmem] * len(parts)
        + [pl.BlockSpec(memory_space=pl.ANY)] * len(after),
        out_specs=vmem,
        flops=0,
        moved=0,
        vmem=16,
    )(bases, picks, *parts, *after)


def zscore(mine, theirs):
    tokens = mine.shape[1]
    gate = mine[0].astype(jnp.float32) + theirs[0].astype(jnp.float32)
    up = mine[1].astype(jnp.float32) + theirs[1].astype(jnp.float32)
    hidden = (gate / (1.0 + jnp.exp(-gate)) * up).astype(jnp.bfloat16).astype(jnp.float32)
    mean = jnp.sum(hidden, axis=0, keepdims=True) / tokens
    var = jnp.sum(hidden * hidden, axis=0, keepdims=True) / tokens - mean * mean
    return (hidden - mean) * lax.rsqrt(var + epsilon)


def unit_kernel(model_ref, mine_ref, theirs_ref, *refs):
    @pl.when(model_ref[0] == 1)
    def _():
        refs[-1][...] = zscore(mine_ref[...], theirs_ref[...]).astype(jnp.bfloat16)

    @pl.when(model_ref[0] == 0)
    def _():
        refs[-1][...] = jnp.zeros_like(refs[-1])


def unit_scores(model_number, mine, theirs, tile, first, after):
    _, tokens, units = theirs.shape
    return call(
        unit_kernel,
        out_shape=jax.ShapeDtypeStruct((tokens, units), jnp.bfloat16),
        grid_spec=pltpu.PrefetchScalarGridSpec(
            num_scalar_prefetch=1,
            grid=(units // tile,),
            in_specs=[
                pl.BlockSpec((2, tokens, tile), lambda i, model: (0, 0, (first + i) * model[0])),
                pl.BlockSpec((2, tokens, tile), lambda i, model: (0, 0, i * model[0])),
            ]
            + [pl.BlockSpec(memory_space=pl.ANY)] * len(after),
            out_specs=pl.BlockSpec((tokens, tile), lambda i, model: (0, i)),
        ),
        flops=0,
        moved=0,
        vmem=16,
    )(model_number, mine, theirs, *after)


def panel_kernel(mine_ref, theirs_ref, out_ref):
    out_ref[...] = zscore(mine_ref[...], theirs_ref[...]).T.astype(jnp.bfloat16)


def panel_kernel_or(model_ref, mine_ref, theirs_ref, given_ref, *refs):
    out_ref = refs[-1]

    @pl.when(model_ref[0] == 0)
    def _():
        panel_kernel(mine_ref, theirs_ref, out_ref)

    @pl.when(model_ref[0] == 1)
    def _():
        out_ref[...] = given_ref[...]


def panel_scores(mine, theirs, first, given=(), after=()):
    _, tokens, count = theirs.shape
    rows = pl.BlockSpec((count, tokens), lambda i: (0, 0))
    units = [
        pl.BlockSpec((2, tokens, count), lambda i: (0, 0, first)),
        pl.BlockSpec((2, tokens, count), lambda i: (0, 0, 0)),
    ]
    return call(
        panel_kernel_or if given else panel_kernel,
        out_shape=jax.ShapeDtypeStruct((count, tokens), jnp.bfloat16),
        grid=(1,),
        in_specs=(
            [pl.BlockSpec(memory_space=pltpu.SMEM), *units, rows]
            + [pl.BlockSpec(memory_space=pl.ANY)] * len(after)
            if given
            else units
        ),
        out_specs=rows,
        flops=0,
        moved=0,
        vmem=16,
    )(*given[:1], mine, theirs, *given[1:], *after)


def score_kernel(scale, tile, cores, widths, n_after, where_ref, *refs):
    panels, refs = refs[: len(cores)], refs[len(cores) :]
    pieces = []
    for side in widths:
        pieces.append(refs[: 2 * len(side)])
        refs = refs[2 * len(side) :]
    out_ref, panel_ref, refs = refs[n_after], refs[n_after + 1], refs[n_after + 2 :]
    units_refs, block_refs = refs[: len(widths)], refs[len(widths) : 2 * len(widths)]
    in_sems, out_sems = refs[2 * len(widths) :]
    model, chip, core = (where_ref[i] for i in range(3))
    rows = panel_ref.shape[1] // CHIPS

    def fetch(holder):
        pairs = [(ref, panel_ref.at[i]) for i, ref in enumerate(panels)]
        for side, into in zip(pieces, units_refs):
            start = 0
            for ref in side[holder::2]:
                pairs.append((ref, into.at[:, start : start + ref.shape[1]]))
                start += ref.shape[1]
        copies = [
            pltpu.make_async_copy(source, into, in_sems.at[i])
            for i, (source, into) in enumerate(pairs)
        ]
        for copy in copies:
            copy.start()
        for copy in copies:
            copy.wait()

    for holder in range(2):

        @pl.when(model == holder)
        def _():
            fetch(holder)

    copies = []
    for which, other in enumerate(cores):
        for side, (units_ref, block_ref) in enumerate(zip(units_refs, block_refs)):
            for start in range(0, units_ref.shape[1], tile):
                total = jnp.dot(
                    panel_ref[which],
                    units_ref[:, start : start + tile],
                    preferred_element_type=jnp.float32,
                )
                block_ref[which, :, :, start : start + tile] = (
                    (total * scale).astype(jnp.bfloat16).reshape(CHIPS, rows, tile)
                )
                for i in range(CHIPS):
                    line = lax.bitwise_xor(chip, SWAPS[i])
                    place = line * 2 + (1 - core if other else core)
                    copies.append(
                        pltpu.make_async_copy(
                            block_ref.at[which, i, :, start : start + tile],
                            out_ref.at[
                                pl.ds(pl.multiple_of(place * rows, rows), rows),
                                pl.ds(pl.multiple_of(where_ref[3 + side] + start, 128), tile),
                            ],
                            out_sems.at[len(copies)],
                        )
                    )
                    copies[-1].start()
    for copy in copies:
        copy.wait()


def scores(where, panels, cores, sides, tile, shape, before):
    rows, tokens = panels[0].shape
    widths = [[piece[0].shape[1] for piece in side] for side in sides]
    anywhere = pl.BlockSpec(memory_space=pl.ANY)
    flat = [array for side in sides for piece in side for array in piece]
    columns = [sum(side) for side in widths]
    return call(
        functools.partial(
            score_kernel, 1.0 / math.sqrt(tokens), tile, cores, widths, len(before)
        ),
        out_shape=jax.ShapeDtypeStruct(shape, jnp.bfloat16),
        in_specs=[pl.BlockSpec(memory_space=pltpu.SMEM)]
        + [anywhere] * (len(panels) + len(flat) + len(before)),
        out_specs=anywhere,
        scratch_shapes=[pltpu.VMEM((len(panels), rows, tokens), jnp.bfloat16)]
        + [pltpu.VMEM((tokens, count), jnp.bfloat16) for count in columns]
        + [pltpu.VMEM((len(panels), CHIPS, rows // CHIPS, count), jnp.bfloat16) for count in columns]
        + [
            pltpu.SemaphoreType.DMA((len(panels) + sum(map(len, widths)),)),
            pltpu.SemaphoreType.DMA((len(panels) * CHIPS * sum(columns) // tile,)),
        ],
        input_output_aliases={1 + len(panels) + len(flat): 0} if before else {},
        flops=2 * len(panels) * rows * tokens * sum(columns),
        moved=2 * len(panels) * rows * sum(columns),
        vmem=24,
    )(where, *panels, *flat, *before)


def paired_body(acts, gate_w, up_w, panel_units):
    model = lax.axis_index("mp")
    block = lax.axis_index("dp")
    side = lax.axis_index("tensor")
    sizes = tuple(lax.axis_size(name) for name in AXES)
    chip, core = block // 2, block % 2
    gate, up = gate_w[0], up_w[0]
    units = gate.shape[1]
    picks = panel_units.reshape(2, 2, sizes[1], -1)
    tile = picks.shape[3]
    half = units // 2 // tile
    chunks = [half - half // 2, half // 2]

    def b_sides(m, d, t):
        return (m, d, 1 - t) if m == 1 else None

    def both_sides(m, d, t):
        return m, d, 1 - t

    def a_sides(m, d, t):
        return (m, d, 1 - t) if m == 0 else None

    def b_to_a(m, d, t):
        return (0, d, t) if m == 1 else None

    def a_to_b(m, d, t):
        return (1, d, t) if m == 0 else None

    own = join([acts[0]], [])
    blocks = [own, *shifts(acts[0], sizes)[1:]]
    blocks += [send(part, sizes, other_core) for part in blocks]

    picks = lax.dynamic_index_in_dim(picks, block, axis=2, keepdims=False) - block * units
    picks_far = lax.dynamic_index_in_dim(picks, 1 - side, axis=1, keepdims=False)
    picks_b, picks_a = picks_far[1:], picks_far[:1]
    picks_own = lax.dynamic_index_in_dim(picks, side, axis=1, keepdims=False).reshape(1, -1)
    bases = [((1 - side) * half + first) * tile for first in (0, chunks[0])]
    bases += [side * half * tile, model]
    bases = jnp.stack(bases).astype(jnp.int32)
    model_number = jnp.reshape(model, (1,)).astype(jnp.int32)
    near, far = side * half * tile, (1 - side) * half * tile
    targets = [[model, chip, core, near, far], [model, chip, core, far + chunks[0] * tile]]
    targets = [jnp.stack(target).astype(jnp.int32) for target in targets]

    to_side, own_side = (1 - side) * half, side * half
    places = [[chip, core, to_side], [chip, core, to_side + chunks[0], own_side]]
    places = [jnp.stack(place).astype(jnp.int32) for place in places]
    ready = [picks_b, picks_a, picks_own, bases, model_number, *places, *targets]
    sent = products(places[0], blocks, gate, up, tile, chunks[:1], ready)
    sent += products(places[1], blocks, gate, up, tile, [chunks[1], half], sent)
    kept = sent[-1]
    came = [send(part, sizes, b_sides) for part in sent[:2]]

    z = unit_scores(model_number, kept, came[0], tile, 0, [])
    a_mine = send(z, sizes, b_to_a)
    nears, fars = [(a_mine, z)], [(send(a_mine, sizes, a_sides), send(z, sizes, b_sides))]

    picked_b = pick(bases, picks_b, sent, tile, [z])
    picked_a = pick(bases, picks_a, sent, tile, [picked_b])
    picked_own = pick(bases, picks_own, sent, tile, [picked_a])
    rows_b = panel_scores(picked_own, send(picked_b, sizes, a_sides), 1)
    rows_b = send(rows_b, sizes, a_to_b)
    rows = panel_scores(
        picked_own, send(picked_a, sizes, a_sides), 0, (model_number, rows_b)
    )

    z = unit_scores(model_number, kept, came[1], tile, chunks[0], [rows])
    nears.append((send(z, sizes, b_to_a), z))
    fars.append((send(nears[1][0], sizes, a_sides), send(z, sizes, b_sides)))

    panel = join([rows, swapped(rows, sizes, 2)], [z])
    panel = join([panel, swapped(panel, sizes, 1)], [*fars[0], nears[1][0], fars[1][1]])
    panel_other = send(panel, sizes, other_core)
    shape = (2 * CHIPS * rows.shape[0], units)
    sides = [nears, fars[:1]]
    result = scores(targets[0], [panel], (0,), sides, tile, shape, [])
    result = scores(targets[0], [panel_other], (1,), sides, tile, shape, [result])
    return scores(
        targets[1], [panel, panel_other], (0, 1), [fars[1:]], tile, shape, [result]
    )


def solution(mesh):
    in_specs = (P("mp", "dp", "tensor"), P("mp", "tensor", "dp"), P("mp", "tensor", "dp"), P())
    out_specs = P(("mp", "tensor"), "dp")
    paired = mesh.shape["mp"] == 2 and mesh.shape["tensor"] == 2 and mesh.shape["dp"] == 2 * CHIPS

    def body(acts, gate_w, up_w, panel_units):
        picked = panel_units.shape[0] // (4 * 2 * CHIPS)
        units = gate_w.shape[2]
        fits = picked % 128 == 0 and units % (2 * picked) == 0 and units % 512 == 0
        fits = fits and units >= 10 * picked
        if paired and fits and acts.shape[1] % 16 == 0:
            return paired_body(acts, gate_w, up_w, panel_units)
        return general_body(acts, gate_w, up_w, panel_units)

    return jax.shard_map(body, mesh=mesh, in_specs=in_specs, out_specs=out_specs, check_vma=False)
```
